32 devices in a mesh: win: 4 (over y, x), head: 8 (over z, core).
Axes of the slice: x: 2, y: 2, z: 4, core: 2. Of those that a mesh axis runs over, the one named last changes fastest.
Arguments:
- section_rows: bfloat16 [384, 100, 4, 256], P('win', None, None, 'head'), may hold values from -6 to 6
- reduce_weight: bfloat16 [4, 256, 512], replicated, may hold values from -0.1875 to 0.1875
- norm0_gain: float32 [4, 256], replicated, may hold values from 0.5 to 1.5
- norm0_bias: float32 [4, 256], replicated, may hold values from -1.75 to 1.75
- norm1_gain: float32 [512], replicated, may hold values from 0.5 to 1.5
- norm1_bias: float32 [512], replicated, may hold values from -1.75 to 1.75
- qkv_weight: bfloat16 [512, 1536], replicated, may hold values from -0.25 to 0.25
- q_bias: float32 [512], replicated, may hold values from -3 to 3
- v_bias: float32 [512], replicated, may hold values from -3 to 3
- rel_table: float32 [16, 361], replicated, may hold values from -6 to 6
- proj_weight: bfloat16 [512, 512], replicated, may hold values from -0.75 to 0.75
- proj_bias: float32 [512], replicated, may hold values from -1.75 to 1.75
- norm2_gain: float32 [512], replicated, may hold values from 0.5 to 1.5
- norm2_bias: float32 [512], replicated, may hold values from -1.75 to 1.75
- fc1_weight: bfloat16 [512, 2048], replicated, may hold values from -0.25 to 0.25
- fc1_bias: float32 [2048], replicated, may hold values from -3 to 3
- fc2_weight: bfloat16 [2048, 512], replicated, may hold values from -0.25 to 0.25
- fc2_bias: float32 [512], replicated, may hold values from -1.75 to 1.75
- window_valid: int32 [384], P(('win', 'head')), may hold values 0 or 1
- cotangent: bfloat16 [384, 100, 512], P(('win', 'head')), may hold values from -6 to 6
Outputs:
- block_out: bfloat16 [384, 100, 512], P(('win', 'head'))
- section_grad: bfloat16 [384, 100, 4, 256], P('win', None, None, 'head')
- reduce_grad: float32 [4, 256, 512], P(None, 'head')
- norm0_gain_grad: float32 [4, 256], P(None, 'head')
- norm0_bias_grad: float32 [4, 256], P(None, 'head')
- norm1_gain_grad: float32 [512], P(('win', 'head'))
- norm1_bias_grad: float32 [512], P(('win', 'head'))
- qkv_grad: float32 [512, 1536], P(('win', 'head'))
- q_bias_grad: float32 [512], P(('win', 'head'))
- v_bias_grad: float32 [512], P(('win', 'head'))
- table_grad: float32 [16, 361], replicated
- proj_grad: float32 [512, 512], P(('win', 'head'))
- proj_bias_grad: float32 [512], P(('win', 'head'))
- norm2_gain_grad: float32 [512], P(('win', 'head'))
- norm2_bias_grad: float32 [512], P(('win', 'head'))
- fc1_grad: float32 [512, 2048], P(('win', 'head'))
- fc1_bias_grad: float32 [2048], P(('win', 'head'))
- fc2_grad: float32 [2048, 512], P(('win', 'head'))
- fc2_bias_grad: float32 [512], P(('win', 'head'))
The draws below stay inside these ranges and needn't reach their ends.
All inputs are finite; a program needn't handle non-finite values. No bound on the sum of `window_valid` on one device may be relied on, other than what follows from the above.
Results may differ from the reference program's by a relative error of at most 0.02.
Values may be sent and summed in bfloat16 or wider, within the bound.
A program may use at most 192 MiB of HBM per device.

```python
import jax
import jax.numpy as jnp
from jax import lax

C2 = 256
DM = 512
HEADS = 16
HD = 32
FF = 2048
WIN = 10
W_DEV = 12
WT = 100
RELS = 361
WINDOWS = 384
N_HEAD = 8


def with_ends(entries, stream_key, low, high):
    longest = entries.shape.index(max(entries.shape))
    spots = []
    for shift in (0, 1):
        where = [jax.random.randint(jax.random.fold_in(stream_key, axis), (), 0, length) for axis, length in enumerate(entries.shape)]
        where[longest] = (where[longest] + shift) % entries.shape[longest]
        spots.append(tuple(where))
    return entries.at[spots[0]].set(low).at[spots[1]].set(high)


def shard_levels(own_key, extent, shards, low, top_value):
    level = 1.0
    for position, shards_of in shards:
        steps = jax.random.uniform(jax.random.fold_in(jax.random.fold_in(own_key, 6), position), (shards_of,), jnp.float32, low / len(shards), top_value / len(shards))
        level = level * jnp.repeat(jnp.exp(steps), extent[position] // shards_of).reshape((-1,) + (1,) * (len(extent) - 1 - position))
    return level


def bell_draw(rng, extent, scale, reach, cuts=(), kind=jnp.bfloat16):
    drawn = scale * jax.random.normal(rng, extent, jnp.float32)
    if cuts:
        drawn = drawn * shard_levels(rng, extent, cuts, -0.22, 0.18)
    return jnp.clip(drawn, -reach, reach).astype(kind)


def setup_inputs(seed: int = 0) -> dict:
    splits = jax.random.split(jax.random.key(seed), 21)
    return {
        "section_rows": bell_draw(splits[0], (WINDOWS, WT, 4, C2), 1.0, 6.0, ((0, 4), (3, 8))),
        "reduce_weight": bell_draw(splits[1], (4, C2, DM), (4 * C2) ** -0.5, 0.1875),
        "norm0_gain": jnp.clip(1.0 + 0.1 * jax.random.normal(splits[2], (4, C2), jnp.float32), 0.5, 1.5),
        "norm0_bias": bell_draw(splits[3], (4, C2), 0.3, 1.75, (), jnp.float32),
        "norm1_gain": jnp.clip(1.0 + 0.1 * jax.random.normal(splits[4], (DM,), jnp.float32), 0.5, 1.5),
        "norm1_bias": bell_draw(splits[5], (DM,), 0.3, 1.75, (), jnp.float32),
        "qkv_weight": bell_draw(splits[6], (DM, 3 * DM), DM ** -0.5, 0.25),
        "q_bias": bell_draw(splits[7], (DM,), 0.5, 3.0, (), jnp.float32),
        "v_bias": bell_draw(splits[8], (DM,), 0.5, 3.0, (), jnp.float32),
        "rel_table": bell_draw(splits[9], (HEADS, RELS), 1.0, 6.0, (), jnp.float32),
        "proj_weight": bell_draw(splits[10], (DM, DM), (DM // 8) ** -0.5, 0.75),
        "proj_bias": bell_draw(splits[11], (DM,), 0.3, 1.75, (), jnp.float32),
        "norm2_gain": jnp.clip(1.0 + 0.1 * jax.random.normal(splits[12], (DM,), jnp.float32), 0.5, 1.5),
        "norm2_bias": bell_draw(splits[13], (DM,), 0.3, 1.75, (), jnp.float32),
        "fc1_weight": bell_draw(splits[14], (DM, FF), DM ** -0.5, 0.25),
        "fc1_bias": bell_draw(splits[15], (FF,), 0.5, 3.0, (), jnp.float32),
        "fc2_weight": bell_draw(splits[16], (FF, DM), (FF // 4) ** -0.5, 0.25),
        "fc2_bias": bell_draw(splits[17], (DM,), 0.3, 1.75, (), jnp.float32),
        "window_valid": with_ends((jax.random.randint(splits[18], (WINDOWS,), 0, 4) < 3).astype(jnp.int32), jax.random.fold_in(splits[18], 1), 0, 1),
        "cotangent": bell_draw(splits[19], (WINDOWS, WT, DM), 1.0, 6.0, ((0, 32),)),
    }


@jax.custom_vjp
def low(v):
    return lax.optimization_barrier(v.astype(jnp.bfloat16)).astype(jnp.float32)

@jax.custom_vjp
def low_back(v):
    return v

def low_keep(v):
    return (low(v), None)

def low_pass(kept, grad):
    return (grad,)

def back_keep(v):
    return (v, None)

def back_low(kept, grad):
    return (low(grad),)
low.defvjp(low_keep, low_pass)
low_back.defvjp(back_keep, back_low)
epsilon = 1e-05

def product(left, right):
    return jnp.matmul(left, right, precision=lax.Precision.HIGHEST)

def layer_norm(values, gain, shift):
    average = lax.optimization_barrier(jnp.mean(values, axis=-1, keepdims=True))
    centred = values - average
    variance = lax.optimization_barrier(jnp.mean(centred * centred, axis=-1, keepdims=True))
    return centred * lax.rsqrt(variance + epsilon) * gain + shift

def relative_onehot():
    positions = jnp.arange(WT, dtype=jnp.int32)
    pos_row = positions // WIN
    pos_col = positions % WIN
    rel_index = (pos_row[:, None] - pos_row[None, :] + WIN - 1) * (2 * WIN - 1) + (pos_col[:, None] - pos_col[None, :] + WIN - 1)
    offsets = jnp.arange(RELS, dtype=jnp.int32)
    return (rel_index[:, :, None] == offsets[None, None, :]).astype(jnp.float32)

def forward(params, windows_in, valid_flags, onehot):
    number = windows_in.shape[0]
    merged = windows_in.reshape(number, WT, 4 * C2)
    normed = low(layer_norm(merged, params['norm0_gain'].reshape(4 * C2), params['norm0_bias'].reshape(4 * C2)))
    resid = low_back(product(normed, params['reduce_weight'].reshape(4 * C2, DM)))
    first = low(layer_norm(resid, params['norm1_gain'], params['norm1_bias']))
    packed = product(first, params['qkv_weight'])
    query = low(low_back(packed[..., :DM] + params['q_bias'])).reshape(number, WT, HEADS, HD)
    key_heads = low(low_back(packed[..., DM:2 * DM])).reshape(number, WT, HEADS, HD)
    value_heads = low(low_back(packed[..., 2 * DM:] + params['v_bias'])).reshape(number, WT, HEADS, HD)
    raw_scores = low_back(jnp.einsum('wihd,wjhd->whij', query, key_heads, precision=lax.Precision.HIGHEST))
    pos_bias = jnp.einsum('ijr,hr->hij', onehot, params['rel_table'], precision=lax.Precision.HIGHEST)
    scores = raw_scores * HD ** (-0.5) + pos_bias[None]
    peak = lax.optimization_barrier(jnp.max(scores, axis=-1, keepdims=True))
    expo = jnp.exp(scores - peak)
    probs = low(expo / lax.optimization_barrier(jnp.sum(expo, axis=-1, keepdims=True)))
    attended = jnp.einsum('whij,wjhd->wihd', probs, value_heads, precision=lax.Precision.HIGHEST)
    attended = low(low_back(attended)).reshape(number, WT, DM)
    branch = low_back(product(attended, params['proj_weight']) + params['proj_bias'])
    second = resid + branch
    second_norm = low(layer_norm(second, params['norm2_gain'], params['norm2_bias']))
    hidden = low_back(product(second_norm, params['fc1_weight']) + params['fc1_bias'])
    activated = low(jax.nn.gelu(hidden, approximate=False))
    result = second + product(activated, params['fc2_weight']) + params['fc2_bias']
    return result * valid_flags[:, None, None].astype(jnp.float32)

def reference(section_rows, reduce_weight, norm0_gain, norm0_bias, norm1_gain, norm1_bias, qkv_weight, q_bias, v_bias, rel_table, proj_weight, proj_bias, norm2_gain, norm2_bias, fc1_weight, fc1_bias, fc2_weight, fc2_bias, window_valid, cotangent):
    params = {'reduce_weight': reduce_weight.astype(jnp.float32), 'norm0_gain': norm0_gain.astype(jnp.float32), 'norm0_bias': norm0_bias.astype(jnp.float32), 'norm1_gain': norm1_gain.astype(jnp.float32), 'norm1_bias': norm1_bias.astype(jnp.float32), 'qkv_weight': qkv_weight.astype(jnp.float32), 'q_bias': q_bias.astype(jnp.float32), 'v_bias': v_bias.astype(jnp.float32), 'rel_table': rel_table.astype(jnp.float32), 'proj_weight': proj_weight.astype(jnp.float32), 'proj_bias': proj_bias.astype(jnp.float32), 'norm2_gain': norm2_gain.astype(jnp.float32), 'norm2_bias': norm2_bias.astype(jnp.float32), 'fc1_weight': fc1_weight.astype(jnp.float32), 'fc1_bias': fc1_bias.astype(jnp.float32), 'fc2_weight': fc2_weight.astype(jnp.float32), 'fc2_bias': fc2_bias.astype(jnp.float32)}
    onehot = relative_onehot()
    group = W_DEV * N_HEAD
    blocks = section_rows.shape[0] // group
    inputs = (section_rows.astype(jnp.float32).reshape(blocks, group, WT, 4, C2), window_valid.reshape(blocks, group), cotangent.astype(jnp.float32).reshape(blocks, group, WT, DM))

    def advance(running, pieces):
        block_in, block_valid, block_cot = pieces
        result, pullback = jax.vjp(lambda weights, data: forward(weights, data, block_valid, onehot), params, block_in)
        gradients, data_grad = pullback(block_cot)
        running = jax.tree.map(lambda left, right: left + right, running, gradients)
        return (running, (result.astype(jnp.bfloat16), data_grad.astype(jnp.bfloat16)))
    initial = jax.tree.map(jnp.zeros_like, params)
    totals, (results, data_grads) = lax.scan(advance, initial, inputs)
    block_out = results.reshape(section_rows.shape[0], WT, DM)
    section_grad = data_grads.reshape(section_rows.shape)
    return (block_out, section_grad, totals['reduce_weight'], totals['norm0_gain'], totals['norm0_bias'], totals['norm1_gain'], totals['norm1_bias'], totals['qkv_weight'], totals['q_bias'], totals['v_bias'], totals['rel_table'], totals['proj_weight'], totals['proj_bias'], totals['norm2_gain'], totals['norm2_bias'], totals['fc1_weight'], totals['fc1_bias'], totals['fc2_weight'], totals['fc2_bias'])
```

```python
import functools

import jax
import jax.numpy as jnp
from jax import lax
from jax.experimental import pallas as pl
from jax.experimental.pallas import tpu as pltpu
from jax.sharding import PartitionSpec as P

C2 = 256
DM = 512
HEADS = 16
HD = 32
FF = 2048
WIN = 10
WT = 100
RELS = 361
SPAN = 2 * WIN - 1

QUADS = 4
WIDTH = QUADS * C2
CW = 2
RW = 104
R = CW * RW
JP = 112
LN = 128
GROUPS = 4
PER = 4
LAG = 3
SLOTS = LAG + 1
RB = 16
TILE = 512
EPS = 1e-05
LOG2E = 1.4426950408889634
SCALE = HD ** (-0.5)

MESH = pl.DeviceIdType.MESH
F32 = jnp.float32
BF16 = jnp.bfloat16

O_QB, O_VB, O_PB, O_FC1B, O_FC2B = 0, 512, 1024, 1536, 3584
O_N1G, O_N1B, O_N2G, O_N2B, O_N0G, O_N0B, O_END = 4096, 4608, 5120, 5632, 6144, 7168, 8192


def dot(a, b):
    return lax.dot_general(a, b, (((1,), (0,)), ((), ())), preferred_element_type=F32)


def dot_nt(a, b):
    return lax.dot_general(a, b, (((1,), (1,)), ((), ())), preferred_element_type=F32)


def dot_tn(a, b):
    return lax.dot_general(a, b, (((0,), (0,)), ((), ())), preferred_element_type=F32)


def normalised(v):
    centred = v - jnp.mean(v, axis=-1, keepdims=True)
    inv = lax.rsqrt(jnp.mean(centred * centred, axis=-1, keepdims=True) + EPS)
    return centred * inv, inv


def norm_back(d_out, gain, xhat, inv):
    u = d_out * gain
    mean_u = jnp.mean(u, axis=-1, keepdims=True)
    mean_ux = jnp.mean(u * xhat, axis=-1, keepdims=True)
    return (u - mean_u - xhat * mean_ux) * inv


def fold(v):
    total = v[0:8]
    for r in range(8, v.shape[0], 8):
        total = total + v[r : r + 8]
    return total


def gelu_parts(x):
    z = jnp.abs(x) * 0.7071067811865476
    t = 1.0 / (1.0 + 0.3275911 * z)
    e = jnp.exp2(x * x * (-0.5 * LOG2E))
    poly = ((((1.061405429 * t - 1.453152027) * t + 1.421413741) * t - 0.284496736) * t + 0.254829592) * t
    half = 0.5 * poly * e
    cdf = jnp.where(x < 0, half, 1.0 - half)
    return x * cdf, cdf + x * e * 0.3989422804014327


def split3(v):
    hi = v.astype(BF16)
    rest = v - hi.astype(F32)
    mid = rest.astype(BF16)
    low = (rest - mid.astype(F32)).astype(BF16)
    return hi, mid, low


def offset_of(j):
    return (j // WIN) * SPAN + j % WIN


def kernel(
    n_head, n_chunk, share,
    x_hbm, wp_hbm, n0g, n0b, n1g, n1b, wqkv_hbm, qb, vb, table, wproj_hbm, pb, n2g, n2b,
    wfc1_hbm, fc1b, wfc2_hbm, fc2b, valid, cot_hbm,
    out_ref, sect_hbm, g_fc1, g_fc2, g_qkv, g_proj, g_red, g_small, g_table,
    xv, send_in, rin, rout, wp, wqkv, wproj, wfc1, wfc2, cot,
    nrm, res, fst, qkv, prob, att, stage, sec, sn, dy, wide, act, dh, ffo, dsn, dsec, dpk, d_heads, sums, bias_t, ds_acc,
    in_send, in_recv, out_send, out_recv, x_sem, w_sem, own_sem, sect_sem,
):
    me = lax.axis_index("head")
    lanes = QUADS * share

    def peer(k):
        return lax.rem(me + k, n_head)

    def in_copy(c, k):
        to = peer(k)
        return pltpu.make_async_remote_copy(
            src_ref=send_in.at[c, to], dst_ref=rin.at[c, me], send_sem=in_send.at[c, k], recv_sem=in_recv.at[c, k],
            device_id={"head": to}, device_id_type=MESH,
        )

    def out_copy(c, k):
        to = peer(k)
        return pltpu.make_async_remote_copy(
            src_ref=rin.at[c, to], dst_ref=rout.at[c, me], send_sem=out_send.at[c, k], recv_sem=out_recv.at[c, k],
            device_id={"head": to}, device_id_type=MESH,
        )

    def own_in(c):
        return pltpu.make_async_copy(send_in.at[c, me], rin.at[c, me], own_sem)

    def own_out(c):
        return pltpu.make_async_copy(rin.at[c, me], rout.at[c, me], own_sem)

    def x_copy(c):
        return pltpu.make_async_copy(x_hbm.at[:, c], xv.at[c % 2], x_sem.at[c % 2])

    def sect_copy(c):
        return pltpu.make_async_copy(xv.at[c % 2], sect_hbm.at[:, c], sect_sem.at[c % 2])

    weights = [
        pltpu.make_async_copy(wqkv_hbm, wqkv, w_sem.at[1]),
        pltpu.make_async_copy(wproj_hbm, wproj, w_sem.at[2]),
        pltpu.make_async_copy(wfc1_hbm, wfc1, w_sem.at[3]),
        pltpu.make_async_copy(wfc2_hbm, wfc2, w_sem.at[4]),
        pltpu.make_async_copy(cot_hbm, cot, w_sem.at[5]),
    ]

    for c in range(min(2, n_chunk)):
        x_copy(c).start()
    barrier = pltpu.get_barrier_semaphore()
    for k in range(1, n_head):
        pl.semaphore_signal(barrier, inc=1, device_id={"head": peer(k)}, device_id_type=MESH)
    for q in range(QUADS):
        for s in range(n_head):
            pltpu.make_async_copy(
                wp_hbm.at[q, s], wp.at[pl.ds((s * QUADS + q) * share, share), :], w_sem.at[0]
            ).start()
    for w in weights:
        w.start()

    eye_rows = (
        lax.broadcasted_iota(jnp.int32, (RW, WT), 0) == lax.broadcasted_iota(jnp.int32, (RW, WT), 1)
    ).astype(F32).astype(BF16)
    eye_lanes = (
        lax.broadcasted_iota(jnp.int32, (lanes, lanes), 0) == lax.broadcasted_iota(jnp.int32, (lanes, lanes), 1)
    ).astype(F32).astype(BF16)

    def repack(c):
        x_copy(c).wait()
        for d in range(n_head):
            rows = [dot_nt(eye_rows, xv[c % 2, d, w]) for w in range(CW)]
            send_in[c, d] = jnp.concatenate(rows, axis=0).astype(BF16)

    def send(c):
        for k in range(1, n_head):
            in_copy(c, k).start()
        own_in(c).start()
        own_in(c).wait()

    repack(0)
    pl.semaphore_wait(barrier, n_head - 1)
    send(0)

    def send_rest(c, carry):
        @pl.when(c < n_chunk - 1)
        def _():
            x_copy(c + 1).start()

        repack(c)
        send(c)
        return carry

    lax.fori_loop(1, n_chunk, send_rest, 0)

    def zero(ref):
        def body(r, carry):
            ref[pl.ds(pl.multiple_of(r * 8, 8), 8), :] = jnp.zeros((8, ref.shape[1]), F32)
            return carry
        lax.fori_loop(0, ref.shape[0] // 8, body, 0)

    for ref in (g_fc1, g_fc2, g_qkv, g_proj, g_red, sums):
        zero(ref)
    ds_acc[...] = jnp.zeros_like(ds_acc)

    def zero_heads(c, carry):
        qkv[c] = jnp.zeros(qkv.shape[1:], BF16)
        return carry

    lax.fori_loop(0, SLOTS, zero_heads, 0)
    d_heads[...] = jnp.zeros_like(d_heads)
    bias_t[:, WT:, :] = jnp.full((HEADS, JP - WT, LN), -1e30, F32)

    spot = lax.broadcasted_iota(jnp.int32, (2 * LN, LN), 0)
    token = lax.broadcasted_iota(jnp.int32, (2 * LN, LN), 1)
    token_row = (token * 205) >> 11
    pick = ((spot == token_row * SPAN + token - token_row * WIN) & (token < WT)).astype(F32).astype(BF16)
    for row in range(WIN):
        parts = []
        for col in range(WIN):
            off = offset_of(WT - 1) - offset_of(row * WIN + col)
            parts.append(table[:, off : off + 2 * LN])
        hi, mid, low = split3(jnp.concatenate(parts, axis=0))
        found = (dot(hi, pick) + dot(mid, pick) + dot(low, pick)) * LOG2E
        for col in range(WIN):
            bias_t[:, row * WIN + col, :] = found[col * HEADS : (col + 1) * HEADS]

    pltpu.make_async_copy(wp, wp, w_sem.at[0]).wait()
    for w in weights:
        w.wait()

    lane = lax.broadcasted_iota(jnp.int32, (1, LN), 1)
    masks = [((lane >= h * HD) & (lane < (h + 1) * HD)).astype(F32).astype(BF16) for h in range(PER)]

    def by_head(v):
        return jnp.concatenate([v * m for m in masks], axis=0)

    def merged_rows(c, r):
        return jnp.concatenate([rin[c, s, pl.ds(r, RB), :] for s in range(n_head)], axis=1).astype(F32)

    def padded(v):
        return jnp.concatenate([v, jnp.zeros((JP - RW, v.shape[1]), F32)], axis=0)

    def first_half(c):
        p = lax.rem(c, SLOTS)
        for k in range(1, n_head):
            in_copy_wait = pltpu.make_async_remote_copy(
                src_ref=send_in.at[c, me], dst_ref=rin.at[c, lax.rem(me + n_head - k, n_head)],
                send_sem=in_send.at[c, k], recv_sem=in_recv.at[c, k],
                device_id={"head": peer(k)}, device_id_type=MESH,
            )
            in_copy_wait.wait_recv()
        for r in range(0, R, RB):
            xhat, unused = normalised(merged_rows(c, r))
            nrm[r : r + RB, :] = (xhat * n0g[...] + n0b[...]).astype(BF16)
        res[p] = dot(nrm[...], wp[...])
        for r in range(0, R, RB):
            xhat, unused = normalised(res[p, r : r + RB, :])
            fst[r : r + RB, :] = (xhat * n1g[...] + n1b[...]).astype(BF16)
        for t in range(3):
            part = dot(fst[...], wqkv[:, t * DM : (t + 1) * DM])
            if t == 0:
                part = part + qb[...]
            if t == 2:
                part = part + vb[...]
            for w in range(CW):
                for g in range(GROUPS):
                    piece = part[w * RW : (w + 1) * RW, g * LN : (g + 1) * LN]
                    qkv[p, w, t, g, 0:JP, :] = padded(piece).astype(BF16)

        def attend(w, carry):
            for g in range(GROUPS):
                scores = dot_nt(qkv[p, w, 1, g, 0:JP, :], by_head(qkv[p, w, 0, g]))
                found = []
                for h in range(PER):
                    s = scores[:, h * LN : (h + 1) * LN] * (SCALE * LOG2E) + bias_t[g * PER + h]
                    e = jnp.exp2(s - jnp.max(s, axis=0, keepdims=True))
                    found.append((e * (1.0 / jnp.sum(e, axis=0, keepdims=True))).astype(BF16))
                probs = jnp.concatenate(found, axis=1)
                prob[p, w, g] = probs
                mixed = dot_tn(qkv[p, w, 2, g, 0:JP, :], probs)
                own = jnp.concatenate(
                    [mixed[h * HD : (h + 1) * HD, h * LN : (h + 1) * LN] for h in range(PER)], axis=0
                )
                stage[pl.ds(pl.multiple_of(w * RW, 8), RW), g * LN : (g + 1) * LN] = own.T[0:RW]
            return carry

        lax.fori_loop(0, CW, attend, 0)
        att[p] = stage[:, 0:DM].astype(BF16)
        sec[...] = res[p] + dot(att[p], wproj[...]) + pb[...]
        for r in range(0, R, RB):
            xhat, unused = normalised(sec[r : r + RB, :])
            sn[r : r + RB, :] = (xhat * n2g[...] + n2b[...]).astype(BF16)
        flags = [valid[c * CW + w].astype(F32) for w in range(CW)]
        tail = jnp.zeros((RW - WT, DM), F32)
        pieces = []
        for w in range(CW):
            pieces += [cot[c * CW + w].astype(F32) * flags[w], tail]
        up = jnp.concatenate(pieces, axis=0)
        dy[...] = up.astype(BF16)
        sums[:, O_FC2B : O_FC2B + DM] += fold(up)
        ffo[...] = sec[...] + fc2b[...]
        dsn[...] = jnp.zeros_like(dsn)

        def feed(t, carry):
            cols = pl.ds(pl.multiple_of(t * TILE, TILE), TILE)
            wide[:, 0:TILE] = dot(sn[...], wfc1[:, cols]) + fc1b[:, cols]
            wide[:, TILE : 2 * TILE] = dot_nt(dy[...], wfc2[cols, :])
            total = jnp.zeros((8, TILE), F32)
            for r in range(0, R, RB):
                value, slope = gelu_parts(wide[r : r + RB, 0:TILE])
                act[r : r + RB, :] = value.astype(BF16)
                low = (wide[r : r + RB, TILE : 2 * TILE] * slope).astype(BF16)
                dh[r : r + RB, :] = low
                total = total + fold(low.astype(F32))
            sums[:, pl.ds(pl.multiple_of(O_FC1B + t * TILE, TILE), TILE)] += total
            ffo[...] += dot(act[...], wfc2[cols, :])
            dsn[...] += dot_nt(dh[...], wfc1[:, cols])
            g_fc2[cols, :] += dot_tn(act[...], dy[...])
            g_fc1[:, cols] += dot_tn(sn[...], dh[...])
            return carry

        lax.fori_loop(0, FF // TILE, feed, 0)
        for w in range(CW):
            out_ref[c * CW + w] = (ffo[w * RW : w * RW + WT, :] * flags[w]).astype(BF16)
        sum_g = jnp.zeros((8, DM), F32)
        sum_b = jnp.zeros((8, DM), F32)
        for r in range(0, R, RB):
            xhat, inv = normalised(sec[r : r + RB, :])
            d_out = dsn[r : r + RB, :]
            sum_g = sum_g + fold(d_out * xhat)
            sum_b = sum_b + fold(d_out)
            dsec[p, r : r + RB, :] = norm_back(d_out, n2g[...], xhat, inv) + dy[r : r + RB, :].astype(F32)
        sums[:, O_N2G : O_N2G + DM] += sum_g
        sums[:, O_N2B : O_N2B + DM] += sum_b

    def second_half(c):
        p = lax.rem(c, SLOTS)
        low = dsec[p].astype(BF16)
        sums[:, O_PB : O_PB + DM] += fold(low.astype(F32))
        dy[...] = low
        g_proj[...] += dot_tn(att[p], dy[...])
        back = dot_nt(dy[...], wproj[...])
        for w in range(CW):
            for g in range(GROUPS):
                piece = back[w * RW : (w + 1) * RW, g * LN : (g + 1) * LN]
                d_heads[w, g, 0:JP, :] = padded(piece).astype(BF16)

        def attend(w, carry):
            for g in range(GROUPS):
                d_out = by_head(d_heads[w, g])
                q_all = by_head(qkv[p, w, 0, g])
                d_probs = dot_nt(qkv[p, w, 2, g, 0:JP, :], d_out)
                raw = []
                for h in range(PER):
                    pr = prob[p, w, g, :, h * LN : (h + 1) * LN].astype(F32)
                    dp = d_probs[:, h * LN : (h + 1) * LN]
                    pd = pr * dp
                    d_s = pd - pr * jnp.sum(pd, axis=0, keepdims=True)
                    ds_acc[g * PER + h] += d_s
                    raw.append((d_s * SCALE).astype(BF16))
                d_raw = jnp.concatenate(raw, axis=1)
                rows = pl.ds(pl.multiple_of(w * RW, 8), RW)
                d_v = dot(prob[p, w, g], d_out)
                d_k = dot(d_raw, q_all)
                mixed = dot_tn(qkv[p, w, 1, g, 0:JP, :], d_raw)
                own = jnp.concatenate(
                    [mixed[h * HD : (h + 1) * HD, h * LN : (h + 1) * LN] for h in range(PER)], axis=0
                )
                stage[rows, g * LN : (g + 1) * LN] = own.T[0:RW]
                stage[rows, DM + g * LN : DM + (g + 1) * LN] = d_k[0:RW]
                stage[rows, 2 * DM + g * LN : 2 * DM + (g + 1) * LN] = d_v[0:RW]
            return carry

        lax.fori_loop(0, CW, attend, 0)
        sum_g = jnp.zeros((8, DM), F32)
        sum_b = jnp.zeros((8, DM), F32)
        sum_q = jnp.zeros((8, DM), F32)
        sum_v = jnp.zeros((8, DM), F32)
        for r in range(0, R, RB):
            low = stage[r : r + RB, :].astype(BF16)
            dpk[r : r + RB, :] = low
            sum_q = sum_q + fold(low[:, 0:DM].astype(F32))
            sum_v = sum_v + fold(low[:, 2 * DM :].astype(F32))
        sums[:, O_QB : O_QB + DM] += sum_q
        sums[:, O_VB : O_VB + DM] += sum_v
        dsn[...] = dot_nt(dpk[...], wqkv[...])
        for r in range(0, R, RB):
            xhat, inv = normalised(res[p, r : r + RB, :])
            fst[r : r + RB, :] = (xhat * n1g[...] + n1b[...]).astype(BF16)
            d_out = dsn[r : r + RB, :]
            sum_g = sum_g + fold(d_out * xhat)
            sum_b = sum_b + fold(d_out)
            d_res = norm_back(d_out, n1g[...], xhat, inv) + dsec[p, r : r + RB, :]
            sn[r : r + RB, :] = d_res.astype(BF16)
        sums[:, O_N1G : O_N1G + DM] += sum_g
        sums[:, O_N1B : O_N1B + DM] += sum_b
        wide[...] = dot_nt(sn[...], wp[...])
        sum_g = jnp.zeros((8, WIDTH), F32)
        sum_b = jnp.zeros((8, WIDTH), F32)
        for r in range(0, R, RB):
            xhat, inv = normalised(merged_rows(c, r))
            nrm[r : r + RB, :] = (xhat * n0g[...] + n0b[...]).astype(BF16)
            d_out = wide[r : r + RB, :]
            sum_g = sum_g + fold(d_out * xhat)
            sum_b = sum_b + fold(d_out)
            low = norm_back(d_out, n0g[...], xhat, inv).astype(BF16)
            for s in range(n_head):
                rin[c, s, r : r + RB, :] = low[:, s * lanes : (s + 1) * lanes]
        sums[:, O_N0G : O_N0G + WIDTH] += sum_g
        sums[:, O_N0B : O_N0B + WIDTH] += sum_b
        for k in range(1, n_head):
            out_copy(c, k).start()
        own_out(c).start()
        g_qkv[...] += dot_tn(fst[...], dpk[...])
        g_red[...] += dot_tn(nrm[...], sn[...])
        own_out(c).wait()

    def step(s, carry):
        @pl.when(s < n_chunk)
        def _():
            first_half(s)

        @pl.when(s >= LAG)
        def _():
            second_half(s - LAG)

        return carry

    lax.fori_loop(0, n_chunk + LAG, step, 0)

    def unpack(c, carry):
        for k in range(1, n_head):
            pltpu.make_async_remote_copy(
                src_ref=rin.at[c, me], dst_ref=rout.at[c, lax.rem(me + n_head - k, n_head)],
                send_sem=out_send.at[c, k], recv_sem=out_recv.at[c, k],
                device_id={"head": peer(k)}, device_id_type=MESH,
            ).wait_recv()

        @pl.when(c >= 2)
        def _():
            sect_copy(c - 2).wait()

        for s in range(n_head):
            turned = dot_nt(eye_lanes, rout[c, s])
            for w in range(CW):
                xv[c % 2, s, w] = turned[:, w * RW : w * RW + WT].astype(BF16)
        sect_copy(c).start()
        return carry

    lax.fori_loop(0, n_chunk, unpack, 0)
    for c in range(max(0, n_chunk - 2), n_chunk):
        sect_copy(c).wait()

    g_small[...] = jnp.sum(sums[...], axis=0, keepdims=True)
    g_table[...] = jnp.zeros_like(g_table)
    for row in range(WIN):
        spread = jnp.zeros((WIN * HEADS, 2 * LN), F32)
        whole = jnp.concatenate([ds_acc[:, row * WIN + col, :] for col in range(WIN)], axis=0)
        for part in split3(whole):
            spread = spread + dot_nt(part, pick)
        for col in range(WIN):
            off = offset_of(WT - 1) - offset_of(row * WIN + col)
            g_table[:, off : off + 2 * LN] += spread[col * HEADS : (col + 1) * HEADS]

    def drain(c, carry):
        for k in range(1, n_head):
            in_copy(c, k).wait_send()
            out_copy(c, k).wait_send()
        return carry

    lax.fori_loop(0, n_chunk, drain, 0)


def run_kernel(n_head, n_chunk, share, args):
    lanes = QUADS * share
    any_, vmem = pl.BlockSpec(memory_space=pl.ANY), pl.BlockSpec(memory_space=pltpu.VMEM)
    smem = pl.BlockSpec(memory_space=pltpu.SMEM)
    windows = n_chunk * CW
    in_specs = [
        any_, any_, vmem, vmem, vmem, vmem, any_, vmem, vmem, vmem, any_, vmem, vmem, vmem,
        any_, vmem, any_, vmem, smem, any_,
    ]
    out_shape = [
        jax.ShapeDtypeStruct((windows, WT, DM), BF16),
        jax.ShapeDtypeStruct((n_head, n_chunk, CW, lanes, WT), BF16),
        jax.ShapeDtypeStruct((DM, FF), F32),
        jax.ShapeDtypeStruct((FF, DM), F32),
        jax.ShapeDtypeStruct((DM, 3 * DM), F32),
        jax.ShapeDtypeStruct((DM, DM), F32),
        jax.ShapeDtypeStruct((WIDTH, DM), F32),
        jax.ShapeDtypeStruct((1, O_END), F32),
        jax.ShapeDtypeStruct((HEADS, 4 * LN), F32),
    ]
    out_specs = [vmem, any_] + [vmem] * 7
    dma = pltpu.SemaphoreType.DMA
    scratch = [
        pltpu.VMEM((2, n_head, CW, lanes, WT), BF16),
        pltpu.VMEM((n_chunk, n_head, R, lanes), BF16),
        pltpu.VMEM((n_chunk, n_head, R, lanes), BF16),
        pltpu.VMEM((n_chunk, n_head, R, lanes), BF16),
        pltpu.VMEM((WIDTH, DM), BF16),
        pltpu.VMEM((DM, 3 * DM), BF16),
        pltpu.VMEM((DM, DM), BF16),
        pltpu.VMEM((DM, FF), BF16),
        pltpu.VMEM((FF, DM), BF16),
        pltpu.VMEM((windows, WT, DM), BF16),
        pltpu.VMEM((R, WIDTH), BF16),
        pltpu.VMEM((SLOTS, R, DM), F32),
        pltpu.VMEM((R, DM), BF16),
        pltpu.VMEM((SLOTS, CW, 3, GROUPS, LN, LN), BF16),
        pltpu.VMEM((SLOTS, CW, GROUPS, JP, PER * LN), BF16),
        pltpu.VMEM((SLOTS, R, DM), BF16),
        pltpu.VMEM((R, 3 * DM), F32),
        pltpu.VMEM((R, DM), F32),
        pltpu.VMEM((R, DM), BF16),
        pltpu.VMEM((R, DM), BF16),
        pltpu.VMEM((R, WIDTH), F32),
        pltpu.VMEM((R, TILE), BF16),
        pltpu.VMEM((R, TILE), BF16),
        pltpu.VMEM((R, DM), F32),
        pltpu.VMEM((R, DM), F32),
        pltpu.VMEM((SLOTS, R, DM), F32),
        pltpu.VMEM((R, 3 * DM), BF16),
        pltpu.VMEM((CW, GROUPS, LN, LN), BF16),
        pltpu.VMEM((8, O_END), F32),
        pltpu.VMEM((HEADS, JP, LN), F32),
        pltpu.VMEM((HEADS, JP, LN), F32),
        dma((n_chunk, n_head)), dma((n_chunk, n_head)), dma((n_chunk, n_head)), dma((n_chunk, n_head)),
        dma((2,)), dma((6,)), dma, dma((2,)),
    ]
    return pl.pallas_call(
        functools.partial(kernel, n_head, n_chunk, share),
        out_shape=out_shape, in_specs=in_specs, out_specs=out_specs, scratch_shapes=scratch,
        compiler_params=pltpu.CompilerParams(
            collective_id=0, has_side_effects=True, vmem_limit_bytes=63 * 1024 * 1024
        ),
        cost_estimate=pl.CostEstimate(flops=27 * 10**9, bytes_accessed=30 * 10**6, transcendentals=10**7),
    )(*args)


def local(
    n_head, section_rows, reduce_weight, norm0_gain, norm0_bias, norm1_gain, norm1_bias, qkv_weight, q_bias, v_bias,
    rel_table, proj_weight, proj_bias, norm2_gain, norm2_bias, fc1_weight, fc1_bias, fc2_weight, fc2_bias,
    window_valid, cotangent,
):
    group_windows, tokens, quads, share = section_rows.shape
    windows = cotangent.shape[0]
    n_chunk = windows // CW
    lanes = quads * share
    rows = section_rows.transpose(0, 2, 3, 1).reshape(n_head, n_chunk, CW, lanes, tokens)

    def by_source(v):
        return v.reshape(quads, n_head, share).transpose(1, 0, 2).reshape(1, WIDTH)

    def row(v):
        return v.reshape(1, -1)

    args = (
        rows, reduce_weight.reshape(quads, n_head, share, DM), by_source(norm0_gain), by_source(norm0_bias),
        row(norm1_gain), row(norm1_bias), qkv_weight, row(q_bias), row(v_bias),
        jnp.pad(rel_table, ((0, 0), (0, 4 * LN - RELS))), proj_weight, row(proj_bias), row(norm2_gain), row(norm2_bias),
        fc1_weight, row(fc1_bias), fc2_weight, row(fc2_bias), window_valid, cotangent,
    )
    block_out, section, fc1, fc2, qkv, proj, red, small, table = run_kernel(n_head, n_chunk, share, args)
    section_grad = section.reshape(group_windows, quads, share, tokens).transpose(0, 3, 1, 2)
    both = ("win", "head")

    def scattered(v):
        return lax.psum_scatter(v.astype(BF16), both, scatter_dimension=0, tiled=True).astype(F32)

    mine = lax.psum_scatter(red.astype(BF16), "head", scatter_dimension=0, tiled=True)
    reduce_grad = lax.psum(mine, "win").astype(F32).reshape(quads, share, DM)
    vectors, table_grad = lax.psum((small[0], table), both)
    table_grad = table_grad[:, :RELS]
    at = lax.axis_index("win") * n_head + lax.axis_index("head")
    devices = lax.axis_size("win") * n_head

    def part(start, length):
        size = length // devices
        return lax.dynamic_slice_in_dim(vectors, start + at * size, size)

    def part0(start):
        return lax.dynamic_slice_in_dim(vectors, start + lax.axis_index("head") * lanes, lanes).reshape(quads, share)

    return (
        block_out, section_grad, reduce_grad, part0(O_N0G), part0(O_N0B), part(O_N1G, DM), part(O_N1B, DM),
        scattered(qkv), part(O_QB, DM), part(O_VB, DM), table_grad, scattered(proj), part(O_PB, DM),
        part(O_N2G, DM), part(O_N2B, DM), scattered(fc1), part(O_FC1B, FF), scattered(fc2), part(O_FC2B, DM),
    )

def solution(mesh):
    in_specs = (
        P("win", None, None, "head"),
        P(),
        P(),
        P(),
        P(),
        P(),
        P(),
        P(),
        P(),
        P(),
        P(),
        P(),
        P(),
        P(),
        P(),
        P(),
        P(),
        P(),
        P(("win", "head")),
        P(("win", "head"), None, None),
    )
    out_specs = (
        P(("win", "head"), None, None),
        P("win", None, None, "head"),
        P(None, "head", None),
        P(None, "head"),
        P(None, "head"),
        P(("win", "head")),
        P(("win", "head")),
        P(("win", "head"), None),
        P(("win", "head")),
        P(("win", "head")),
        P(),
        P(("win", "head"), None),
        P(("win", "head")),
        P(("win", "head")),
        P(("win", "head")),
        P(("win", "head"), None),
        P(("win", "head")),
        P(("win", "head"), None),
        P(("win", "head")),
    )
    return jax.shard_map(
        functools.partial(local, mesh.shape["head"]), mesh=mesh, in_specs=in_specs, out_specs=out_specs, check_vma=False)
```

```python
import functools

import jax
import jax.numpy as jnp
from jax import lax
from jax.experimental import pallas as pl
from jax.experimental.pallas import tpu as pltpu
from jax.sharding import PartitionSpec as P

C2 = 256
DM = 512
HEADS = 16
HD = 32
FF = 2048
WIN = 10
WT = 100
RELS = 361
SPAN = 2 * WIN - 1

QUADS = 4
WIDTH = QUADS * C2
CW = 2
RW = 104
R = CW * RW
JP = 112
LN = 128
GROUPS = 4
PER = 4
LAG = 3
SLOTS = LAG + 1
UNPACK_LAG = LAG + 2
RB = 16
TILE = 512
EPS = 1e-05
LOG2E = 1.4426950408889634
SCALE = HD ** (-0.5)

MESH = pl.DeviceIdType.MESH
F32 = jnp.float32
BF16 = jnp.bfloat16

O_QB, O_VB, O_PB, O_FC1B, O_FC2B = 0, 512, 1024, 1536, 3584
O_N1G, O_N1B, O_N2G, O_N2B, O_N0G, O_N0B, O_END = 4096, 4608, 5120, 5632, 6144, 7168, 8192


MATRICES = ((DM, FF), (FF, DM), (DM, 3 * DM), (DM, DM), (WIDTH, DM))


def dot(a, b):
    return lax.dot_general(a, b, (((1,), (0,)), ((), ())), preferred_element_type=F32)


def dot_nt(a, b):
    return lax.dot_general(a, b, (((1,), (1,)), ((), ())), preferred_element_type=F32)


def dot_tn(a, b):
    return lax.dot_general(a, b, (((0,), (0,)), ((), ())), preferred_element_type=F32)


def normalised(v):
    centred = v - jnp.mean(v, axis=-1, keepdims=True)
    inv = lax.rsqrt(jnp.mean(centred * centred, axis=-1, keepdims=True) + EPS)
    return centred * inv, inv


def norm_back(d_out, gain, xhat, inv):
    u = d_out * gain
    mean_u = jnp.mean(u, axis=-1, keepdims=True)
    mean_ux = jnp.mean(u * xhat, axis=-1, keepdims=True)
    return (u - mean_u - xhat * mean_ux) * inv


def fold(v):
    total = v[0:8]
    for r in range(8, v.shape[0], 8):
        total = total + v[r : r + 8]
    return total


def gelu_parts(x):
    z = jnp.abs(x) * 0.7071067811865476
    t = 1.0 / (1.0 + 0.3275911 * z)
    e = jnp.exp2(x * x * (-0.5 * LOG2E))
    poly = ((((1.061405429 * t - 1.453152027) * t + 1.421413741) * t - 0.284496736) * t + 0.254829592) * t
    half = 0.5 * poly * e
    cdf = jnp.where(x < 0, half, 1.0 - half)
    return x * cdf, cdf + x * e * 0.3989422804014327


def split3(v):
    hi = v.astype(BF16)
    rest = v - hi.astype(F32)
    mid = rest.astype(BF16)
    low = (rest - mid.astype(F32)).astype(BF16)
    return hi, mid, low


def offset_of(j):
    return (j // WIN) * SPAN + j % WIN


def kernel(
    n_head, n_win, n_chunk, share,
    x_hbm, wp_hbm, n0g, n0b, n1g, n1b, wqkv_hbm, qb, vb, table, wproj_hbm, pb, n2g, n2b,
    wfc1_hbm, fc1b, wfc2_hbm, fc2b, valid, cot_hbm,
    *refs,
):
    if n_win is None:
        (out_ref, sect_hbm, g_fc1, g_fc2, g_qkv, g_proj, g_red, g_small), refs = refs[:8], refs[8:]
    else:
        (out_ref, sect_hbm, o_fc1, o_fc2, o_qkv, o_proj, o_red, g_small), refs = refs[:8], refs[8:]
        (g_fc1, g_fc2, g_qkv, g_proj, g_red), refs = refs[:5], refs[5:]
        first_in, refs = refs[:5], refs[5:]
        plane_in, refs = refs[:5], refs[5:]
        near_in, refs = refs[:5], refs[5:]
        far_in, refs = refs[:5], refs[5:]
        (gather_in, small_in, sum_send, sum_recv), refs = refs[:4], refs[4:]
    (xv, send_in, rin, rout, wp, wqkv, wproj, wfc1, wfc2, cot,
    nrm, res, fst, qkv, prob, att, stage, sec, sn, dy, wide, act, dh, ffo, dsn, dsec, dpk, d_heads, sums, bias_t, ds_acc,
    in_send, in_recv, out_send, out_recv, x_sem, w_sem, own_sem, sect_sem) = refs
    me = lax.axis_index("head")
    lanes = QUADS * share

    def peer(k):
        return lax.rem(me + k, n_head)

    if n_win is not None:
        my_win = lax.axis_index("win")
        core, my_z = lax.rem(me, 2), me // 2
        n_z = n_head // 2
        sibling = me + 1 - 2 * core
        near_z = my_z + 1 - 2 * lax.rem(my_z, 2)
        far_z = my_z + 2 - 4 * (my_z // 2)

        def win_peer(k):
            return lax.rem(my_win + k, n_win)

        class Scatter:
            def __init__(self, spot, total, hold, out, by_head=False):
                self.spot, self.total, self.hold, self.out = spot, total, hold, out
                self.rows = total.shape[0] // (n_win * n_head)
                self.cols = total.shape[1]
                self.by_head = by_head
                half = total.shape[0] // 2
                self.at_plane = half
                self.at_near = half + (n_win - 1) * n_z * self.rows
                self.at_far = self.at_near + (n_z // 2) * self.rows

            def block(self, w, z, c):
                head = z * 2 + c
                spot = head * n_win + w if self.by_head else w * n_head + head
                return pl.ds(pl.multiple_of(spot * self.rows, 16), self.rows)

            def span(self, start, count=1):
                return pl.ds(pl.multiple_of(start, 16), count * self.rows)

            def copy(self, j, source, target, to):
                return pltpu.make_async_remote_copy(
                    src_ref=source, dst_ref=target, send_sem=sum_send.at[self.spot, j], recv_sem=sum_recv.at[self.spot, j],
                    device_id=to, device_id_type=MESH,
                )

            def pair_copy(self):
                return self.copy(
                    0, self.hold.at[pl.ds(0, self.at_plane), :], first_in[self.spot], {"head": sibling}
                )

            def plane_copy(self, k):
                source = self.hold.at[self.span(self.at_plane + (k - 1) * n_z * self.rows, n_z), :]
                return self.copy(k, source, plane_in[self.spot].at[k - 1], {"win": win_peer(k)})

            def near_copy(self):
                source = self.hold.at[self.span(self.at_near, n_z // 2), :]
                return self.copy(n_win, source, near_in[self.spot], {"head": near_z * 2 + core})

            def far_copy(self):
                source = self.hold.at[self.span(self.at_far), :]
                return self.copy(n_win + 1, source, far_in[self.spot], {"head": far_z * 2 + core})

            def start_pair(self):
                def body(i, carry):
                    w, z = i // n_z, lax.rem(i, n_z)
                    self.hold[self.span(i * self.rows), :] = self.total[self.block(w, z, 1 - core), :].astype(BF16)
                    return carry

                lax.fori_loop(0, n_win * n_z, body, 0)
                self.pair_copy().start()

            def start_plane(self):
                self.pair_copy().wait_recv()
                for k in range(1, n_win + 1):
                    w = lax.rem(my_win + k, n_win)

                    def body(z, carry):
                        mine = self.block(w, z, core)
                        value = self.total[mine, :] + first_in[self.spot][
                            self.span((w * n_z + z) * self.rows), :
                        ].astype(F32)
                        if k == n_win:
                            self.total[mine, :] = value
                        else:
                            at = self.at_plane + ((k - 1) * n_z + z) * self.rows
                            self.hold[self.span(at), :] = value.astype(BF16)
                        return carry

                    lax.fori_loop(0, n_z, body, 0)
                    if k < n_win:
                        self.plane_copy(k).start()

            def start_near(self):
                for k in range(1, n_win):
                    self.plane_copy(k).wait_recv()

                def both(z):
                    value = self.total[self.block(my_win, z, core), :]
                    for k in range(1, n_win):
                        value = value + plane_in[self.spot][k - 1, self.span(z * self.rows), :].astype(F32)
                    return value

                for j in range(n_z // 2):
                    sent = both(j * 2 + lax.rem(near_z, 2))
                    self.hold[self.span(self.at_near + j * self.rows), :] = sent.astype(BF16)
                self.near_copy().start()
                for j in range(n_z // 2):
                    z = j * 2 + lax.rem(my_z, 2)
                    self.total[self.block(my_win, z, core), :] = both(z)

            def after_near(self, j):
                kept = self.total[self.block(my_win, j * 2 + lax.rem(my_z, 2), core), :]
                return kept + near_in[self.spot][self.span(j * self.rows), :].astype(F32)

            def start_far(self):
                self.near_copy().wait_recv()
                self.hold[self.span(self.at_far), :] = self.after_near(far_z // 2).astype(BF16)
                self.far_copy().start()

            def finish(self):
                self.far_copy().wait_recv()
                value = self.after_near(my_z // 2) + far_in[self.spot][...].astype(F32)
                if not self.by_head:
                    self.out[...] = value
                    return
                gather_in[my_win] = value.astype(BF16)
                for k in range(1, n_win):
                    self.gather_copy(k).start()

            def gather_copy(self, k):
                return self.copy(
                    n_win + 1 + k, gather_in.at[my_win], gather_in.at[my_win], {"win": win_peer(k)}
                )

            def finish_gather(self):
                for k in range(1, n_win):
                    source = lax.rem(my_win + n_win - k, n_win)
                    self.copy(
                        n_win + 1 + k, gather_in.at[my_win], gather_in.at[source], {"win": win_peer(k)}
                    ).wait_recv()
                for w in range(n_win):
                    self.out[w * self.rows : (w + 1) * self.rows, :] = gather_in[w].astype(F32)

            def drain(self):
                self.pair_copy().wait_send()
                for k in range(1, n_win):
                    self.plane_copy(k).wait_send()
                    if self.by_head:
                        self.gather_copy(k).wait_send()
                self.near_copy().wait_send()
                self.far_copy().wait_send()

        feeds = [Scatter(0, g_fc1, wfc1, o_fc1), Scatter(1, g_fc2, wfc2, o_fc2)]
        others = [Scatter(2, g_qkv, wqkv, o_qkv), Scatter(3, g_proj, wproj, o_proj), Scatter(4, g_red, wp, o_red, True)]

        def small_copy(j, source, target, to):
            return pltpu.make_async_remote_copy(
                src_ref=small_in.at[source], dst_ref=small_in.at[target], send_sem=sum_send.at[5, j],
                recv_sem=sum_recv.at[5, j], device_id=to, device_id_type=MESH,
            )

        at_pair, at_plane, at_near, at_far = 0, 2, 2 + n_win, 4 + n_win

        def small_pair():
            return small_copy(0, at_pair, at_pair + 1, {"head": sibling})

        def small_plane(k, target=None):
            return small_copy(k, at_plane + my_win, at_plane + (my_win if target is None else target), {"win": win_peer(k)})

        def small_near():
            return small_copy(n_win, at_near, at_near + 1, {"head": near_z * 2 + core})

        def small_far():
            return small_copy(n_win + 1, at_far, at_far + 1, {"head": far_z * 2 + core})

    def in_copy(c, k):
        to = peer(k)
        return pltpu.make_async_remote_copy(
            src_ref=send_in.at[c, to], dst_ref=rin.at[c, me], send_sem=in_send.at[c, k], recv_sem=in_recv.at[c, k],
            device_id={"head": to}, device_id_type=MESH,
        )

    def out_copy(c, k):
        to = peer(k)
        return pltpu.make_async_remote_copy(
            src_ref=rin.at[c, to], dst_ref=rout.at[c, me], send_sem=out_send.at[c, k], recv_sem=out_recv.at[c, k],
            device_id={"head": to}, device_id_type=MESH,
        )

    def own_in(c):
        return pltpu.make_async_copy(send_in.at[c, me], rin.at[c, me], own_sem)

    def own_out(c):
        return pltpu.make_async_copy(rin.at[c, me], rout.at[c, me], own_sem)

    def x_copy(c):
        return pltpu.make_async_copy(x_hbm.at[:, c], xv.at[c % 2], x_sem.at[c % 2])

    def sect_copy(c):
        return pltpu.make_async_copy(xv.at[c % 2], sect_hbm.at[:, c], sect_sem.at[c % 2])

    weights = [
        pltpu.make_async_copy(wqkv_hbm, wqkv, w_sem.at[1]),
        pltpu.make_async_copy(wproj_hbm, wproj, w_sem.at[2]),
        pltpu.make_async_copy(wfc1_hbm, wfc1, w_sem.at[3]),
        pltpu.make_async_copy(wfc2_hbm, wfc2, w_sem.at[4]),
        pltpu.make_async_copy(cot_hbm, cot, w_sem.at[5]),
    ]

    for c in range(min(2, n_chunk)):
        x_copy(c).start()
    barrier = pltpu.get_barrier_semaphore()
    for k in range(1, n_head):
        pl.semaphore_signal(barrier, inc=1, device_id={"head": peer(k)}, device_id_type=MESH)
    if n_win is not None:
        for k in range(1, n_win):
            pl.semaphore_signal(barrier, inc=1, device_id={"win": win_peer(k)}, device_id_type=MESH)
    for q in range(QUADS):
        for s in range(n_head):
            pltpu.make_async_copy(
                wp_hbm.at[q, s], wp.at[pl.ds((s * QUADS + q) * share, share), :], w_sem.at[0]
            ).start()
    for w in weights:
        w.start()

    eye_rows = (
        lax.broadcasted_iota(jnp.int32, (RW, WT), 0) == lax.broadcasted_iota(jnp.int32, (RW, WT), 1)
    ).astype(F32).astype(BF16)
    eye_lanes = (
        lax.broadcasted_iota(jnp.int32, (lanes, lanes), 0) == lax.broadcasted_iota(jnp.int32, (lanes, lanes), 1)
    ).astype(F32).astype(BF16)

    def repack(c):
        x_copy(c).wait()
        for d in range(n_head):
            rows = [dot_nt(eye_rows, xv[c % 2, d, w]) for w in range(CW)]
            send_in[c, d] = jnp.concatenate(rows, axis=0).astype(BF16)

    def send(c):
        for k in range(1, n_head):
            in_copy(c, k).start()
        own_in(c).start()
        own_in(c).wait()

    repack(0)
    pl.semaphore_wait(barrier, n_head - 1 + (0 if n_win is None else n_win - 1))
    send(0)

    def send_rest(c, carry):
        @pl.when(c < n_chunk - 1)
        def _():
            x_copy(c + 1).start()

        repack(c)
        send(c)
        return carry

    lax.fori_loop(1, n_chunk, send_rest, 0)

    def zero(ref):
        def body(r, carry):
            ref[pl.ds(pl.multiple_of(r * 8, 8), 8), :] = jnp.zeros((8, ref.shape[1]), F32)
            return carry
        lax.fori_loop(0, ref.shape[0] // 8, body, 0)

    for ref in (g_fc1, g_fc2, g_qkv, g_proj, g_red, sums):
        zero(ref)
    ds_acc[...] = jnp.zeros_like(ds_acc)

    def zero_heads(c, carry):
        qkv[c] = jnp.zeros(qkv.shape[1:], BF16)
        return carry

    lax.fori_loop(0, SLOTS, zero_heads, 0)
    d_heads[...] = jnp.zeros_like(d_heads)
    bias_t[:, WT:, :] = jnp.full((HEADS, JP - WT, LN), -1e30, F32)

    spot = lax.broadcasted_iota(jnp.int32, (2 * LN, LN), 0)
    token = lax.broadcasted_iota(jnp.int32, (2 * LN, LN), 1)
    token_row = (token * 205) >> 11
    pick = ((spot == token_row * SPAN + token - token_row * WIN) & (token < WT)).astype(F32).astype(BF16)
    for row in range(WIN):
        parts = []
        for col in range(WIN):
            off = offset_of(WT - 1) - offset_of(row * WIN + col)
            parts.append(table[:, off : off + 2 * LN])
        hi, mid, low = split3(jnp.concatenate(parts, axis=0))
        found = (dot(hi, pick) + dot(mid, pick) + dot(low, pick)) * LOG2E
        for col in range(WIN):
            bias_t[:, row * WIN + col, :] = found[col * HEADS : (col + 1) * HEADS]

    pltpu.make_async_copy(wp, wp, w_sem.at[0]).wait()
    for w in weights:
        w.wait()

    lane = lax.broadcasted_iota(jnp.int32, (1, LN), 1)
    masks = [((lane >= h * HD) & (lane < (h + 1) * HD)).astype(F32).astype(BF16) for h in range(PER)]

    def by_head(v):
        return jnp.concatenate([v * m for m in masks], axis=0)

    def merged_rows(c, r):
        return jnp.concatenate([rin[c, s, pl.ds(r, RB), :] for s in range(n_head)], axis=1).astype(F32)

    def padded(v):
        return jnp.concatenate([v, jnp.zeros((JP - RW, v.shape[1]), F32)], axis=0)

    def first_half(c):
        p = lax.rem(c, SLOTS)
        for k in range(1, n_head):
            in_copy_wait = pltpu.make_async_remote_copy(
                src_ref=send_in.at[c, me], dst_ref=rin.at[c, lax.rem(me + n_head - k, n_head)],
                send_sem=in_send.at[c, k], recv_sem=in_recv.at[c, k],
                device_id={"head": peer(k)}, device_id_type=MESH,
            )
            in_copy_wait.wait_recv()
        for r in range(0, R, RB):
            xhat, unused = normalised(merged_rows(c, r))
            nrm[r : r + RB, :] = (xhat * n0g[...] + n0b[...]).astype(BF16)
        res[p] = dot(nrm[...], wp[...])
        for r in range(0, R, RB):
            xhat, unused = normalised(res[p, r : r + RB, :])
            fst[r : r + RB, :] = (xhat * n1g[...] + n1b[...]).astype(BF16)
        for t in range(3):
            part = dot(fst[...], wqkv[:, t * DM : (t + 1) * DM])
            if t == 0:
                part = part + qb[...]
            if t == 2:
                part = part + vb[...]
            for w in range(CW):
                for g in range(GROUPS):
                    piece = part[w * RW : (w + 1) * RW, g * LN : (g + 1) * LN]
                    qkv[p, w, t, g, 0:JP, :] = padded(piece).astype(BF16)

        def attend(w, carry):
            for g in range(GROUPS):
                scores = dot_nt(qkv[p, w, 1, g, 0:JP, :], by_head(qkv[p, w, 0, g]))
                found = []
                for h in range(PER):
                    s = scores[:, h * LN : (h + 1) * LN] * (SCALE * LOG2E) + bias_t[g * PER + h]
                    e = jnp.exp2(s - jnp.max(s, axis=0, keepdims=True))
                    found.append((e * (1.0 / jnp.sum(e, axis=0, keepdims=True))).astype(BF16))
                probs = jnp.concatenate(found, axis=1)
                prob[p, w, g] = probs
                mixed = dot_tn(qkv[p, w, 2, g, 0:JP, :], probs)
                own = jnp.concatenate(
                    [mixed[h * HD : (h + 1) * HD, h * LN : (h + 1) * LN] for h in range(PER)], axis=0
                )
                stage[pl.ds(pl.multiple_of(w * RW, 8), RW), g * LN : (g + 1) * LN] = own.T[0:RW]
            return carry

        lax.fori_loop(0, CW, attend, 0)
        att[p] = stage[:, 0:DM].astype(BF16)
        sec[...] = res[p] + dot(att[p], wproj[...]) + pb[...]
        for r in range(0, R, RB):
            xhat, unused = normalised(sec[r : r + RB, :])
            sn[r : r + RB, :] = (xhat * n2g[...] + n2b[...]).astype(BF16)
        flags = [valid[c * CW + w].astype(F32) for w in range(CW)]
        tail = jnp.zeros((RW - WT, DM), F32)
        pieces = []
        for w in range(CW):
            pieces += [cot[c * CW + w].astype(F32) * flags[w], tail]
        up = jnp.concatenate(pieces, axis=0)
        dy[...] = up.astype(BF16)
        sums[:, O_FC2B : O_FC2B + DM] += fold(up)
        ffo[...] = sec[...] + fc2b[...]
        dsn[...] = jnp.zeros_like(dsn)

        def feed(t, carry):
            cols = pl.ds(pl.multiple_of(t * TILE, TILE), TILE)
            wide[:, 0:TILE] = dot(sn[...], wfc1[:, cols]) + fc1b[:, cols]
            wide[:, TILE : 2 * TILE] = dot_nt(dy[...], wfc2[cols, :])
            total = jnp.zeros((8, TILE), F32)
            for r in range(0, R, RB):
                value, slope = gelu_parts(wide[r : r + RB, 0:TILE])
                act[r : r + RB, :] = value.astype(BF16)
                low = (wide[r : r + RB, TILE : 2 * TILE] * slope).astype(BF16)
                dh[r : r + RB, :] = low
                total = total + fold(low.astype(F32))
            sums[:, pl.ds(pl.multiple_of(O_FC1B + t * TILE, TILE), TILE)] += total
            ffo[...] += dot(act[...], wfc2[cols, :])
            dsn[...] += dot_nt(dh[...], wfc1[:, cols])
            g_fc2[cols, :] += dot_tn(act[...], dy[...])
            g_fc1[:, cols] += dot_tn(sn[...], dh[...])
            return carry

        lax.fori_loop(0, FF // TILE, feed, 0)
        for w in range(CW):
            out_ref[c * CW + w] = (ffo[w * RW : w * RW + WT, :] * flags[w]).astype(BF16)
        sum_g = jnp.zeros((8, DM), F32)
        sum_b = jnp.zeros((8, DM), F32)
        for r in range(0, R, RB):
            xhat, inv = normalised(sec[r : r + RB, :])
            d_out = dsn[r : r + RB, :]
            sum_g = sum_g + fold(d_out * xhat)
            sum_b = sum_b + fold(d_out)
            dsec[p, r : r + RB, :] = norm_back(d_out, n2g[...], xhat, inv) + dy[r : r + RB, :].astype(F32)
        sums[:, O_N2G : O_N2G + DM] += sum_g
        sums[:, O_N2B : O_N2B + DM] += sum_b

    def second_half(c):
        p = lax.rem(c, SLOTS)
        low = dsec[p].astype(BF16)
        sums[:, O_PB : O_PB + DM] += fold(low.astype(F32))
        dy[...] = low
        g_proj[...] += dot_tn(att[p], dy[...])
        back = dot_nt(dy[...], wproj[...])
        for w in range(CW):
            for g in range(GROUPS):
                piece = back[w * RW : (w + 1) * RW, g * LN : (g + 1) * LN]
                d_heads[w, g, 0:JP, :] = padded(piece).astype(BF16)

        def attend(w, carry):
            for g in range(GROUPS):
                d_out = by_head(d_heads[w, g])
                q_all = by_head(qkv[p, w, 0, g])
                d_probs = dot_nt(qkv[p, w, 2, g, 0:JP, :], d_out)
                raw = []
                for h in range(PER):
                    pr = prob[p, w, g, :, h * LN : (h + 1) * LN].astype(F32)
                    dp = d_probs[:, h * LN : (h + 1) * LN]
                    pd = pr * dp
                    d_s = pd - pr * jnp.sum(pd, axis=0, keepdims=True)
                    ds_acc[g * PER + h] += d_s
                    raw.append((d_s * SCALE).astype(BF16))
                d_raw = jnp.concatenate(raw, axis=1)
                rows = pl.ds(pl.multiple_of(w * RW, 8), RW)
                d_v = dot(prob[p, w, g], d_out)
                d_k = dot(d_raw, q_all)
                mixed = dot_tn(qkv[p, w, 1, g, 0:JP, :], d_raw)
                own = jnp.concatenate(
                    [mixed[h * HD : (h + 1) * HD, h * LN : (h + 1) * LN] for h in range(PER)], axis=0
                )
                stage[rows, g * LN : (g + 1) * LN] = own.T[0:RW]
                stage[rows, DM + g * LN : DM + (g + 1) * LN] = d_k[0:RW]
                stage[rows, 2 * DM + g * LN : 2 * DM + (g + 1) * LN] = d_v[0:RW]
            return carry

        lax.fori_loop(0, CW, attend, 0)
        sum_g = jnp.zeros((8, DM), F32)
        sum_b = jnp.zeros((8, DM), F32)
        sum_q = jnp.zeros((8, DM), F32)
        sum_v = jnp.zeros((8, DM), F32)
        for r in range(0, R, RB):
            low = stage[r : r + RB, :].astype(BF16)
            dpk[r : r + RB, :] = low
            sum_q = sum_q + fold(low[:, 0:DM].astype(F32))
            sum_v = sum_v + fold(low[:, 2 * DM :].astype(F32))
        sums[:, O_QB : O_QB + DM] += sum_q
        sums[:, O_VB : O_VB + DM] += sum_v
        dsn[...] = dot_nt(dpk[...], wqkv[...])
        for r in range(0, R, RB):
            xhat, inv = normalised(res[p, r : r + RB, :])
            fst[r : r + RB, :] = (xhat * n1g[...] + n1b[...]).astype(BF16)
            d_out = dsn[r : r + RB, :]
            sum_g = sum_g + fold(d_out * xhat)
            sum_b = sum_b + fold(d_out)
            d_res = norm_back(d_out, n1g[...], xhat, inv) + dsec[p, r : r + RB, :]
            sn[r : r + RB, :] = d_res.astype(BF16)
        sums[:, O_N1G : O_N1G + DM] += sum_g
        sums[:, O_N1B : O_N1B + DM] += sum_b
        wide[...] = dot_nt(sn[...], wp[...])
        sum_g = jnp.zeros((8, WIDTH), F32)
        sum_b = jnp.zeros((8, WIDTH), F32)
        for r in range(0, R, RB):
            xhat, inv = normalised(merged_rows(c, r))
            nrm[r : r + RB, :] = (xhat * n0g[...] + n0b[...]).astype(BF16)
            d_out = wide[r : r + RB, :]
            sum_g = sum_g + fold(d_out * xhat)
            sum_b = sum_b + fold(d_out)
            low = norm_back(d_out, n0g[...], xhat, inv).astype(BF16)
            for s in range(n_head):
                rin[c, s, r : r + RB, :] = low[:, s * lanes : (s + 1) * lanes]
        sums[:, O_N0G : O_N0G + WIDTH] += sum_g
        sums[:, O_N0B : O_N0B + WIDTH] += sum_b
        for k in range(1, n_head):
            out_copy(c, k).start()
        own_out(c).start()
        g_qkv[...] += dot_tn(fst[...], dpk[...])
        g_red[...] += dot_tn(nrm[...], sn[...])
        own_out(c).wait()

    def unpack(c):
        for k in range(1, n_head):
            pltpu.make_async_remote_copy(
                src_ref=rin.at[c, me], dst_ref=rout.at[c, lax.rem(me + n_head - k, n_head)],
                send_sem=out_send.at[c, k], recv_sem=out_recv.at[c, k],
                device_id={"head": peer(k)}, device_id_type=MESH,
            ).wait_recv()

        @pl.when(c >= 2)
        def _():
            sect_copy(c - 2).wait()

        for s in range(n_head):
            turned = dot_nt(eye_lanes, rout[c, s])
            for w in range(CW):
                xv[lax.rem(c, 2), s, w] = turned[:, w * RW : w * RW + WT].astype(BF16)
        sect_copy(c).start()

    def step(s, carry):
        @pl.when(s < n_chunk)
        def _():
            first_half(s)

        if n_win is not None:
            @pl.when(s == n_chunk - 1)
            def _():
                for f in feeds:
                    f.start_pair()

            @pl.when(s == n_chunk)
            def _():
                for f in feeds:
                    f.start_plane()

        @pl.when((s >= LAG) & (s < n_chunk + LAG))
        def _():
            second_half(s - LAG)

        if n_win is not None:
            @pl.when(s == n_chunk + LAG - 1)
            def _():
                for f in others:
                    f.start_pair()
                table_sums()
                small_in[at_pair, 0:HEADS, :] = vector_rows()
                small_pair().start()

            @pl.when(s == n_chunk + LAG)
            def _():
                for f in feeds:
                    f.start_near()
                for f in others:
                    f.start_plane()
                small_pair().wait_recv()
                small_in[at_plane + my_win] = small_in[at_pair] + small_in[at_pair + 1]
                for k in range(1, n_win):
                    small_plane(k).start()
                for f in feeds:
                    f.start_far()

        @pl.when(s >= UNPACK_LAG)
        def _():
            unpack(s - UNPACK_LAG)

        return carry

    def vector_rows():
        row = jnp.sum(sums[...], axis=0, keepdims=True)
        return jnp.concatenate([row[:, r * DM : (r + 1) * DM] for r in range(O_END // DM)], axis=0)

    def table_sums():
        total = jnp.zeros((HEADS, 4 * LN), F32)
        for row in range(WIN):
            spread = jnp.zeros((WIN * HEADS, 2 * LN), F32)
            whole = jnp.concatenate([ds_acc[:, row * WIN + col, :] for col in range(WIN)], axis=0)
            for part in split3(whole):
                spread = spread + dot_nt(part, pick)
            for col in range(WIN):
                off = offset_of(WT - 1) - offset_of(row * WIN + col)
                piece = jnp.concatenate(
                    [spread[col * HEADS : (col + 1) * HEADS], jnp.zeros((HEADS, 2 * LN), F32)], axis=1
                )
                total = total + pltpu.roll(piece, off, 1)
        if n_win is None:
            g_small[HEADS:, :] = total
        else:
            small_in[at_pair, HEADS:, :] = total

    lax.fori_loop(0, n_chunk + UNPACK_LAG, step, 0)
    for c in range(max(0, n_chunk - 2), n_chunk):
        sect_copy(c).wait()

    if n_win is None:
        g_small[0:HEADS, :] = vector_rows()
        table_sums()
    else:
        for f in others:
            f.start_near()
        for k in range(1, n_win):
            small_plane(k, lax.rem(my_win + n_win - k, n_win)).wait_recv()
        total = small_in[at_plane]
        for w in range(1, n_win):
            total = total + small_in[at_plane + w]
        small_in[at_near] = total
        small_near().start()
        for f in feeds:
            f.finish()
        for f in others:
            f.start_far()
        small_near().wait_recv()
        small_in[at_far] = small_in[at_near] + small_in[at_near + 1]
        small_far().start()
        for f in reversed(others):
            f.finish()
        small_far().wait_recv()
        g_small[...] = small_in[at_far] + small_in[at_far + 1]
        others[-1].finish_gather()
        for f in feeds + others:
            f.drain()
        small_pair().wait_send()
        for k in range(1, n_win):
            small_plane(k).wait_send()
        small_near().wait_send()
        small_far().wait_send()

    def drain(c, carry):
        for k in range(1, n_head):
            in_copy(c, k).wait_send()
            out_copy(c, k).wait_send()
        return carry

    lax.fori_loop(0, n_chunk, drain, 0)


def run_kernel(n_head, n_win, n_chunk, share, args):
    lanes = QUADS * share
    any_, vmem = pl.BlockSpec(memory_space=pl.ANY), pl.BlockSpec(memory_space=pltpu.VMEM)
    smem = pl.BlockSpec(memory_space=pltpu.SMEM)
    windows = n_chunk * CW
    in_specs = [
        any_, any_, vmem, vmem, vmem, vmem, any_, vmem, vmem, vmem, any_, vmem, vmem, vmem,
        any_, vmem, any_, vmem, smem, any_,
    ]
    out_shape = [
        jax.ShapeDtypeStruct((windows, WT, DM), BF16),
        jax.ShapeDtypeStruct((n_head, n_chunk, CW, lanes, WT), BF16),
    ]
    dma = pltpu.SemaphoreType.DMA
    scratch = []
    if n_win is None:
        out_shape += [jax.ShapeDtypeStruct(m, F32) for m in MATRICES]
    else:
        devices, n_z = n_win * n_head, n_head // 2
        scratch += [pltpu.VMEM(m, F32) for m in MATRICES]
        shares = [(m // devices, cols) for m, cols in MATRICES]
        out_shape += [jax.ShapeDtypeStruct(m, F32) for m in shares[:-1]]
        out_shape += [jax.ShapeDtypeStruct((shares[-1][0] * n_win, DM), F32)]
        scratch += [pltpu.VMEM((rows * n_win * n_z, cols), BF16) for rows, cols in shares]
        scratch += [pltpu.VMEM((n_win - 1, rows * n_z, cols), BF16) for rows, cols in shares]
        scratch += [pltpu.VMEM((rows * (n_z // 2), cols), BF16) for rows, cols in shares]
        scratch += [pltpu.VMEM((rows, cols), BF16) for rows, cols in shares]
        scratch += [
            pltpu.VMEM((n_win, shares[-1][0], DM), BF16),
            pltpu.VMEM((n_win + 6, 2 * HEADS, DM), F32),
            dma((6, 2 * n_win + 2)), dma((6, 2 * n_win + 2)),
        ]
    out_shape += [jax.ShapeDtypeStruct((2 * HEADS, DM), F32)]
    out_specs = [vmem, any_] + [vmem] * 6
    scratch += [
        pltpu.VMEM((2, n_head, CW, lanes, WT), BF16),
        pltpu.VMEM((n_chunk, n_head, R, lanes), BF16),
        pltpu.VMEM((n_chunk, n_head, R, lanes), BF16),
        pltpu.VMEM((n_chunk, n_head, R, lanes), BF16),
        pltpu.VMEM((WIDTH, DM), BF16),
        pltpu.VMEM((DM, 3 * DM), BF16),
        pltpu.VMEM((DM, DM), BF16),
        pltpu.VMEM((DM, FF), BF16),
        pltpu.VMEM((FF, DM), BF16),
        pltpu.VMEM((windows, WT, DM), BF16),
        pltpu.VMEM((R, WIDTH), BF16),
        pltpu.VMEM((SLOTS, R, DM), F32),
        pltpu.VMEM((R, DM), BF16),
        pltpu.VMEM((SLOTS, CW, 3, GROUPS, LN, LN), BF16),
        pltpu.VMEM((SLOTS, CW, GROUPS, JP, PER * LN), BF16),
        pltpu.VMEM((SLOTS, R, DM), BF16),
        pltpu.VMEM((R, 3 * DM), F32),
        pltpu.VMEM((R, DM), F32),
        pltpu.VMEM((R, DM), BF16),
        pltpu.VMEM((R, DM), BF16),
        pltpu.VMEM((R, WIDTH), F32),
        pltpu.VMEM((R, TILE), BF16),
        pltpu.VMEM((R, TILE), BF16),
        pltpu.VMEM((R, DM), F32),
        pltpu.VMEM((R, DM), F32),
        pltpu.VMEM((SLOTS, R, DM), F32),
        pltpu.VMEM((R, 3 * DM), BF16),
        pltpu.VMEM((CW, GROUPS, LN, LN), BF16),
        pltpu.VMEM((8, O_END), F32),
        pltpu.VMEM((HEADS, JP, LN), F32),
        pltpu.VMEM((HEADS, JP, LN), F32),
        dma((n_chunk, n_head)), dma((n_chunk, n_head)), dma((n_chunk, n_head)), dma((n_chunk, n_head)),
        dma((2,)), dma((6,)), dma, dma((2,)),
    ]
    return pl.pallas_call(
        functools.partial(kernel, n_head, n_win, n_chunk, share),
        out_shape=out_shape, in_specs=in_specs, out_specs=out_specs, scratch_shapes=scratch,
        compiler_params=pltpu.CompilerParams(
            collective_id=0, has_side_effects=True, vmem_limit_bytes=63 * 1024 * 1024
        ),
        cost_estimate=pl.CostEstimate(flops=27 * 10**9, bytes_accessed=30 * 10**6, transcendentals=10**7),
    )(*args)


def local(
    n_head, section_rows, reduce_weight, norm0_gain, norm0_bias, norm1_gain, norm1_bias, qkv_weight, q_bias, v_bias,
    rel_table, proj_weight, proj_bias, norm2_gain, norm2_bias, fc1_weight, fc1_bias, fc2_weight, fc2_bias,
    window_valid, cotangent,
):
    group_windows, tokens, quads, share = section_rows.shape
    windows = cotangent.shape[0]
    n_chunk = windows // CW
    lanes = quads * share
    rows = section_rows.transpose(0, 2, 3, 1).reshape(n_head, n_chunk, CW, lanes, tokens)

    def by_source(v):
        return v.reshape(quads, n_head, share).transpose(1, 0, 2).reshape(1, WIDTH)

    def row(v):
        return v.reshape(1, -1)

    args = (
        rows, reduce_weight.reshape(quads, n_head, share, DM), by_source(norm0_gain), by_source(norm0_bias),
        row(norm1_gain), row(norm1_bias), qkv_weight, row(q_bias), row(v_bias),
        jnp.pad(rel_table, ((0, 0), (0, 4 * LN - RELS))), proj_weight, row(proj_bias), row(norm2_gain), row(norm2_bias),
        fc1_weight, row(fc1_bias), fc2_weight, row(fc2_bias), window_valid, cotangent,
    )
    n_win = lax.axis_size("win")
    devices = n_win * n_head
    inside = n_head == 8 and all((m // devices) % 16 == 0 for m, unused in MATRICES)
    block_out, section, fc1, fc2, qkv, proj, red, small = run_kernel(
        n_head, n_win if inside else None, n_chunk, share, args
    )
    section_grad = section.reshape(group_windows, quads, share, tokens).transpose(0, 3, 1, 2)
    both = ("win", "head")

    def scattered(v):
        return lax.psum_scatter(v.astype(BF16), both, scatter_dimension=0, tiled=True).astype(F32)

    if not inside:
        fc1, fc2, qkv, proj = scattered(fc1), scattered(fc2), scattered(qkv), scattered(proj)
        red = lax.psum_scatter(red.astype(BF16), "head", scatter_dimension=0, tiled=True)
        red = lax.psum(red, "win").astype(F32)
        small = lax.psum(small, both)
    reduce_grad = red.reshape(quads, share, DM)
    vectors, table_grad = small[:HEADS].reshape(-1), small[HEADS:, :RELS]
    at = lax.axis_index("win") * n_head + lax.axis_index("head")

    def part(start, length):
        size = length // devices
        return lax.dynamic_slice_in_dim(vectors, start + at * size, size)

    def part0(start):
        return lax.dynamic_slice_in_dim(vectors, start + lax.axis_index("head") * lanes, lanes).reshape(quads, share)

    return (
        block_out, section_grad, reduce_grad, part0(O_N0G), part0(O_N0B), part(O_N1G, DM), part(O_N1B, DM),
        qkv, part(O_QB, DM), part(O_VB, DM), table_grad, proj, part(O_PB, DM),
        part(O_N2G, DM), part(O_N2B, DM), fc1, part(O_FC1B, FF), fc2, part(O_FC2B, DM),
    )


def solution(mesh):
    in_specs = (
        P("win", None, None, "head"),
        P(),
        P(),
        P(),
        P(),
        P(),
        P(),
        P(),
        P(),
        P(),
        P(),
        P(),
        P(),
        P(),
        P(),
        P(),
        P(),
        P(),
        P(("win", "head")),
        P(("win", "head"), None, None),
    )
    out_specs = (
        P(("win", "head"), None, None),
        P("win", None, None, "head"),
        P(None, "head", None),
        P(None, "head"),
        P(None, "head"),
        P(("win", "head")),
        P(("win", "head")),
        P(("win", "head"), None),
        P(("win", "head")),
        P(("win", "head")),
        P(),
        P(("win", "head"), None),
        P(("win", "head")),
        P(("win", "head")),
        P(("win", "head")),
        P(("win", "head"), None),
        P(("win", "head")),
        P(("win", "head"), None),
        P(("win", "head")),
    )
    return jax.shard_map(
        functools.partial(local, mesh.shape["head"]), mesh=mesh, in_specs=in_specs, out_specs=out_specs, check_vma=False)
```

```python
import functools

import jax
import jax.numpy as jnp
from jax import lax
from jax.experimental import pallas as pl
from jax.experimental.pallas import tpu as pltpu
from jax.sharding import PartitionSpec as P

C2 = 256
DM = 512
HEADS = 16
HD = 32
FF = 2048
WIN = 10
WT = 100
RELS = 361
SPAN = 2 * WIN - 1

QUADS = 4
WIDTH = QUADS * C2
CW = 2
RW = 104
R = CW * RW
JP = 112
LN = 128
GROUPS = 4
PER = 4
LAG = 4
SLOTS = LAG + 1
AHEAD = 2
RB = 16
TILE = 512
EPS = 1e-05
LOG2E = 1.4426950408889634
SCALE = HD ** (-0.5)

MESH = pl.DeviceIdType.MESH
F32 = jnp.float32
BF16 = jnp.bfloat16

O_QB, O_VB, O_PB, O_FC1B, O_FC2B = 0, 512, 1024, 1536, 3584
O_N1G, O_N1B, O_N2G, O_N2B, O_N0G, O_N0B, O_END = 4096, 4608, 5120, 5632, 6144, 7168, 8192


MATRICES = ((DM, FF), (FF, DM), (DM, 3 * DM), (DM, DM), (WIDTH, DM))


def dot(a, b):
    return lax.dot_general(a, b, (((1,), (0,)), ((), ())), preferred_element_type=F32)


def dot_nt(a, b):
    return lax.dot_general(a, b, (((1,), (1,)), ((), ())), preferred_element_type=F32)


def dot_tn(a, b):
    return lax.dot_general(a, b, (((0,), (0,)), ((), ())), preferred_element_type=F32)


def normalised(v):
    centred = v - jnp.mean(v, axis=-1, keepdims=True)
    inv = lax.rsqrt(jnp.mean(centred * centred, axis=-1, keepdims=True) + EPS)
    return centred * inv, inv


def norm_back(d_out, gain, xhat, inv):
    u = d_out * gain
    mean_u = jnp.mean(u, axis=-1, keepdims=True)
    mean_ux = jnp.mean(u * xhat, axis=-1, keepdims=True)
    return (u - mean_u - xhat * mean_ux) * inv


def fold(v):
    total = v[0:8]
    for r in range(8, v.shape[0], 8):
        total = total + v[r : r + 8]
    return total


def weave(one, two):
    marks = [((i + 0.5) / len(one), piece) for i, piece in enumerate(one)]
    marks += [((i + 0.5) / len(two), piece) for i, piece in enumerate(two)]
    for unused, piece in sorted(marks, key=lambda m: m[0]):
        piece()


def gelu_parts(x):
    z = jnp.abs(x) * 0.7071067811865476
    t = 1.0 / (1.0 + 0.3275911 * z)
    e = jnp.exp2(x * x * (-0.5 * LOG2E))
    poly = ((((1.061405429 * t - 1.453152027) * t + 1.421413741) * t - 0.284496736) * t + 0.254829592) * t
    half = 0.5 * poly * e
    cdf = jnp.where(x < 0, half, 1.0 - half)
    return x * cdf, cdf + x * e * 0.3989422804014327


def split3(v):
    hi = v.astype(BF16)
    rest = v - hi.astype(F32)
    mid = rest.astype(BF16)
    low = (rest - mid.astype(F32)).astype(BF16)
    return hi, mid, low


def offset_of(j):
    return (j // WIN) * SPAN + j % WIN


def kernel(
    n_head, n_win, n_chunk, share,
    x_hbm, wp_hbm, n0g, n0b, n1g, n1b, wqkv_hbm, qb, vb, table, wproj_hbm, pb, n2g, n2b,
    wfc1_hbm, fc1b, wfc2_hbm, fc2b, valid, cot_hbm,
    *refs,
):
    if n_win is None:
        (out_ref, sect_hbm, g_fc1, g_fc2, g_qkv, g_proj, g_red, g_small), refs = refs[:8], refs[8:]
    else:
        (out_ref, sect_hbm, o_fc1, o_fc2, o_qkv, o_proj, o_red, g_small), refs = refs[:8], refs[8:]
        (g_fc1, g_fc2, g_qkv, g_proj, g_red), refs = refs[:5], refs[5:]
        first_in, refs = refs[:5], refs[5:]
        plane_in, refs = refs[:5], refs[5:]
        near_in, refs = refs[:5], refs[5:]
        far_in, refs = refs[:5], refs[5:]
        (gather_in, small_in, sum_send, sum_recv), refs = refs[:4], refs[4:]
    (xv, send_in, rin, wp, wqkv, wproj, wfc1, wfc2, cot,
    nrm, res, fst, qkv, prob, att, stage, sec, sn, dy, wide, slim, ffo, dsn, dsec, dpk, d_heads, owns, out_stage, sums, bias_t, ds_acc,
    in_send, in_recv, out_send, out_recv, x_sem, w_sem, cot_sem, own_sem, sect_sem, free_sem, done_sem) = refs
    rout = send_in
    me = lax.axis_index("head")
    lanes = QUADS * share

    def peer(k):
        return lax.rem(me + k, n_head)

    if n_win is not None:
        my_win = lax.axis_index("win")
        core, my_z = lax.rem(me, 2), me // 2
        n_z = n_head // 2
        sibling = me + 1 - 2 * core
        near_z = my_z + 1 - 2 * lax.rem(my_z, 2)
        far_z = my_z + 2 - 4 * (my_z // 2)

        def win_peer(k):
            return lax.rem(my_win + k, n_win)

        class Scatter:
            def __init__(self, spot, total, hold, out, by_head=False):
                self.spot, self.total, self.hold, self.out = spot, total, hold, out
                self.rows = total.shape[0] // (n_win * n_head)
                self.cols = total.shape[1]
                self.by_head = by_head
                half = total.shape[0] // 2
                self.at_plane = half
                self.at_near = half + (n_win - 1) * n_z * self.rows
                self.at_far = self.at_near + (n_z // 2) * self.rows

            def block(self, w, z, c):
                head = z * 2 + c
                spot = head * n_win + w if self.by_head else w * n_head + head
                return pl.ds(pl.multiple_of(spot * self.rows, 16), self.rows)

            def span(self, start, count=1):
                return pl.ds(pl.multiple_of(start, 16), count * self.rows)

            def copy(self, j, source, target, to):
                return pltpu.make_async_remote_copy(
                    src_ref=source, dst_ref=target, send_sem=sum_send.at[self.spot, j], recv_sem=sum_recv.at[self.spot, j],
                    device_id=to, device_id_type=MESH,
                )

            def pair_copy(self):
                return self.copy(
                    0, self.hold.at[pl.ds(0, self.at_plane), :], first_in[self.spot], {"head": sibling}
                )

            def plane_copy(self, k):
                source = self.hold.at[self.span(self.at_plane + (k - 1) * n_z * self.rows, n_z), :]
                return self.copy(k, source, plane_in[self.spot].at[k - 1], {"win": win_peer(k)})

            def near_copy(self):
                source = self.hold.at[self.span(self.at_near, n_z // 2), :]
                return self.copy(n_win, source, near_in[self.spot], {"head": near_z * 2 + core})

            def far_copy(self):
                source = self.hold.at[self.span(self.at_far), :]
                return self.copy(n_win + 1, source, far_in[self.spot], {"head": far_z * 2 + core})

            def start_pair(self):
                def body(i, carry):
                    w, z = i // n_z, lax.rem(i, n_z)
                    self.hold[self.span(i * self.rows), :] = self.total[self.block(w, z, 1 - core), :].astype(BF16)
                    return carry

                lax.fori_loop(0, n_win * n_z, body, 0)
                self.pair_copy().start()

            def start_plane(self):
                self.pair_copy().wait_recv()
                for k in range(1, n_win + 1):
                    w = lax.rem(my_win + k, n_win)

                    def body(z, carry):
                        mine = self.block(w, z, core)
                        value = self.total[mine, :] + first_in[self.spot][
                            self.span((w * n_z + z) * self.rows), :
                        ].astype(F32)
                        if k == n_win:
                            self.total[mine, :] = value
                        else:
                            at = self.at_plane + ((k - 1) * n_z + z) * self.rows
                            self.hold[self.span(at), :] = value.astype(BF16)
                        return carry

                    lax.fori_loop(0, n_z, body, 0)
                    if k < n_win:
                        self.plane_copy(k).start()

            def start_near(self):
                for k in range(1, n_win):
                    self.plane_copy(k).wait_recv()

                def both(z):
                    value = self.total[self.block(my_win, z, core), :]
                    for k in range(1, n_win):
                        value = value + plane_in[self.spot][k - 1, self.span(z * self.rows), :].astype(F32)
                    return value

                for j in range(n_z // 2):
                    sent = both(j * 2 + lax.rem(near_z, 2))
                    self.hold[self.span(self.at_near + j * self.rows), :] = sent.astype(BF16)
                self.near_copy().start()
                for j in range(n_z // 2):
                    z = j * 2 + lax.rem(my_z, 2)
                    self.total[self.block(my_win, z, core), :] = both(z)

            def after_near(self, j):
                kept = self.total[self.block(my_win, j * 2 + lax.rem(my_z, 2), core), :]
                return kept + near_in[self.spot][self.span(j * self.rows), :].astype(F32)

            def start_far(self):
                self.near_copy().wait_recv()
                self.hold[self.span(self.at_far), :] = self.after_near(far_z // 2).astype(BF16)
                self.far_copy().start()

            def finish(self):
                self.far_copy().wait_recv()
                value = self.after_near(my_z // 2) + far_in[self.spot][...].astype(F32)
                if not self.by_head:
                    self.out[...] = value
                    return
                gather_in[my_win] = value.astype(BF16)
                for k in range(1, n_win):
                    self.gather_copy(k).start()

            def gather_copy(self, k):
                return self.copy(
                    n_win + 1 + k, gather_in.at[my_win], gather_in.at[my_win], {"win": win_peer(k)}
                )

            def finish_gather(self):
                for k in range(1, n_win):
                    source = lax.rem(my_win + n_win - k, n_win)
                    self.copy(
                        n_win + 1 + k, gather_in.at[my_win], gather_in.at[source], {"win": win_peer(k)}
                    ).wait_recv()
                for w in range(n_win):
                    self.out[w * self.rows : (w + 1) * self.rows, :] = gather_in[w].astype(F32)

            def drain(self):
                self.pair_copy().wait_send()
                for k in range(1, n_win):
                    self.plane_copy(k).wait_send()
                    if self.by_head:
                        self.gather_copy(k).wait_send()
                self.near_copy().wait_send()
                self.far_copy().wait_send()

        feeds = [Scatter(0, g_fc1, wfc1, o_fc1), Scatter(1, g_fc2, wfc2, o_fc2)]
        others = [Scatter(2, g_qkv, wqkv, o_qkv), Scatter(3, g_proj, wproj, o_proj), Scatter(4, g_red, wp, o_red, True)]

        def small_copy(j, source, target, to):
            return pltpu.make_async_remote_copy(
                src_ref=small_in.at[source], dst_ref=small_in.at[target], send_sem=sum_send.at[5, j],
                recv_sem=sum_recv.at[5, j], device_id=to, device_id_type=MESH,
            )

        at_pair, at_plane, at_near, at_far = 0, 2, 2 + n_win, 4 + n_win

        def small_pair():
            return small_copy(0, at_pair, at_pair + 1, {"head": sibling})

        def small_plane(k, target=None):
            return small_copy(k, at_plane + my_win, at_plane + (my_win if target is None else target), {"win": win_peer(k)})

        def small_near():
            return small_copy(n_win, at_near, at_near + 1, {"head": near_z * 2 + core})

        def small_far():
            return small_copy(n_win + 1, at_far, at_far + 1, {"head": far_z * 2 + core})

    def in_copy(c, k):
        to = peer(k)
        return pltpu.make_async_remote_copy(
            src_ref=send_in.at[c, to], dst_ref=rin.at[c, me], send_sem=in_send.at[c, k], recv_sem=in_recv.at[c, k],
            device_id={"head": to}, device_id_type=MESH,
        )

    def out_copy(c, k):
        to = peer(k)
        return pltpu.make_async_remote_copy(
            src_ref=rin.at[c, to], dst_ref=rout.at[c, me], send_sem=out_send.at[c, k], recv_sem=out_recv.at[c, k],
            device_id={"head": to}, device_id_type=MESH,
        )

    def own_in(c):
        return pltpu.make_async_copy(send_in.at[c, me], rin.at[c, me], own_sem)

    def own_out(c):
        return pltpu.make_async_copy(rin.at[c, me], rout.at[c, me], own_sem)

    def x_copy(c):
        return pltpu.make_async_copy(x_hbm.at[:, c], xv.at[c % 2], x_sem.at[c % 2])

    def cot_copy(c):
        return pltpu.make_async_copy(cot_hbm.at[pl.ds(c * CW, CW)], cot.at[lax.rem(c, 2)], cot_sem.at[lax.rem(c, 2)])

    def done_copy(c):
        return pltpu.make_async_copy(out_stage.at[lax.rem(c, 2)], out_ref.at[pl.ds(c * CW, CW)], done_sem.at[lax.rem(c, 2)])

    def sect_copy(c):
        return pltpu.make_async_copy(xv.at[c % 2], sect_hbm.at[:, c], sect_sem.at[c % 2])

    weights = [
        pltpu.make_async_copy(wqkv_hbm, wqkv, w_sem.at[1]),
        pltpu.make_async_copy(wproj_hbm, wproj, w_sem.at[2]),
        pltpu.make_async_copy(wfc1_hbm, wfc1, w_sem.at[3]),
        pltpu.make_async_copy(wfc2_hbm, wfc2, w_sem.at[4]),
    ]

    for c in range(min(2, n_chunk)):
        x_copy(c).start()
    barrier = pltpu.get_barrier_semaphore()
    for k in range(1, n_head):
        pl.semaphore_signal(barrier, inc=1, device_id={"head": peer(k)}, device_id_type=MESH)
    if n_win is not None:
        for k in range(1, n_win):
            pl.semaphore_signal(barrier, inc=1, device_id={"win": win_peer(k)}, device_id_type=MESH)
    for q in range(QUADS):
        for s in range(n_head):
            pltpu.make_async_copy(
                wp_hbm.at[q, s], wp.at[pl.ds((s * QUADS + q) * share, share), :], w_sem.at[0]
            ).start()
    for w in weights:
        w.start()
    cot_copy(0).start()

    def eye(rows, cols):
        spot = lax.broadcasted_iota(jnp.int32, (rows, cols), 0) - lax.broadcasted_iota(jnp.int32, (rows, cols), 1)
        return (spot == 0).astype(F32).astype(BF16)

    eye_rows, eye_lanes = eye(RW, WT), eye(lanes, lanes)
    eye_tokens, eye_heads = eye(RW, LN), eye(LN, LN)

    def repack(c):
        x_copy(c).wait()
        for d in range(n_head):
            rows = [dot_nt(eye_rows, xv[c % 2, d, w]) for w in range(CW)]
            send_in[c, d] = jnp.concatenate(rows, axis=0).astype(BF16)

    def send(c):
        for k in range(1, n_head):
            in_copy(c, k).start()
        own_in(c).start()
        own_in(c).wait()

    repack(0)
    pl.semaphore_wait(barrier, n_head - 1 + (0 if n_win is None else n_win - 1))
    send(0)

    def send_rest(c, carry):
        @pl.when(c < n_chunk - 1)
        def _():
            x_copy(c + 1).start()

        repack(c)

        @pl.when(c < AHEAD)
        def _():
            send(c)

        return carry

    lax.fori_loop(1, n_chunk, send_rest, 0)

    def zero(ref):
        def body(r, carry):
            ref[pl.ds(pl.multiple_of(r * 8, 8), 8), :] = jnp.zeros((8, ref.shape[1]), F32)
            return carry
        lax.fori_loop(0, ref.shape[0] // 8, body, 0)

    for ref in (g_fc1, g_fc2, g_qkv, g_proj, g_red, sums):
        zero(ref)
    ds_acc[...] = jnp.zeros_like(ds_acc)

    def zero_heads(c, carry):
        qkv[c] = jnp.zeros(qkv.shape[1:], BF16)
        return carry

    lax.fori_loop(0, SLOTS, zero_heads, 0)
    d_heads[...] = jnp.zeros_like(d_heads)
    bias_t[:, WT:, :] = jnp.full((HEADS, JP - WT, LN), -1e30, F32)

    spot = lax.broadcasted_iota(jnp.int32, (2 * LN, LN), 0)
    token = lax.broadcasted_iota(jnp.int32, (2 * LN, LN), 1)
    token_row = (token * 205) >> 11
    pick = ((spot == token_row * SPAN + token - token_row * WIN) & (token < WT)).astype(F32).astype(BF16)
    for row in range(WIN):
        parts = []
        for col in range(WIN):
            off = offset_of(WT - 1) - offset_of(row * WIN + col)
            parts.append(table[:, off : off + 2 * LN])
        hi, mid, low = split3(jnp.concatenate(parts, axis=0))
        found = (dot(hi, pick) + dot(mid, pick) + dot(low, pick)) * LOG2E
        for col in range(WIN):
            bias_t[:, row * WIN + col, :] = found[col * HEADS : (col + 1) * HEADS]

    pltpu.make_async_copy(wp, wp, w_sem.at[0]).wait()
    for w in weights:
        w.wait()

    lane = lax.broadcasted_iota(jnp.int32, (1, LN), 1)
    masks = [((lane >= h * HD) & (lane < (h + 1) * HD)).astype(F32).astype(BF16) for h in range(PER)]

    def by_head(v):
        return jnp.concatenate([v * m for m in masks], axis=0)

    def merged_rows(c, r):
        return jnp.concatenate([rin[c, s, pl.ds(r, RB), :] for s in range(n_head)], axis=1).astype(F32)

    def padded(v):
        return jnp.concatenate([v, jnp.zeros((JP - RW, v.shape[1]), F32)], axis=0)

    def first_half(c):
        p = lax.rem(c, SLOTS)
        for k in range(1, n_head):
            in_copy_wait = pltpu.make_async_remote_copy(
                src_ref=send_in.at[c, me], dst_ref=rin.at[c, lax.rem(me + n_head - k, n_head)],
                send_sem=in_send.at[c, k], recv_sem=in_recv.at[c, k],
                device_id={"head": peer(k)}, device_id_type=MESH,
            )
            in_copy_wait.wait_recv()

        @pl.when(c + AHEAD < n_chunk)
        def _():
            send(c + AHEAD)

        for r in range(0, R, RB):
            xhat, unused = normalised(merged_rows(c, r))
            nrm[r : r + RB, :] = (xhat * n0g[...] + n0b[...]).astype(BF16)
        res[p] = dot(nrm[...], wp[...])
        for r in range(0, R, RB):
            xhat, unused = normalised(res[p, r : r + RB, :])
            fst[r : r + RB, :] = (xhat * n1g[...] + n1b[...]).astype(BF16)
        for t in range(3):
            part = dot(fst[...], wqkv[:, t * DM : (t + 1) * DM])
            if t == 0:
                part = part + qb[...]
            if t == 2:
                part = part + vb[...]
            for w in range(CW):
                for g in range(GROUPS):
                    piece = part[w * RW : (w + 1) * RW, g * LN : (g + 1) * LN]
                    qkv[p, w, t, g, 0:JP, :] = padded(piece).astype(BF16)

        def attend(w, carry):
            for g in range(GROUPS):
                wide[0, g * JP : (g + 1) * JP, :] = dot_nt(qkv[p, w, 1, g, 0:JP, :], by_head(qkv[p, w, 0, g]))
            for g in range(GROUPS):
                for h in range(PER):
                    lane_h = slice(h * LN, (h + 1) * LN)
                    s = wide[0, g * JP : (g + 1) * JP, lane_h] * (SCALE * LOG2E) + bias_t[g * PER + h]
                    e = jnp.exp2(s - jnp.max(s, axis=0, keepdims=True))
                    prob[p, w, g, :, lane_h] = (e * (1.0 / jnp.sum(e, axis=0, keepdims=True))).astype(BF16)
            for g in range(GROUPS):
                mixed = dot_tn(qkv[p, w, 2, g, 0:JP, :], prob[p, w, g])
                for h in range(PER):
                    owns[g, h * HD : (h + 1) * HD, :] = mixed[h * HD : (h + 1) * HD, h * LN : (h + 1) * LN]
            for g in range(GROUPS):
                stage[pl.ds(pl.multiple_of(w * RW, 8), RW), g * LN : (g + 1) * LN] = owns[g].T[0:RW]
            return carry

        lax.fori_loop(0, CW, attend, 0)
        att[p] = stage[:, 0:DM].astype(BF16)
        sec[...] = res[p] + dot(att[p], wproj[...]) + pb[...]
        for r in range(0, R, RB):
            xhat, unused = normalised(sec[r : r + RB, :])
            sn[r : r + RB, :] = (xhat * n2g[...] + n2b[...]).astype(BF16)
        cot_copy(c).wait()

        @pl.when(c + 1 < n_chunk)
        def _():
            cot_copy(c + 1).start()

        flags = [valid[c * CW + w].astype(F32) for w in range(CW)]
        tail = jnp.zeros((RW - WT, DM), F32)
        pieces = []
        for w in range(CW):
            pieces += [cot[lax.rem(c, 2), w].astype(F32) * flags[w], tail]
        up = jnp.concatenate(pieces, axis=0)
        dy[...] = up.astype(BF16)
        sums[:, O_FC2B : O_FC2B + DM] += fold(up)
        ffo[...] = sec[...] + fc2b[...]
        dsn[...] = jnp.zeros_like(dsn)

        def spread(t):
            b, half = t % 2, TILE // 2
            for n in range(2):
                cols = slice(t * TILE + n * half, t * TILE + (n + 1) * half)
                into = slice(n * half, (n + 1) * half)

                def one(cols=cols, into=into):
                    wide[b, 0:R, into] = dot(sn[...], wfc1[:, cols]) + fc1b[:, cols]

                def two(cols=cols, into=into):
                    wide[b, R : 2 * R, into] = dot_nt(dy[...], wfc2[cols, :])

                yield one
                yield two

        def bend(t):
            b = t % 2
            at = slice(O_FC1B + t * TILE, O_FC1B + (t + 1) * TILE)
            for r in range(0, R, RB):

                def one(r=r):
                    value, slope = gelu_parts(wide[b, r : r + RB, :])
                    slim[b, r : r + RB, :] = value.astype(BF16)
                    low = (wide[b, R + r : R + r + RB, :] * slope).astype(BF16)
                    slim[b, R + r : R + r + RB, :] = low
                    sums[:, at] += fold(low.astype(F32))

                yield one

        def gather(t):
            b, half = t % 2, TILE // 2
            cols = slice(t * TILE, (t + 1) * TILE)
            for n in range(2):
                into = slice(n * half, (n + 1) * half)

                def one(into=into):
                    ffo[:, into] += dot(slim[b, 0:R, :], wfc2[cols, into])

                def two(into=into):
                    dsn[:, into] += dot_nt(slim[b, R : 2 * R, :], wfc1[into, cols])

                yield one
                yield two
            for n in range(4):
                lanes_n = slice(n * LN, (n + 1) * LN)
                rows_n = slice(t * TILE + n * LN, t * TILE + (n + 1) * LN)

                def one(lanes_n=lanes_n, rows_n=rows_n):
                    g_fc2[rows_n, :] += dot_tn(slim[b, 0:R, lanes_n], dy[...])

                def two(lanes_n=lanes_n):
                    g_fc1[lanes_n, cols] += dot_tn(sn[:, lanes_n], slim[b, R : 2 * R, :])

                yield one
                yield two

        tiles = FF // TILE
        for piece in spread(0):
            piece()
        for t in range(tiles + 1):
            heavy = (list(gather(t - 1)) if t else []) + (list(spread(t + 1)) if t + 1 < tiles else [])
            light = list(bend(t)) if t < tiles else []
            weave(heavy, light)
        @pl.when(c >= 2)
        def _():
            done_copy(c - 2).wait()

        for w in range(CW):
            out_stage[lax.rem(c, 2), w] = (ffo[w * RW : w * RW + WT, :] * flags[w]).astype(BF16)
        done_copy(c).start()
        sum_g = jnp.zeros((8, DM), F32)
        sum_b = jnp.zeros((8, DM), F32)
        for r in range(0, R, RB):
            xhat, inv = normalised(sec[r : r + RB, :])
            d_out = dsn[r : r + RB, :]
            sum_g = sum_g + fold(d_out * xhat)
            sum_b = sum_b + fold(d_out)
            dsec[p, r : r + RB, :] = norm_back(d_out, n2g[...], xhat, inv) + dy[r : r + RB, :].astype(F32)
        sums[:, O_N2G : O_N2G + DM] += sum_g
        sums[:, O_N2B : O_N2B + DM] += sum_b

    def second_half(c):
        p = lax.rem(c, SLOTS)
        low = dsec[p].astype(BF16)
        sums[:, O_PB : O_PB + DM] += fold(low.astype(F32))
        dy[...] = low
        g_proj[...] += dot_tn(att[p], dy[...])
        back = dot_nt(dy[...], wproj[...])
        for w in range(CW):
            for g in range(GROUPS):
                piece = back[w * RW : (w + 1) * RW, g * LN : (g + 1) * LN]
                d_heads[w, g, 0:JP, :] = padded(piece).astype(BF16)

        def attend(w, carry):
            rows = pl.ds(pl.multiple_of(w * RW, 8), RW)
            for g in range(GROUPS):
                wide[0, g * JP : (g + 1) * JP, :] = dot_nt(qkv[p, w, 2, g, 0:JP, :], by_head(d_heads[w, g]))
            for g in range(GROUPS):
                stage[rows, 2 * DM + g * LN : 2 * DM + (g + 1) * LN] = dot(prob[p, w, g], by_head(d_heads[w, g]))[0:RW]
            for g in range(GROUPS):
                for h in range(PER):
                    lane_h = slice(h * LN, (h + 1) * LN)
                    pr = prob[p, w, g, :, lane_h].astype(F32)
                    pd = pr * wide[0, g * JP : (g + 1) * JP, lane_h]
                    d_s = pd - pr * jnp.sum(pd, axis=0, keepdims=True)
                    ds_acc[g * PER + h] += d_s
                    slim[0, g * JP : (g + 1) * JP, lane_h] = (d_s * SCALE).astype(BF16)
            for g in range(GROUPS):
                mixed = dot_tn(qkv[p, w, 1, g, 0:JP, :], slim[0, g * JP : (g + 1) * JP, :])
                for h in range(PER):
                    owns[g, h * HD : (h + 1) * HD, :] = mixed[h * HD : (h + 1) * HD, h * LN : (h + 1) * LN]
            for g in range(GROUPS):
                stage[rows, DM + g * LN : DM + (g + 1) * LN] = dot(slim[0, g * JP : (g + 1) * JP, :], by_head(qkv[p, w, 0, g]))[0:RW]
            for g in range(GROUPS):
                stage[rows, g * LN : (g + 1) * LN] = owns[g].T[0:RW]
            return carry

        lax.fori_loop(0, CW, attend, 0)
        sum_g = jnp.zeros((8, DM), F32)
        sum_b = jnp.zeros((8, DM), F32)
        sum_q = jnp.zeros((8, DM), F32)
        sum_v = jnp.zeros((8, DM), F32)
        for r in range(0, R, RB):
            low = stage[r : r + RB, :].astype(BF16)
            dpk[r : r + RB, :] = low
            sum_q = sum_q + fold(low[:, 0:DM].astype(F32))
            sum_v = sum_v + fold(low[:, 2 * DM :].astype(F32))
        sums[:, O_QB : O_QB + DM] += sum_q
        sums[:, O_VB : O_VB + DM] += sum_v
        dsn[...] = dot_nt(dpk[...], wqkv[...])
        for r in range(0, R, RB):
            xhat, inv = normalised(res[p, r : r + RB, :])
            fst[r : r + RB, :] = (xhat * n1g[...] + n1b[...]).astype(BF16)
            d_out = dsn[r : r + RB, :]
            sum_g = sum_g + fold(d_out * xhat)
            sum_b = sum_b + fold(d_out)
            d_res = norm_back(d_out, n1g[...], xhat, inv) + dsec[p, r : r + RB, :]
            sn[r : r + RB, :] = d_res.astype(BF16)
        sums[:, O_N1G : O_N1G + DM] += sum_g
        sums[:, O_N1B : O_N1B + DM] += sum_b
        wide[0, 0:R, :] = dot_nt(sn[...], wp[0:DM, :])
        wide[0, R : 2 * R, :] = dot_nt(sn[...], wp[DM:WIDTH, :])
        sum_g = jnp.zeros((8, WIDTH), F32)
        sum_b = jnp.zeros((8, WIDTH), F32)
        for r in range(0, R, RB):
            xhat, inv = normalised(merged_rows(c, r))
            nrm[r : r + RB, :] = (xhat * n0g[...] + n0b[...]).astype(BF16)
            d_out = jnp.concatenate([wide[0, r : r + RB, :], wide[0, R + r : R + r + RB, :]], axis=1)
            sum_g = sum_g + fold(d_out * xhat)
            sum_b = sum_b + fold(d_out)
            low = norm_back(d_out, n0g[...], xhat, inv).astype(BF16)
            for s in range(n_head):
                rin[c, s, r : r + RB, :] = low[:, s * lanes : (s + 1) * lanes]
        sums[:, O_N0G : O_N0G + WIDTH] += sum_g
        sums[:, O_N0B : O_N0B + WIDTH] += sum_b
        for k in range(1, n_head):
            out_copy(c, k).start()
        own_out(c).start()
        g_qkv[...] += dot_tn(fst[...], dpk[...])
        g_red[...] += dot_tn(nrm[...], sn[...])
        own_out(c).wait()

    def unpack(c):
        for k in range(1, n_head):
            pltpu.make_async_remote_copy(
                src_ref=rin.at[c, me], dst_ref=rout.at[c, lax.rem(me + n_head - k, n_head)],
                send_sem=out_send.at[c, k], recv_sem=out_recv.at[c, k],
                device_id={"head": peer(k)}, device_id_type=MESH,
            ).wait_recv()

        @pl.when(c >= 2)
        def _():
            sect_copy(c - 2).wait()

        for s in range(n_head):
            turned = dot_nt(eye_lanes, rout[c, s])
            for w in range(CW):
                xv[lax.rem(c, 2), s, w] = turned[:, w * RW : w * RW + WT].astype(BF16)
        sect_copy(c).start()

    def sent(c, carry):
        for k in range(1, n_head):
            in_copy(c, k).wait_send()
        return carry

    def step(s, carry):
        @pl.when(s < n_chunk)
        def _():
            first_half(s)

        if n_win is not None:
            @pl.when(s == n_chunk - 1)
            def _():
                for f in feeds:
                    f.start_pair()

            @pl.when(s == n_chunk)
            def _():
                for f in feeds:
                    f.start_plane()

        @pl.when(s == LAG)
        def _():
            lax.fori_loop(0, n_chunk, sent, 0)
            for k in range(1, n_head):
                pl.semaphore_signal(free_sem, inc=1, device_id={"head": peer(k)}, device_id_type=MESH)
            pl.semaphore_wait(free_sem, n_head - 1)

        @pl.when(s >= LAG)
        def _():
            second_half(s - LAG)

        if n_win is not None:
            @pl.when(s == n_chunk + LAG - 1)
            def _():
                for f in others:
                    f.start_pair()
                table_sums()
                small_in[at_pair, 0:HEADS, :] = vector_rows()
                small_pair().start()

        return carry

    def vector_rows():
        row = jnp.sum(sums[...], axis=0, keepdims=True)
        return jnp.concatenate([row[:, r * DM : (r + 1) * DM] for r in range(O_END // DM)], axis=0)

    def table_sums():
        total = jnp.zeros((HEADS, 4 * LN), F32)
        for row in range(WIN):
            spread = jnp.zeros((WIN * HEADS, 2 * LN), F32)
            whole = jnp.concatenate([ds_acc[:, row * WIN + col, :] for col in range(WIN)], axis=0)
            for part in split3(whole):
                spread = spread + dot_nt(part, pick)
            for col in range(WIN):
                off = offset_of(WT - 1) - offset_of(row * WIN + col)
                piece = jnp.concatenate(
                    [spread[col * HEADS : (col + 1) * HEADS], jnp.zeros((HEADS, 2 * LN), F32)], axis=1
                )
                total = total + pltpu.roll(piece, off, 1)
        if n_win is None:
            g_small[HEADS:, :] = total
        else:
            small_in[at_pair, HEADS:, :] = total

    lax.fori_loop(0, n_chunk + LAG, step, 0)

    def unpack_range(low, high):
        def body(c, carry):
            unpack(c)
            return carry

        lax.fori_loop(low, high, body, 0)

    if n_win is None:
        g_small[0:HEADS, :] = vector_rows()
        table_sums()
        unpack_range(0, n_chunk)
    else:
        for f in others:
            f.start_plane()
        small_pair().wait_recv()
        small_in[at_plane + my_win] = small_in[at_pair] + small_in[at_pair + 1]
        for k in range(1, n_win):
            small_plane(k).start()
        for f in feeds:
            f.start_near()
        unpack_range(0, n_chunk - 4)
        for f in feeds:
            f.start_far()
        unpack_range(n_chunk - 4, n_chunk - 3)
        for k in range(1, n_win):
            small_plane(k, lax.rem(my_win + n_win - k, n_win)).wait_recv()
        total = small_in[at_plane]
        for w in range(1, n_win):
            total = total + small_in[at_plane + w]
        small_in[at_near] = total
        small_near().start()
        for f in others:
            f.start_near()
        for f in feeds:
            f.finish()
        small_near().wait_recv()
        small_in[at_far] = small_in[at_near] + small_in[at_near + 1]
        small_far().start()
        for f in others:
            f.start_far()
        unpack_range(n_chunk - 3, n_chunk - 1)
        for f in reversed(others):
            f.finish()
        small_far().wait_recv()
        g_small[...] = small_in[at_far] + small_in[at_far + 1]
        unpack_range(n_chunk - 1, n_chunk)
        others[-1].finish_gather()
        for f in feeds + others:
            f.drain()
        small_pair().wait_send()
        for k in range(1, n_win):
            small_plane(k).wait_send()
        small_near().wait_send()
        small_far().wait_send()
    for c in range(max(0, n_chunk - 2), n_chunk):
        sect_copy(c).wait()
        done_copy(c).wait()

    def drain(c, carry):
        for k in range(1, n_head):
            out_copy(c, k).wait_send()
        return carry

    lax.fori_loop(0, n_chunk, drain, 0)


def run_kernel(n_head, n_win, n_chunk, share, args):
    lanes = QUADS * share
    any_, vmem = pl.BlockSpec(memory_space=pl.ANY), pl.BlockSpec(memory_space=pltpu.VMEM)
    smem = pl.BlockSpec(memory_space=pltpu.SMEM)
    windows = n_chunk * CW
    in_specs = [
        any_, any_, vmem, vmem, vmem, vmem, any_, vmem, vmem, vmem, any_, vmem, vmem, vmem,
        any_, vmem, any_, vmem, smem, any_,
    ]
    out_shape = [
        jax.ShapeDtypeStruct((windows, WT, DM), BF16),
        jax.ShapeDtypeStruct((n_head, n_chunk, CW, lanes, WT), BF16),
    ]
    dma = pltpu.SemaphoreType.DMA
    scratch = []
    if n_win is None:
        out_shape += [jax.ShapeDtypeStruct(m, F32) for m in MATRICES]
    else:
        devices, n_z = n_win * n_head, n_head // 2
        scratch += [pltpu.VMEM(m, F32) for m in MATRICES]
        shares = [(m // devices, cols) for m, cols in MATRICES]
        out_shape += [jax.ShapeDtypeStruct(m, F32) for m in shares[:-1]]
        out_shape += [jax.ShapeDtypeStruct((shares[-1][0] * n_win, DM), F32)]
        scratch += [pltpu.VMEM((rows * n_win * n_z, cols), BF16) for rows, cols in shares]
        scratch += [pltpu.VMEM((n_win - 1, rows * n_z, cols), BF16) for rows, cols in shares]
        scratch += [pltpu.VMEM((rows * (n_z // 2), cols), BF16) for rows, cols in shares]
        scratch += [pltpu.VMEM((rows, cols), BF16) for rows, cols in shares]
        scratch += [
            pltpu.VMEM((n_win, shares[-1][0], DM), BF16),
            pltpu.VMEM((n_win + 6, 2 * HEADS, DM), F32),
            dma((6, 2 * n_win + 2)), dma((6, 2 * n_win + 2)),
        ]
    out_shape += [jax.ShapeDtypeStruct((2 * HEADS, DM), F32)]
    out_specs = [any_, any_] + [vmem] * 6
    scratch += [
        pltpu.VMEM((2, n_head, CW, lanes, WT), BF16),
        pltpu.VMEM((n_chunk, n_head, R, lanes), BF16),
        pltpu.VMEM((n_chunk, n_head, R, lanes), BF16),
        pltpu.VMEM((WIDTH, DM), BF16),
        pltpu.VMEM((DM, 3 * DM), BF16),
        pltpu.VMEM((DM, DM), BF16),
        pltpu.VMEM((DM, FF), BF16),
        pltpu.VMEM((FF, DM), BF16),
        pltpu.VMEM((2, CW, WT, DM), BF16),
        pltpu.VMEM((R, WIDTH), BF16),
        pltpu.VMEM((SLOTS, R, DM), F32),
        pltpu.VMEM((R, DM), BF16),
        pltpu.VMEM((SLOTS, CW, 3, GROUPS, LN, LN), BF16),
        pltpu.VMEM((SLOTS, CW, GROUPS, JP, PER * LN), BF16),
        pltpu.VMEM((SLOTS, R, DM), BF16),
        pltpu.VMEM((R, 3 * DM), F32),
        pltpu.VMEM((R, DM), F32),
        pltpu.VMEM((R, DM), BF16),
        pltpu.VMEM((R, DM), BF16),
        pltpu.VMEM((2, GROUPS * JP, TILE), F32),
        pltpu.VMEM((2, GROUPS * JP, TILE), BF16),
        pltpu.VMEM((R, DM), F32),
        pltpu.VMEM((R, DM), F32),
        pltpu.VMEM((SLOTS, R, DM), F32),
        pltpu.VMEM((R, 3 * DM), BF16),
        pltpu.VMEM((CW, GROUPS, LN, LN), BF16),
        pltpu.VMEM((GROUPS, LN, LN), F32),
        pltpu.VMEM((2, CW, WT, DM), BF16),
        pltpu.VMEM((8, O_END), F32),
        pltpu.VMEM((HEADS, JP, LN), F32),
        pltpu.VMEM((HEADS, JP, LN), F32),
        dma((n_chunk, n_head)), dma((n_chunk, n_head)), dma((n_chunk, n_head)), dma((n_chunk, n_head)),
        dma((2,)), dma((5,)), dma((2,)), dma, dma((2,)), pltpu.SemaphoreType.REGULAR, dma((2,)),
    ]
    return pl.pallas_call(
        functools.partial(kernel, n_head, n_win, n_chunk, share),
        out_shape=out_shape, in_specs=in_specs, out_specs=out_specs, scratch_shapes=scratch,
        compiler_params=pltpu.CompilerParams(
            collective_id=0, has_side_effects=True, vmem_limit_bytes=63 * 1024 * 1024
        ),
        cost_estimate=pl.CostEstimate(flops=27 * 10**9, bytes_accessed=30 * 10**6, transcendentals=10**7),
    )(*args)


def local(
    n_head, section_rows, reduce_weight, norm0_gain, norm0_bias, norm1_gain, norm1_bias, qkv_weight, q_bias, v_bias,
    rel_table, proj_weight, proj_bias, norm2_gain, norm2_bias, fc1_weight, fc1_bias, fc2_weight, fc2_bias,
    window_valid, cotangent,
):
    group_windows, tokens, quads, share = section_rows.shape
    windows = cotangent.shape[0]
    n_chunk = windows // CW
    lanes = quads * share
    rows = section_rows.transpose(0, 2, 3, 1).reshape(n_head, n_chunk, CW, lanes, tokens)

    def by_source(v):
        return v.reshape(quads, n_head, share).transpose(1, 0, 2).reshape(1, WIDTH)

    def row(v):
        return v.reshape(1, -1)

    args = (
        rows, reduce_weight.reshape(quads, n_head, share, DM), by_source(norm0_gain), by_source(norm0_bias),
        row(norm1_gain), row(norm1_bias), qkv_weight, row(q_bias), row(v_bias),
        jnp.pad(rel_table, ((0, 0), (0, 4 * LN - RELS))), proj_weight, row(proj_bias), row(norm2_gain), row(norm2_bias),
        fc1_weight, row(fc1_bias), fc2_weight, row(fc2_bias), window_valid, cotangent,
    )
    n_win = lax.axis_size("win")
    devices = n_win * n_head
    inside = n_head == 8 and all((m // devices) % 16 == 0 for m, unused in MATRICES)
    block_out, section, fc1, fc2, qkv, proj, red, small = run_kernel(
        n_head, n_win if inside else None, n_chunk, share, args
    )
    section_grad = section.reshape(group_windows, quads, share, tokens).transpose(0, 3, 1, 2)
    both = ("win", "head")

    def scattered(v):
        return lax.psum_scatter(v.astype(BF16), both, scatter_dimension=0, tiled=True).astype(F32)

    if not inside:
        fc1, fc2, qkv, proj = scattered(fc1), scattered(fc2), scattered(qkv), scattered(proj)
        red = lax.psum_scatter(red.astype(BF16), "head", scatter_dimension=0, tiled=True)
        red = lax.psum(red, "win").astype(F32)
        small = lax.psum(small, both)
    reduce_grad = red.reshape(quads, share, DM)
    vectors, table_grad = small[:HEADS].reshape(-1), small[HEADS:, :RELS]
    at = lax.axis_index("win") * n_head + lax.axis_index("head")

    def part(start, length):
        size = length // devices
        return lax.dynamic_slice_in_dim(vectors, start + at * size, size)

    def part0(start):
        return lax.dynamic_slice_in_dim(vectors, start + lax.axis_index("head") * lanes, lanes).reshape(quads, share)

    return (
        block_out, section_grad, reduce_grad, part0(O_N0G), part0(O_N0B), part(O_N1G, DM), part(O_N1B, DM),
        qkv, part(O_QB, DM), part(O_VB, DM), table_grad, proj, part(O_PB, DM),
        part(O_N2G, DM), part(O_N2B, DM), fc1, part(O_FC1B, FF), fc2, part(O_FC2B, DM),
    )


def solution(mesh):
    in_specs = (
        P("win", None, None, "head"),
        P(),
        P(),
        P(),
        P(),
        P(),
        P(),
        P(),
        P(),
        P(),
        P(),
        P(),
        P(),
        P(),
        P(),
        P(),
        P(),
        P(),
        P(("win", "head")),
        P(("win", "head"), None, None),
    )
    out_specs = (
        P(("win", "head"), None, None),
        P("win", None, None, "head"),
        P(None, "head", None),
        P(None, "head"),
        P(None, "head"),
        P(("win", "head")),
        P(("win", "head")),
        P(("win", "head"), None),
        P(("win", "head")),
        P(("win", "head")),
        P(),
        P(("win", "head"), None),
        P(("win", "head")),
        P(("win", "head")),
        P(("win", "head")),
        P(("win", "head"), None),
        P(("win", "head")),
        P(("win", "head"), None),
        P(("win", "head")),
    )
    return jax.shard_map(
        functools.partial(local, mesh.shape["head"]), mesh=mesh, in_specs=in_specs, out_specs=out_specs, check_vma=False)
```

```python
import functools

import jax
import jax.numpy as jnp
from jax import lax
from jax.experimental import pallas as pl
from jax.experimental.pallas import tpu as pltpu
from jax.sharding import PartitionSpec as P

C2 = 256
DM = 512
HEADS = 16
HD = 32
FF = 2048
WIN = 10
WT = 100
RELS = 361
SPAN = 2 * WIN - 1

QUADS = 4
WIDTH = QUADS * C2
CW = 2
RW = 104
R = CW * RW
JP = 112
LN = 128
GROUPS = 4
PER = 4
LAG = 4
SLOTS = LAG + 1
AHEAD = 2
RB = 16
TILE = 512
EPS = 1e-05
LOG2E = 1.4426950408889634
SCALE = HD ** (-0.5)

MESH = pl.DeviceIdType.MESH
F32 = jnp.float32
BF16 = jnp.bfloat16

O_QB, O_VB, O_PB, O_FC1B, O_FC2B = 0, 512, 1024, 1536, 3584
O_N1G, O_N1B, O_N2G, O_N2B, O_N0G, O_N0B, O_END = 4096, 4608, 5120, 5632, 6144, 7168, 8192


MATRICES = ((DM, FF), (FF, DM), (DM, 3 * DM), (DM, DM), (WIDTH, DM))


def dot(a, b):
    return lax.dot_general(a, b, (((1,), (0,)), ((), ())), preferred_element_type=F32)


def dot_nt(a, b):
    return lax.dot_general(a, b, (((1,), (1,)), ((), ())), preferred_element_type=F32)


def dot_tn(a, b):
    return lax.dot_general(a, b, (((0,), (0,)), ((), ())), preferred_element_type=F32)


def normalised(v):
    centred = v - jnp.mean(v, axis=-1, keepdims=True)
    inv = lax.rsqrt(jnp.mean(centred * centred, axis=-1, keepdims=True) + EPS)
    return centred * inv, inv


def norm_back(d_out, gain, xhat, inv):
    u = d_out * gain
    mean_u = jnp.mean(u, axis=-1, keepdims=True)
    mean_ux = jnp.mean(u * xhat, axis=-1, keepdims=True)
    return (u - mean_u - xhat * mean_ux) * inv


def fold(v):
    total = v[0:8]
    for r in range(8, v.shape[0], 8):
        total = total + v[r : r + 8]
    return total


def weave(one, two):
    marks = [((i + 0.5) / len(one), piece) for i, piece in enumerate(one)]
    marks += [((i + 0.5) / len(two), piece) for i, piece in enumerate(two)]
    for unused, piece in sorted(marks, key=lambda m: m[0]):
        piece()


def gelu_parts(x):
    z = jnp.abs(x) * 0.7071067811865476
    t = 1.0 / (1.0 + 0.3275911 * z)
    e = jnp.exp2(x * x * (-0.5 * LOG2E))
    poly = ((((1.061405429 * t - 1.453152027) * t + 1.421413741) * t - 0.284496736) * t + 0.254829592) * t
    half = 0.5 * poly * e
    cdf = jnp.where(x < 0, half, 1.0 - half)
    return x * cdf, cdf + x * e * 0.3989422804014327


def split3(v):
    hi = v.astype(BF16)
    rest = v - hi.astype(F32)
    mid = rest.astype(BF16)
    low = (rest - mid.astype(F32)).astype(BF16)
    return hi, mid, low


def offset_of(j):
    return (j // WIN) * SPAN + j % WIN


def kernel(
    n_head, n_win, n_chunk, share,
    x_hbm, wp_hbm, gain0, bias0, n1g, n1b, wqkv_hbm, qb, vb, table_in, wproj_hbm, pb, n2g, n2b,
    wfc1_hbm, fc1b, wfc2_hbm, fc2b, valid, cot_hbm,
    *refs,
):
    if n_win is None:
        (out_ref, sect_hbm, g_fc1, g_fc2, g_qkv, g_proj, g_red, g_small), refs = refs[:8], refs[8:]
    else:
        (out_ref, sect_hbm, o_fc1, o_fc2, o_qkv, o_proj, o_red, g_small), refs = refs[:8], refs[8:]
        (g_fc1, g_fc2, g_qkv, g_proj, g_red), refs = refs[:5], refs[5:]
        first_in, refs = refs[:5], refs[5:]
        plane_in, refs = refs[:5], refs[5:]
        near_in, refs = refs[:5], refs[5:]
        far_in, refs = refs[:5], refs[5:]
        (gather_in, small_in, sum_send, sum_recv), refs = refs[:4], refs[4:]
    (xv, send_in, rin, wp, wqkv, wproj, wfc1, wfc2, cot,
    nrm, res, fst, qkv, prob, att, stage, sec, sn, dy, wide, slim, ffo, dsn, dsec, dpk, d_heads, n0g, n0b, table, owns, out_stage, sums, bias_t, ds_acc,
    in_send, in_recv, out_send, out_recv, x_sem, w_sem, cot_sem, own_sem, sect_sem, free_sem, done_sem) = refs
    rout = send_in
    me = lax.axis_index("head")
    lanes = QUADS * share

    def peer(k):
        return lax.rem(me + k, n_head)

    if n_win is not None:
        my_win = lax.axis_index("win")
        core, my_z = lax.rem(me, 2), me // 2
        n_z = n_head // 2
        sibling = me + 1 - 2 * core
        near_z = my_z + 1 - 2 * lax.rem(my_z, 2)
        far_z = my_z + 2 - 4 * (my_z // 2)

        def win_peer(k):
            return lax.rem(my_win + k, n_win)

        class Scatter:
            def __init__(self, spot, total, hold, out, by_head=False):
                self.spot, self.total, self.hold, self.out = spot, total, hold, out
                self.rows = total.shape[0] // (n_win * n_head)
                self.cols = total.shape[1]
                self.by_head = by_head
                half = total.shape[0] // 2
                self.at_plane = half
                self.at_near = half + (n_win - 1) * n_z * self.rows
                self.at_far = self.at_near + (n_z // 2) * self.rows

            def block(self, w, z, c):
                head = z * 2 + c
                spot = head * n_win + w if self.by_head else w * n_head + head
                return pl.ds(pl.multiple_of(spot * self.rows, 16), self.rows)

            def span(self, start, count=1):
                return pl.ds(pl.multiple_of(start, 16), count * self.rows)

            def copy(self, j, source, target, to):
                return pltpu.make_async_remote_copy(
                    src_ref=source, dst_ref=target, send_sem=sum_send.at[self.spot, j], recv_sem=sum_recv.at[self.spot, j],
                    device_id=to, device_id_type=MESH,
                )

            def pair_copy(self):
                return self.copy(
                    0, self.hold.at[pl.ds(0, self.at_plane), :], first_in[self.spot], {"head": sibling}
                )

            def plane_copy(self, k):
                source = self.hold.at[self.span(self.at_plane + (k - 1) * n_z * self.rows, n_z), :]
                return self.copy(k, source, plane_in[self.spot].at[k - 1], {"win": win_peer(k)})

            def near_copy(self):
                source = self.hold.at[self.span(self.at_near, n_z // 2), :]
                return self.copy(n_win, source, near_in[self.spot], {"head": near_z * 2 + core})

            def far_copy(self):
                source = self.hold.at[self.span(self.at_far), :]
                return self.copy(n_win + 1, source, far_in[self.spot], {"head": far_z * 2 + core})

            def start_pair(self):
                def body(i, carry):
                    w, z = i // n_z, lax.rem(i, n_z)
                    self.hold[self.span(i * self.rows), :] = self.total[self.block(w, z, 1 - core), :].astype(BF16)
                    return carry

                lax.fori_loop(0, n_win * n_z, body, 0)
                self.pair_copy().start()

            def start_plane(self):
                self.pair_copy().wait_recv()
                for k in range(1, n_win + 1):
                    w = lax.rem(my_win + k, n_win)

                    def body(z, carry):
                        mine = self.block(w, z, core)
                        value = self.total[mine, :] + first_in[self.spot][
                            self.span((w * n_z + z) * self.rows), :
                        ].astype(F32)
                        if k == n_win:
                            self.total[mine, :] = value
                        else:
                            at = self.at_plane + ((k - 1) * n_z + z) * self.rows
                            self.hold[self.span(at), :] = value.astype(BF16)
                        return carry

                    lax.fori_loop(0, n_z, body, 0)
                    if k < n_win:
                        self.plane_copy(k).start()

            def start_near(self):
                for k in range(1, n_win):
                    self.plane_copy(k).wait_recv()

                def both(z):
                    value = self.total[self.block(my_win, z, core), :]
                    for k in range(1, n_win):
                        value = value + plane_in[self.spot][k - 1, self.span(z * self.rows), :].astype(F32)
                    return value

                for j in range(n_z // 2):
                    sent = both(j * 2 + lax.rem(near_z, 2))
                    self.hold[self.span(self.at_near + j * self.rows), :] = sent.astype(BF16)
                self.near_copy().start()
                for j in range(n_z // 2):
                    z = j * 2 + lax.rem(my_z, 2)
                    self.total[self.block(my_win, z, core), :] = both(z)

            def after_near(self, j):
                kept = self.total[self.block(my_win, j * 2 + lax.rem(my_z, 2), core), :]
                return kept + near_in[self.spot][self.span(j * self.rows), :].astype(F32)

            def start_far(self):
                self.near_copy().wait_recv()
                self.hold[self.span(self.at_far), :] = self.after_near(far_z // 2).astype(BF16)
                self.far_copy().start()

            def finish(self):
                self.far_copy().wait_recv()
                value = self.after_near(my_z // 2) + far_in[self.spot][...].astype(F32)
                if not self.by_head:
                    self.out[...] = value
                    return
                gather_in[my_win] = value.astype(BF16)
                for k in range(1, n_win):
                    self.gather_copy(k).start()

            def gather_copy(self, k):
                return self.copy(
                    n_win + 1 + k, gather_in.at[my_win], gather_in.at[my_win], {"win": win_peer(k)}
                )

            def finish_gather(self):
                for k in range(1, n_win):
                    source = lax.rem(my_win + n_win - k, n_win)
                    self.copy(
                        n_win + 1 + k, gather_in.at[my_win], gather_in.at[source], {"win": win_peer(k)}
                    ).wait_recv()
                for w in range(n_win):
                    self.out[w * self.rows : (w + 1) * self.rows, :] = gather_in[w].astype(F32)

            def drain(self):
                self.pair_copy().wait_send()
                for k in range(1, n_win):
                    self.plane_copy(k).wait_send()
                    if self.by_head:
                        self.gather_copy(k).wait_send()
                self.near_copy().wait_send()
                self.far_copy().wait_send()

        feeds = [Scatter(0, g_fc1, wfc1, o_fc1), Scatter(1, g_fc2, wfc2, o_fc2)]
        others = [Scatter(2, g_qkv, wqkv, o_qkv), Scatter(3, g_proj, wproj, o_proj), Scatter(4, g_red, wp, o_red, True)]

        def small_copy(j, source, target, to):
            return pltpu.make_async_remote_copy(
                src_ref=small_in.at[source], dst_ref=small_in.at[target], send_sem=sum_send.at[5, j],
                recv_sem=sum_recv.at[5, j], device_id=to, device_id_type=MESH,
            )

        at_pair, at_plane, at_near, at_far = 0, 2, 2 + n_win, 4 + n_win

        def small_pair():
            return small_copy(0, at_pair, at_pair + 1, {"head": sibling})

        def small_plane(k, target=None):
            return small_copy(k, at_plane + my_win, at_plane + (my_win if target is None else target), {"win": win_peer(k)})

        def small_near():
            return small_copy(n_win, at_near, at_near + 1, {"head": near_z * 2 + core})

        def small_far():
            return small_copy(n_win + 1, at_far, at_far + 1, {"head": far_z * 2 + core})

    def in_copy(c, k):
        to = peer(k)
        return pltpu.make_async_remote_copy(
            src_ref=send_in.at[c, to], dst_ref=rin.at[c, me], send_sem=in_send.at[c, k], recv_sem=in_recv.at[c, k],
            device_id={"head": to}, device_id_type=MESH,
        )

    def out_copy(c, k):
        to = peer(k)
        return pltpu.make_async_remote_copy(
            src_ref=rin.at[c, to], dst_ref=rout.at[c, me], send_sem=out_send.at[c, k], recv_sem=out_recv.at[c, k],
            device_id={"head": to}, device_id_type=MESH,
        )

    def own_in(c):
        return pltpu.make_async_copy(send_in.at[c, me], rin.at[c, me], own_sem)

    def own_out(c):
        return pltpu.make_async_copy(rin.at[c, me], rout.at[c, me], own_sem)

    def x_copy(c):
        return pltpu.make_async_copy(x_hbm.at[:, c], xv.at[c % 2], x_sem.at[c % 2])

    def cot_copy(c):
        return pltpu.make_async_copy(cot_hbm.at[pl.ds(c * CW, CW)], cot.at[lax.rem(c, 2)], cot_sem.at[lax.rem(c, 2)])

    def done_copy(c):
        return pltpu.make_async_copy(out_stage.at[lax.rem(c, 2)], out_ref.at[pl.ds(c * CW, CW)], done_sem.at[lax.rem(c, 2)])

    def sect_copy(c):
        return pltpu.make_async_copy(xv.at[c % 2], sect_hbm.at[:, c], sect_sem.at[c % 2])

    weights = [
        pltpu.make_async_copy(wqkv_hbm, wqkv, w_sem.at[1]),
        pltpu.make_async_copy(wproj_hbm, wproj, w_sem.at[2]),
        pltpu.make_async_copy(wfc1_hbm, wfc1, w_sem.at[3]),
        pltpu.make_async_copy(wfc2_hbm, wfc2, w_sem.at[4]),
    ]

    for c in range(min(2, n_chunk)):
        x_copy(c).start()
    barrier = pltpu.get_barrier_semaphore()
    for k in range(1, n_head):
        pl.semaphore_signal(barrier, inc=1, device_id={"head": peer(k)}, device_id_type=MESH)
    if n_win is not None:
        for k in range(1, n_win):
            pl.semaphore_signal(barrier, inc=1, device_id={"win": win_peer(k)}, device_id_type=MESH)
    for q in range(QUADS):
        for s in range(n_head):
            pltpu.make_async_copy(
                wp_hbm.at[q, s], wp.at[pl.ds((s * QUADS + q) * share, share), :], w_sem.at[0]
            ).start()
    for w in weights:
        w.start()
    cot_copy(0).start()

    def eye(rows, cols):
        spot = lax.broadcasted_iota(jnp.int32, (rows, cols), 0) - lax.broadcasted_iota(jnp.int32, (rows, cols), 1)
        return (spot == 0).astype(F32).astype(BF16)

    eye_rows, eye_lanes = eye(RW, WT), eye(lanes, lanes)
    eye_tokens, eye_heads = eye(RW, LN), eye(LN, LN)

    def repack(c):
        x_copy(c).wait()
        for d in range(n_head):
            rows = [dot_nt(eye_rows, xv[c % 2, d, w]) for w in range(CW)]
            send_in[c, d] = jnp.concatenate(rows, axis=0).astype(BF16)

    def send(c):
        for k in range(1, n_head):
            in_copy(c, k).start()
        own_in(c).start()
        own_in(c).wait()

    repack(0)
    pl.semaphore_wait(barrier, n_head - 1 + (0 if n_win is None else n_win - 1))
    send(0)

    def send_rest(c, carry):
        @pl.when(c < n_chunk - 1)
        def _():
            x_copy(c + 1).start()

        repack(c)

        @pl.when(c < AHEAD)
        def _():
            send(c)

        return carry

    lax.fori_loop(1, n_chunk, send_rest, 0)

    def zero(ref):
        def body(r, carry):
            ref[pl.ds(pl.multiple_of(r * 8, 8), 8), :] = jnp.zeros((8, ref.shape[1]), F32)
            return carry
        lax.fori_loop(0, ref.shape[0] // 8, body, 0)

    for ref in (g_fc1, g_fc2, g_qkv, g_proj, g_red, sums):
        zero(ref)
    ds_acc[...] = jnp.zeros_like(ds_acc)

    def zero_heads(c, carry):
        qkv[c] = jnp.zeros(qkv.shape[1:], BF16)
        return carry

    lax.fori_loop(0, SLOTS, zero_heads, 0)
    d_heads[...] = jnp.zeros_like(d_heads)
    bias_t[:, WT:, :] = jnp.full((HEADS, JP - WT, LN), -1e30, F32)

    for row, given in ((n0g, gain0), (n0b, bias0)):
        for s in range(n_head):
            row[:, s * lanes : (s + 1) * lanes] = jnp.concatenate(
                [given[q : q + 1, s * share : (s + 1) * share] for q in range(QUADS)], axis=1
            )
    table[...] = jnp.zeros_like(table)
    table[:, 0:RELS] = table_in[...]
    spot = lax.broadcasted_iota(jnp.int32, (2 * LN, LN), 0)
    token = lax.broadcasted_iota(jnp.int32, (2 * LN, LN), 1)
    token_row = (token * 205) >> 11
    pick = ((spot == token_row * SPAN + token - token_row * WIN) & (token < WT)).astype(F32).astype(BF16)
    for row in range(WIN):
        parts = []
        for col in range(WIN):
            off = offset_of(WT - 1) - offset_of(row * WIN + col)
            parts.append(table[:, off : off + 2 * LN])
        hi, mid, low = split3(jnp.concatenate(parts, axis=0))
        found = (dot(hi, pick) + dot(mid, pick) + dot(low, pick)) * LOG2E
        for col in range(WIN):
            bias_t[:, row * WIN + col, :] = found[col * HEADS : (col + 1) * HEADS]

    pltpu.make_async_copy(wp, wp, w_sem.at[0]).wait()
    for w in weights:
        w.wait()

    lane = lax.broadcasted_iota(jnp.int32, (1, LN), 1)
    masks = [((lane >= h * HD) & (lane < (h + 1) * HD)).astype(F32).astype(BF16) for h in range(PER)]

    def by_head(v):
        return jnp.concatenate([v * m for m in masks], axis=0)

    def merged_rows(c, r):
        return jnp.concatenate([rin[c, s, pl.ds(r, RB), :] for s in range(n_head)], axis=1).astype(F32)

    def padded(v):
        return jnp.concatenate([v, jnp.zeros((JP - RW, v.shape[1]), F32)], axis=0)

    def first_half(c):
        p = lax.rem(c, SLOTS)
        for k in range(1, n_head):
            in_copy_wait = pltpu.make_async_remote_copy(
                src_ref=send_in.at[c, me], dst_ref=rin.at[c, lax.rem(me + n_head - k, n_head)],
                send_sem=in_send.at[c, k], recv_sem=in_recv.at[c, k],
                device_id={"head": peer(k)}, device_id_type=MESH,
            )
            in_copy_wait.wait_recv()

        @pl.when(c + AHEAD < n_chunk)
        def _():
            send(c + AHEAD)

        for r in range(0, R, RB):
            xhat, unused = normalised(merged_rows(c, r))
            nrm[r : r + RB, :] = (xhat * n0g[...] + n0b[...]).astype(BF16)
        res[p] = dot(nrm[...], wp[...])
        for r in range(0, R, RB):
            xhat, unused = normalised(res[p, r : r + RB, :])
            fst[r : r + RB, :] = (xhat * n1g[...] + n1b[...]).astype(BF16)
        for t in range(3):
            part = dot(fst[...], wqkv[:, t * DM : (t + 1) * DM])
            if t == 0:
                part = part + qb[...]
            if t == 2:
                part = part + vb[...]
            for w in range(CW):
                for g in range(GROUPS):
                    piece = part[w * RW : (w + 1) * RW, g * LN : (g + 1) * LN]
                    qkv[p, w, t, g, 0:JP, :] = padded(piece).astype(BF16)

        def attend(w, carry):
            for g in range(GROUPS):
                wide[0, g * JP : (g + 1) * JP, :] = dot_nt(qkv[p, w, 1, g, 0:JP, :], by_head(qkv[p, w, 0, g]))
            for g in range(GROUPS):
                for h in range(PER):
                    lane_h = slice(h * LN, (h + 1) * LN)
                    s = wide[0, g * JP : (g + 1) * JP, lane_h] * (SCALE * LOG2E) + bias_t[g * PER + h]
                    e = jnp.exp2(s - jnp.max(s, axis=0, keepdims=True))
                    prob[p, w, g, :, lane_h] = (e * (1.0 / jnp.sum(e, axis=0, keepdims=True))).astype(BF16)
            for g in range(GROUPS):
                mixed = dot_tn(qkv[p, w, 2, g, 0:JP, :], prob[p, w, g])
                for h in range(PER):
                    owns[g, h * HD : (h + 1) * HD, :] = mixed[h * HD : (h + 1) * HD, h * LN : (h + 1) * LN]
            for g in range(GROUPS):
                stage[pl.ds(pl.multiple_of(w * RW, 8), RW), g * LN : (g + 1) * LN] = owns[g].T[0:RW]
            return carry

        lax.fori_loop(0, CW, attend, 0)
        att[p] = stage[:, 0:DM].astype(BF16)
        sec[...] = res[p] + dot(att[p], wproj[...]) + pb[...]
        for r in range(0, R, RB):
            xhat, unused = normalised(sec[r : r + RB, :])
            sn[r : r + RB, :] = (xhat * n2g[...] + n2b[...]).astype(BF16)
        cot_copy(c).wait()

        @pl.when(c + 1 < n_chunk)
        def _():
            cot_copy(c + 1).start()

        flags = [valid[c * CW + w].astype(F32) for w in range(CW)]
        tail = jnp.zeros((RW - WT, DM), F32)
        pieces = []
        for w in range(CW):
            pieces += [cot[lax.rem(c, 2), w].astype(F32) * flags[w], tail]
        up = jnp.concatenate(pieces, axis=0)
        dy[...] = up.astype(BF16)
        sums[:, O_FC2B : O_FC2B + DM] += fold(up)
        ffo[...] = sec[...] + fc2b[...]
        dsn[...] = jnp.zeros_like(dsn)

        def spread(t):
            b, half = t % 2, TILE // 2
            for n in range(2):
                cols = slice(t * TILE + n * half, t * TILE + (n + 1) * half)
                into = slice(n * half, (n + 1) * half)

                def one(cols=cols, into=into):
                    wide[b, 0:R, into] = dot(sn[...], wfc1[:, cols]) + fc1b[:, cols]

                def two(cols=cols, into=into):
                    wide[b, R : 2 * R, into] = dot_nt(dy[...], wfc2[cols, :])

                yield one
                yield two

        def bend(t):
            b = t % 2
            at = slice(O_FC1B + t * TILE, O_FC1B + (t + 1) * TILE)
            for r in range(0, R, RB):

                def one(r=r):
                    value, slope = gelu_parts(wide[b, r : r + RB, :])
                    slim[b, r : r + RB, :] = value.astype(BF16)
                    low = (wide[b, R + r : R + r + RB, :] * slope).astype(BF16)
                    slim[b, R + r : R + r + RB, :] = low
                    sums[:, at] += fold(low.astype(F32))

                yield one

        def gather(t):
            b, half = t % 2, TILE // 2
            cols = slice(t * TILE, (t + 1) * TILE)
            for n in range(2):
                into = slice(n * half, (n + 1) * half)

                def one(into=into):
                    ffo[:, into] += dot(slim[b, 0:R, :], wfc2[cols, into])

                def two(into=into):
                    dsn[:, into] += dot_nt(slim[b, R : 2 * R, :], wfc1[into, cols])

                yield one
                yield two
            for n in range(4):
                lanes_n = slice(n * LN, (n + 1) * LN)
                rows_n = slice(t * TILE + n * LN, t * TILE + (n + 1) * LN)

                def one(lanes_n=lanes_n, rows_n=rows_n):
                    g_fc2[rows_n, :] += dot_tn(slim[b, 0:R, lanes_n], dy[...])

                def two(lanes_n=lanes_n):
                    g_fc1[lanes_n, cols] += dot_tn(sn[:, lanes_n], slim[b, R : 2 * R, :])

                yield one
                yield two

        tiles = FF // TILE
        for piece in spread(0):
            piece()
        for t in range(tiles + 1):
            heavy = (list(gather(t - 1)) if t else []) + (list(spread(t + 1)) if t + 1 < tiles else [])
            light = list(bend(t)) if t < tiles else []
            weave(heavy, light)
        @pl.when(c >= 2)
        def _():
            done_copy(c - 2).wait()

        for w in range(CW):
            out_stage[lax.rem(c, 2), w] = (ffo[w * RW : w * RW + WT, :] * flags[w]).astype(BF16)
        done_copy(c).start()
        sum_g = jnp.zeros((8, DM), F32)
        sum_b = jnp.zeros((8, DM), F32)
        for r in range(0, R, RB):
            xhat, inv = normalised(sec[r : r + RB, :])
            d_out = dsn[r : r + RB, :]
            sum_g = sum_g + fold(d_out * xhat)
            sum_b = sum_b + fold(d_out)
            dsec[p, r : r + RB, :] = norm_back(d_out, n2g[...], xhat, inv) + dy[r : r + RB, :].astype(F32)
        sums[:, O_N2G : O_N2G + DM] += sum_g
        sums[:, O_N2B : O_N2B + DM] += sum_b

    def second_half(c):
        p = lax.rem(c, SLOTS)
        low = dsec[p].astype(BF16)
        sums[:, O_PB : O_PB + DM] += fold(low.astype(F32))
        dy[...] = low
        g_proj[...] += dot_tn(att[p], dy[...])
        back = dot_nt(dy[...], wproj[...])
        for w in range(CW):
            for g in range(GROUPS):
                piece = back[w * RW : (w + 1) * RW, g * LN : (g + 1) * LN]
                d_heads[w, g, 0:JP, :] = padded(piece).astype(BF16)

        def attend(w, carry):
            rows = pl.ds(pl.multiple_of(w * RW, 8), RW)
            for g in range(GROUPS):
                wide[0, g * JP : (g + 1) * JP, :] = dot_nt(qkv[p, w, 2, g, 0:JP, :], by_head(d_heads[w, g]))
            for g in range(GROUPS):
                stage[rows, 2 * DM + g * LN : 2 * DM + (g + 1) * LN] = dot(prob[p, w, g], by_head(d_heads[w, g]))[0:RW]
            for g in range(GROUPS):
                for h in range(PER):
                    lane_h = slice(h * LN, (h + 1) * LN)
                    pr = prob[p, w, g, :, lane_h].astype(F32)
                    pd = pr * wide[0, g * JP : (g + 1) * JP, lane_h]
                    d_s = pd - pr * jnp.sum(pd, axis=0, keepdims=True)
                    ds_acc[g * PER + h] += d_s
                    slim[0, g * JP : (g + 1) * JP, lane_h] = (d_s * SCALE).astype(BF16)
            for g in range(GROUPS):
                mixed = dot_tn(qkv[p, w, 1, g, 0:JP, :], slim[0, g * JP : (g + 1) * JP, :])
                for h in range(PER):
                    owns[g, h * HD : (h + 1) * HD, :] = mixed[h * HD : (h + 1) * HD, h * LN : (h + 1) * LN]
            for g in range(GROUPS):
                stage[rows, DM + g * LN : DM + (g + 1) * LN] = dot(slim[0, g * JP : (g + 1) * JP, :], by_head(qkv[p, w, 0, g]))[0:RW]
            for g in range(GROUPS):
                stage[rows, g * LN : (g + 1) * LN] = owns[g].T[0:RW]
            return carry

        lax.fori_loop(0, CW, attend, 0)
        sum_g = jnp.zeros((8, DM), F32)
        sum_b = jnp.zeros((8, DM), F32)
        sum_q = jnp.zeros((8, DM), F32)
        sum_v = jnp.zeros((8, DM), F32)
        for r in range(0, R, RB):
            low = stage[r : r + RB, :].astype(BF16)
            dpk[r : r + RB, :] = low
            sum_q = sum_q + fold(low[:, 0:DM].astype(F32))
            sum_v = sum_v + fold(low[:, 2 * DM :].astype(F32))
        sums[:, O_QB : O_QB + DM] += sum_q
        sums[:, O_VB : O_VB + DM] += sum_v
        dsn[...] = dot_nt(dpk[...], wqkv[...])
        for r in range(0, R, RB):
            xhat, inv = normalised(res[p, r : r + RB, :])
            fst[r : r + RB, :] = (xhat * n1g[...] + n1b[...]).astype(BF16)
            d_out = dsn[r : r + RB, :]
            sum_g = sum_g + fold(d_out * xhat)
            sum_b = sum_b + fold(d_out)
            d_res = norm_back(d_out, n1g[...], xhat, inv) + dsec[p, r : r + RB, :]
            sn[r : r + RB, :] = d_res.astype(BF16)
        sums[:, O_N1G : O_N1G + DM] += sum_g
        sums[:, O_N1B : O_N1B + DM] += sum_b
        wide[0, 0:R, :] = dot_nt(sn[...], wp[0:DM, :])
        wide[0, R : 2 * R, :] = dot_nt(sn[...], wp[DM:WIDTH, :])
        sum_g = jnp.zeros((8, WIDTH), F32)
        sum_b = jnp.zeros((8, WIDTH), F32)
        for r in range(0, R, RB):
            xhat, inv = normalised(merged_rows(c, r))
            nrm[r : r + RB, :] = (xhat * n0g[...] + n0b[...]).astype(BF16)
            d_out = jnp.concatenate([wide[0, r : r + RB, :], wide[0, R + r : R + r + RB, :]], axis=1)
            sum_g = sum_g + fold(d_out * xhat)
            sum_b = sum_b + fold(d_out)
            low = norm_back(d_out, n0g[...], xhat, inv).astype(BF16)
            for s in range(n_head):
                rin[c, s, r : r + RB, :] = low[:, s * lanes : (s + 1) * lanes]
        sums[:, O_N0G : O_N0G + WIDTH] += sum_g
        sums[:, O_N0B : O_N0B + WIDTH] += sum_b
        for k in range(1, n_head):
            out_copy(c, k).start()
        own_out(c).start()
        g_qkv[...] += dot_tn(fst[...], dpk[...])
        g_red[...] += dot_tn(nrm[...], sn[...])
        own_out(c).wait()

    def unpack(c):
        for k in range(1, n_head):
            pltpu.make_async_remote_copy(
                src_ref=rin.at[c, me], dst_ref=rout.at[c, lax.rem(me + n_head - k, n_head)],
                send_sem=out_send.at[c, k], recv_sem=out_recv.at[c, k],
                device_id={"head": peer(k)}, device_id_type=MESH,
            ).wait_recv()

        @pl.when(c >= 2)
        def _():
            sect_copy(c - 2).wait()

        for s in range(n_head):
            turned = dot_nt(eye_lanes, rout[c, s])
            for w in range(CW):
                xv[lax.rem(c, 2), s, w] = turned[:, w * RW : w * RW + WT].astype(BF16)
        sect_copy(c).start()

    def sent(c, carry):
        for k in range(1, n_head):
            in_copy(c, k).wait_send()
        return carry

    def step(s, carry):
        @pl.when(s < n_chunk)
        def _():
            first_half(s)

        if n_win is not None:
            @pl.when(s == n_chunk - 1)
            def _():
                for f in feeds:
                    f.start_pair()

            @pl.when(s == n_chunk)
            def _():
                for f in feeds:
                    f.start_plane()

        @pl.when(s == LAG)
        def _():
            lax.fori_loop(0, n_chunk, sent, 0)
            for k in range(1, n_head):
                pl.semaphore_signal(free_sem, inc=1, device_id={"head": peer(k)}, device_id_type=MESH)
            pl.semaphore_wait(free_sem, n_head - 1)

        @pl.when(s >= LAG)
        def _():
            second_half(s - LAG)

        if n_win is not None:
            @pl.when(s == n_chunk + LAG - 1)
            def _():
                for f in others:
                    f.start_pair()
                table_sums()
                small_in[at_pair, 0:HEADS, :] = vector_rows()
                small_pair().start()

        return carry

    def vector_rows():
        row = jnp.sum(sums[...], axis=0, keepdims=True)
        return jnp.concatenate([row[:, r * DM : (r + 1) * DM] for r in range(O_END // DM)], axis=0)

    def table_sums():
        total = jnp.zeros((HEADS, 4 * LN), F32)
        for row in range(WIN):
            spread = jnp.zeros((WIN * HEADS, 2 * LN), F32)
            whole = jnp.concatenate([ds_acc[:, row * WIN + col, :] for col in range(WIN)], axis=0)
            for part in split3(whole):
                spread = spread + dot_nt(part, pick)
            for col in range(WIN):
                off = offset_of(WT - 1) - offset_of(row * WIN + col)
                piece = jnp.concatenate(
                    [spread[col * HEADS : (col + 1) * HEADS], jnp.zeros((HEADS, 2 * LN), F32)], axis=1
                )
                total = total + pltpu.roll(piece, off, 1)
        if n_win is None:
            g_small[HEADS:, :] = total
        else:
            small_in[at_pair, HEADS:, :] = total

    lax.fori_loop(0, n_chunk + LAG, step, 0)

    def unpack_range(low, high):
        def body(c, carry):
            unpack(c)
            return carry

        lax.fori_loop(low, high, body, 0)

    if n_win is None:
        g_small[0:HEADS, :] = vector_rows()
        table_sums()
        unpack_range(0, n_chunk)
    else:
        for f in others:
            f.start_plane()
        small_pair().wait_recv()
        small_in[at_plane + my_win] = small_in[at_pair] + small_in[at_pair + 1]
        for k in range(1, n_win):
            small_plane(k).start()
        for f in feeds:
            f.start_near()
        unpack_range(0, n_chunk - 4)
        for f in feeds:
            f.start_far()
        unpack_range(n_chunk - 4, n_chunk - 3)
        for k in range(1, n_win):
            small_plane(k, lax.rem(my_win + n_win - k, n_win)).wait_recv()
        total = small_in[at_plane]
        for w in range(1, n_win):
            total = total + small_in[at_plane + w]
        small_in[at_near] = total
        small_near().start()
        for f in others:
            f.start_near()
        for f in feeds:
            f.finish()
        small_near().wait_recv()
        small_in[at_far] = small_in[at_near] + small_in[at_near + 1]
        small_far().start()
        for f in others:
            f.start_far()
        unpack_range(n_chunk - 3, n_chunk - 1)
        for f in reversed(others):
            f.finish()
        small_far().wait_recv()
        g_small[...] = small_in[at_far] + small_in[at_far + 1]
        unpack_range(n_chunk - 1, n_chunk)
        others[-1].finish_gather()
        for f in feeds + others:
            f.drain()
        small_pair().wait_send()
        for k in range(1, n_win):
            small_plane(k).wait_send()
        small_near().wait_send()
        small_far().wait_send()
    for c in range(max(0, n_chunk - 2), n_chunk):
        sect_copy(c).wait()
        done_copy(c).wait()

    def drain(c, carry):
        for k in range(1, n_head):
            out_copy(c, k).wait_send()
        return carry

    lax.fori_loop(0, n_chunk, drain, 0)


def run_kernel(n_head, n_win, n_chunk, share, args):
    lanes = QUADS * share
    any_, vmem = pl.BlockSpec(memory_space=pl.ANY), pl.BlockSpec(memory_space=pltpu.VMEM)
    smem = pl.BlockSpec(memory_space=pltpu.SMEM)
    windows = n_chunk * CW
    in_specs = [
        any_, any_, vmem, vmem, vmem, vmem, any_, vmem, vmem, vmem, any_, vmem, vmem, vmem,
        any_, vmem, any_, vmem, smem, any_,
    ]
    out_shape = [
        jax.ShapeDtypeStruct((windows, WT, DM), BF16),
        jax.ShapeDtypeStruct((n_head, n_chunk, CW, lanes, WT), BF16),
    ]
    dma = pltpu.SemaphoreType.DMA
    scratch = []
    if n_win is None:
        out_shape += [jax.ShapeDtypeStruct(m, F32) for m in MATRICES]
    else:
        devices, n_z = n_win * n_head, n_head // 2
        scratch += [pltpu.VMEM(m, F32) for m in MATRICES]
        shares = [(m // devices, cols) for m, cols in MATRICES]
        out_shape += [jax.ShapeDtypeStruct(m, F32) for m in shares[:-1]]
        out_shape += [jax.ShapeDtypeStruct((shares[-1][0] * n_win, DM), F32)]
        scratch += [pltpu.VMEM((rows * n_win * n_z, cols), BF16) for rows, cols in shares]
        scratch += [pltpu.VMEM((n_win - 1, rows * n_z, cols), BF16) for rows, cols in shares]
        scratch += [pltpu.VMEM((rows * (n_z // 2), cols), BF16) for rows, cols in shares]
        scratch += [pltpu.VMEM((rows, cols), BF16) for rows, cols in shares]
        scratch += [
            pltpu.VMEM((n_win, shares[-1][0], DM), BF16),
            pltpu.VMEM((n_win + 6, 2 * HEADS, DM), F32),
            dma((6, 2 * n_win + 2)), dma((6, 2 * n_win + 2)),
        ]
    out_shape += [jax.ShapeDtypeStruct((2 * HEADS, DM), F32)]
    out_specs = [any_, any_] + [vmem] * 6
    scratch += [
        pltpu.VMEM((2, n_head, CW, lanes, WT), BF16),
        pltpu.VMEM((n_chunk, n_head, R, lanes), BF16),
        pltpu.VMEM((n_chunk, n_head, R, lanes), BF16),
        pltpu.VMEM((WIDTH, DM), BF16),
        pltpu.VMEM((DM, 3 * DM), BF16),
        pltpu.VMEM((DM, DM), BF16),
        pltpu.VMEM((DM, FF), BF16),
        pltpu.VMEM((FF, DM), BF16),
        pltpu.VMEM((2, CW, WT, DM), BF16),
        pltpu.VMEM((R, WIDTH), BF16),
        pltpu.VMEM((SLOTS, R, DM), F32),
        pltpu.VMEM((R, DM), BF16),
        pltpu.VMEM((SLOTS, CW, 3, GROUPS, LN, LN), BF16),
        pltpu.VMEM((SLOTS, CW, GROUPS, JP, PER * LN), BF16),
        pltpu.VMEM((SLOTS, R, DM), BF16),
        pltpu.VMEM((R, 3 * DM), F32),
        pltpu.VMEM((R, DM), F32),
        pltpu.VMEM((R, DM), BF16),
        pltpu.VMEM((R, DM), BF16),
        pltpu.VMEM((2, GROUPS * JP, TILE), F32),
        pltpu.VMEM((2, GROUPS * JP, TILE), BF16),
        pltpu.VMEM((R, DM), F32),
        pltpu.VMEM((R, DM), F32),
        pltpu.VMEM((SLOTS, R, DM), F32),
        pltpu.VMEM((R, 3 * DM), BF16),
        pltpu.VMEM((CW, GROUPS, LN, LN), BF16),
        pltpu.VMEM((1, WIDTH), F32),
        pltpu.VMEM((1, WIDTH), F32),
        pltpu.VMEM((HEADS, 4 * LN), F32),
        pltpu.VMEM((GROUPS, LN, LN), F32),
        pltpu.VMEM((2, CW, WT, DM), BF16),
        pltpu.VMEM((8, O_END), F32),
        pltpu.VMEM((HEADS, JP, LN), F32),
        pltpu.VMEM((HEADS, JP, LN), F32),
        dma((n_chunk, n_head)), dma((n_chunk, n_head)), dma((n_chunk, n_head)), dma((n_chunk, n_head)),
        dma((2,)), dma((5,)), dma((2,)), dma, dma((2,)), pltpu.SemaphoreType.REGULAR, dma((2,)),
    ]
    return pl.pallas_call(
        functools.partial(kernel, n_head, n_win, n_chunk, share),
        out_shape=out_shape, in_specs=in_specs, out_specs=out_specs, scratch_shapes=scratch,
        compiler_params=pltpu.CompilerParams(
            collective_id=0, has_side_effects=True, vmem_limit_bytes=63 * 1024 * 1024
        ),
        cost_estimate=pl.CostEstimate(flops=27 * 10**9, bytes_accessed=30 * 10**6, transcendentals=10**7),
    )(*args)


def finish_kernel(n_head, devices, share, whole, *refs):
    arrays, small, outs = refs[:whole], refs[whole], refs[whole + 1 : -2 - whole]
    held, (in_sem, out_sem) = refs[-2 - whole : -2], refs[-2:]
    arriving, leaving = [], []
    for source, middle, target in zip(arrays, held, outs[:whole]):
        pieces = source.shape[0] if len(source.shape) > 2 else 1
        for i in range(pieces):
            part = pl.ds(i, 1) if pieces > 1 else pl.ds(0, source.shape[0])
            arriving.append(pltpu.make_async_copy(source.at[part], middle.at[part], in_sem.at[len(arriving)]))
            leaving.append(pltpu.make_async_copy(middle.at[part], target.at[part], out_sem.at[len(leaving)]))
    for copy in arriving:
        copy.start()
    n0g, n0b, n1g, n1b, qb, vb, table, pb, n2g, n2b, fc1b, fc2b = outs[whole:]
    head = lax.axis_index("head")
    at = lax.axis_index("win") * n_head + head

    def taken(start, size, spot):
        first = spot * size
        row = small[pl.ds(start // DM + first // DM, 1), :]
        return pltpu.roll(row, lax.rem(DM - lax.rem(first, DM), DM), 1)[:, 0:size]

    for target, start in (
        (n1g, O_N1G), (n1b, O_N1B), (qb, O_QB), (vb, O_VB), (pb, O_PB), (n2g, O_N2G), (n2b, O_N2B), (fc2b, O_FC2B),
    ):
        target[...] = taken(start, DM // devices, at)
    fc1b[...] = taken(O_FC1B, FF // devices, at)
    for target, start in ((n0g, O_N0G), (n0b, O_N0B)):
        row = taken(start, QUADS * share, head)
        for q in range(QUADS):
            target[q : q + 1, :] = row[:, q * share : (q + 1) * share]
    table[...] = small[HEADS:, 0:RELS]
    for copy, onward in zip(arriving, leaving):
        copy.wait()
        onward.start()
    for copy in leaving:
        copy.wait()


def run_finish(n_head, devices, share, args):
    any_, vmem = pl.BlockSpec(memory_space=pl.ANY), pl.BlockSpec(memory_space=pltpu.VMEM)
    block_out, section, red, qkv, proj, fc1, fc2, small = args
    whole = (block_out, section, red, qkv, proj, fc1, fc2)
    one, wide = (1, DM // devices), (1, FF // devices)
    norm = (QUADS, share)
    shapes = [(v.shape, v.dtype) for v in whole]
    shapes += [(m, F32) for m in (norm, norm, one, one, one, one, (HEADS, RELS), one, one, one, wide, one)]
    count = sum(v.shape[0] if v.ndim > 2 else 1 for v in whole)
    outs = pl.pallas_call(
        functools.partial(finish_kernel, n_head, devices, share, len(whole)),
        out_shape=[jax.ShapeDtypeStruct(m, t) for m, t in shapes],
        in_specs=[any_] * len(whole) + [vmem], out_specs=[any_] * len(whole) + [vmem] * 12,
        scratch_shapes=[pltpu.VMEM(v.shape, v.dtype) for v in whole]
        + [pltpu.SemaphoreType.DMA((count,)), pltpu.SemaphoreType.DMA((count,))],
        compiler_params=pltpu.CompilerParams(vmem_limit_bytes=63 * 1024 * 1024),
    )(*args)
    block_out, section, red, qkv, proj, fc1, fc2, n0g, n0b, n1g, n1b, qb, vb, table, pb, n2g, n2b, fc1b, fc2b = outs
    return block_out, section, red, n0g, n0b, n1g, n1b, qkv, qb, vb, table, proj, pb, n2g, n2b, fc1, fc1b, fc2, fc2b


def local(
    n_head, section_rows, reduce_weight, norm0_gain, norm0_bias, norm1_gain, norm1_bias, qkv_weight, q_bias, v_bias,
    rel_table, proj_weight, proj_bias, norm2_gain, norm2_bias, fc1_weight, fc1_bias, fc2_weight, fc2_bias,
    window_valid, cotangent,
):
    group_windows, tokens, quads, share = section_rows.shape
    windows = cotangent.shape[0]
    n_chunk = windows // CW
    lanes = quads * share
    rows = section_rows.transpose(0, 2, 3, 1).reshape(n_head, n_chunk, CW, lanes, tokens)

    def row(v):
        return v.reshape(1, -1)

    args = (
        rows, reduce_weight.reshape(quads, n_head, share, DM), norm0_gain, norm0_bias,
        row(norm1_gain), row(norm1_bias), qkv_weight, row(q_bias), row(v_bias),
        rel_table, proj_weight, row(proj_bias), row(norm2_gain), row(norm2_bias),
        fc1_weight, row(fc1_bias), fc2_weight, row(fc2_bias), window_valid, cotangent,
    )
    n_win = lax.axis_size("win")
    devices = n_win * n_head
    inside = n_head == 8 and all((m // devices) % 16 == 0 for m, unused in MATRICES)
    block_out, section, fc1, fc2, qkv, proj, red, small = run_kernel(
        n_head, n_win if inside else None, n_chunk, share, args
    )
    both = ("win", "head")

    def scattered(v):
        return lax.psum_scatter(v.astype(BF16), both, scatter_dimension=0, tiled=True).astype(F32)

    if not inside:
        fc1, fc2, qkv, proj = scattered(fc1), scattered(fc2), scattered(qkv), scattered(proj)
        red = lax.psum_scatter(red.astype(BF16), "head", scatter_dimension=0, tiled=True)
        red = lax.psum(red, "win").astype(F32)
        small = lax.psum(small, both)
    block_out, section, red, n0g, n0b, n1g, n1b, qkv, qb, vb, table, proj, pb, n2g, n2b, fc1, fc1b, fc2, fc2b = (
        run_finish(n_head, devices, share, (block_out, section, red, qkv, proj, fc1, fc2, small))
    )
    section_grad = section.reshape(group_windows, quads, share, tokens).transpose(0, 3, 1, 2)

    def flat(v):
        return v.reshape(-1)

    return (
        block_out, section_grad, red.reshape(quads, share, DM), n0g, n0b, flat(n1g), flat(n1b), qkv, flat(qb), flat(vb),
        table, proj, flat(pb), flat(n2g), flat(n2b), fc1, flat(fc1b), fc2, flat(fc2b),
    )


def solution(mesh):
    in_specs = (
        P("win", None, None, "head"),
        P(),
        P(),
        P(),
        P(),
        P(),
        P(),
        P(),
        P(),
        P(),
        P(),
        P(),
        P(),
        P(),
        P(),
        P(),
        P(),
        P(),
        P(("win", "head")),
        P(("win", "head"), None, None),
    )
    out_specs = (
        P(("win", "head"), None, None),
        P("win", None, None, "head"),
        P(None, "head", None),
        P(None, "head"),
        P(None, "head"),
        P(("win", "head")),
        P(("win", "head")),
        P(("win", "head"), None),
        P(("win", "head")),
        P(("win", "head")),
        P(),
        P(("win", "head"), None),
        P(("win", "head")),
        P(("win", "head")),
        P(("win", "head")),
        P(("win", "head"), None),
        P(("win", "head")),
        P(("win", "head"), None),
        P(("win", "head")),
    )
    return jax.shard_map(
        functools.partial(local, mesh.shape["head"]), mesh=mesh, in_specs=in_specs, out_specs=out_specs, check_vma=False)
```

```python
import functools

import jax
import jax.numpy as jnp
from jax import lax
from jax.experimental import pallas as pl
from jax.experimental.pallas import tpu as pltpu
from jax.sharding import PartitionSpec as P

C2 = 256
DM = 512
HEADS = 16
HD = 32
FF = 2048
WIN = 10
WT = 100
RELS = 361
SPAN = 2 * WIN - 1

QUADS = 4
WIDTH = QUADS * C2
CW = 2
RW = 104
R = CW * RW
JP = 112
LN = 128
GROUPS = 4
PER = 4
LAG = 4
SLOTS = LAG + 1
AHEAD = 2
RB = 16
TILE = 512
EPS = 1e-05
LOG2E = 1.4426950408889634
SCALE = HD ** (-0.5)

MESH = pl.DeviceIdType.MESH
F32 = jnp.float32
BF16 = jnp.bfloat16

O_QB, O_VB, O_PB, O_FC1B, O_FC2B = 0, 512, 1024, 1536, 3584
O_N1G, O_N1B, O_N2G, O_N2B, O_N0G, O_N0B, O_END = 4096, 4608, 5120, 5632, 6144, 7168, 8192


MATRICES = ((DM, FF), (FF, DM), (DM, 3 * DM), (DM, DM), (WIDTH, DM))


def dot(a, b):
    return lax.dot_general(a, b, (((1,), (0,)), ((), ())), preferred_element_type=F32)


def dot_nt(a, b):
    return lax.dot_general(a, b, (((1,), (1,)), ((), ())), preferred_element_type=F32)


def dot_tn(a, b):
    return lax.dot_general(a, b, (((0,), (0,)), ((), ())), preferred_element_type=F32)


def normalised(v):
    centred = v - jnp.mean(v, axis=-1, keepdims=True)
    inv = lax.rsqrt(jnp.mean(centred * centred, axis=-1, keepdims=True) + EPS)
    return centred * inv, inv


def norm_back(d_out, gain, xhat, inv):
    u = d_out * gain
    mean_u = jnp.mean(u, axis=-1, keepdims=True)
    mean_ux = jnp.mean(u * xhat, axis=-1, keepdims=True)
    return (u - mean_u - xhat * mean_ux) * inv


def fold(v):
    total = v[0:8]
    for r in range(8, v.shape[0], 8):
        total = total + v[r : r + 8]
    return total


def weave(one, two):
    marks = [((i + 0.5) / len(one), piece) for i, piece in enumerate(one)]
    marks += [((i + 0.5) / len(two), piece) for i, piece in enumerate(two)]
    for unused, piece in sorted(marks, key=lambda m: m[0]):
        piece()


def gelu_parts(x):
    z = jnp.abs(x) * 0.7071067811865476
    t = 1.0 / (1.0 + 0.3275911 * z)
    e = jnp.exp2(x * x * (-0.5 * LOG2E))
    poly = ((((1.061405429 * t - 1.453152027) * t + 1.421413741) * t - 0.284496736) * t + 0.254829592) * t
    half = 0.5 * poly * e
    cdf = jnp.where(x < 0, half, 1.0 - half)
    return x * cdf, cdf + x * e * 0.3989422804014327


def split3(v):
    hi = v.astype(BF16)
    rest = v - hi.astype(F32)
    mid = rest.astype(BF16)
    low = (rest - mid.astype(F32)).astype(BF16)
    return hi, mid, low


def offset_of(j):
    return (j // WIN) * SPAN + j % WIN


def kernel(
    n_head, n_win, n_chunk, share,
    x_hbm, wp_hbm, gain0, bias0, n1g, n1b, wqkv_hbm, qb, vb, table_in, wproj_hbm, pb, n2g, n2b,
    wfc1_hbm, fc1b, wfc2_hbm, fc2b, valid, cot_hbm,
    *refs,
):
    if n_win is None:
        (out_ref, sect_hbm, g_fc1, g_fc2, g_qkv, g_proj, g_red, g_small), refs = refs[:8], refs[8:]
    else:
        (out_ref, sect_hbm, o_fc1, o_fc2, o_qkv, o_proj, o_red, g_small), refs = refs[:8], refs[8:]
        (g_fc1, g_fc2, g_qkv, g_proj, g_red), refs = refs[:5], refs[5:]
        first_in, refs = refs[:5], refs[5:]
        plane_in, refs = refs[:5], refs[5:]
        near_in, refs = refs[:5], refs[5:]
        far_in, refs = refs[:5], refs[5:]
        (gather_in, small_in, sum_send, sum_recv), refs = refs[:4], refs[4:]
    (xv, send_in, rin, wp, wqkv, wproj, wfc1, wfc2, cot,
    nrm, res, fst, qkv, prob, att, stage, sec, sn, dy, wide, slim, ffo, dsn, dsec, dpk, d_heads, n0g, n0b, table, owns, out_stage, sums, bias_t, ds_acc,
    in_send, in_recv, out_send, out_recv, x_sem, w_sem, cot_sem, own_sem, sect_sem, free_sem, done_sem) = refs
    rout = send_in
    me = lax.axis_index("head")
    lanes = QUADS * share

    def peer(k):
        return lax.rem(me + k, n_head)

    if n_win is not None:
        my_win = lax.axis_index("win")
        core, my_z = lax.rem(me, 2), me // 2
        n_z = n_head // 2
        sibling = me + 1 - 2 * core
        near_z = my_z + 1 - 2 * lax.rem(my_z, 2)
        far_z = my_z + 2 - 4 * (my_z // 2)

        def win_peer(k):
            return lax.rem(my_win + k, n_win)

        class Scatter:
            def __init__(self, spot, total, hold, out, by_head=False):
                self.spot, self.total, self.hold, self.out = spot, total, hold, out
                self.rows = total.shape[0] // (n_win * n_head)
                self.cols = total.shape[1]
                self.by_head = by_head
                half = total.shape[0] // 2
                self.at_plane = half
                self.at_near = half + (n_win - 1) * n_z * self.rows
                self.at_far = self.at_near + (n_z // 2) * self.rows

            def block(self, w, z, c):
                head = z * 2 + c
                spot = head * n_win + w if self.by_head else w * n_head + head
                return pl.ds(pl.multiple_of(spot * self.rows, 16), self.rows)

            def span(self, start, count=1):
                return pl.ds(pl.multiple_of(start, 16), count * self.rows)

            def copy(self, j, source, target, to):
                return pltpu.make_async_remote_copy(
                    src_ref=source, dst_ref=target, send_sem=sum_send.at[self.spot, j], recv_sem=sum_recv.at[self.spot, j],
                    device_id=to, device_id_type=MESH,
                )

            def pair_copy(self):
                return self.copy(
                    0, self.hold.at[pl.ds(0, self.at_plane), :], first_in[self.spot], {"head": sibling}
                )

            def plane_copy(self, k):
                source = self.hold.at[self.span(self.at_plane + (k - 1) * n_z * self.rows, n_z), :]
                return self.copy(k, source, plane_in[self.spot].at[k - 1], {"win": win_peer(k)})

            def near_copy(self):
                source = self.hold.at[self.span(self.at_near, n_z // 2), :]
                return self.copy(n_win, source, near_in[self.spot], {"head": near_z * 2 + core})

            def far_copy(self):
                source = self.hold.at[self.span(self.at_far), :]
                return self.copy(n_win + 1, source, far_in[self.spot], {"head": far_z * 2 + core})

            def start_pair(self):
                def body(i, carry):
                    w, z = i // n_z, lax.rem(i, n_z)
                    self.hold[self.span(i * self.rows), :] = self.total[self.block(w, z, 1 - core), :].astype(BF16)
                    return carry

                lax.fori_loop(0, n_win * n_z, body, 0)
                self.pair_copy().start()

            def start_plane(self):
                self.pair_copy().wait_recv()
                for k in range(1, n_win + 1):
                    w = lax.rem(my_win + k, n_win)

                    def body(z, carry):
                        mine = self.block(w, z, core)
                        value = self.total[mine, :] + first_in[self.spot][
                            self.span((w * n_z + z) * self.rows), :
                        ].astype(F32)
                        if k == n_win:
                            self.total[mine, :] = value
                        else:
                            at = self.at_plane + ((k - 1) * n_z + z) * self.rows
                            self.hold[self.span(at), :] = value.astype(BF16)
                        return carry

                    lax.fori_loop(0, n_z, body, 0)
                    if k < n_win:
                        self.plane_copy(k).start()

            def start_near(self):
                for k in range(1, n_win):
                    self.plane_copy(k).wait_recv()

                def both(z):
                    value = self.total[self.block(my_win, z, core), :]
                    for k in range(1, n_win):
                        value = value + plane_in[self.spot][k - 1, self.span(z * self.rows), :].astype(F32)
                    return value

                for j in range(n_z // 2):
                    sent = both(j * 2 + lax.rem(near_z, 2))
                    self.hold[self.span(self.at_near + j * self.rows), :] = sent.astype(BF16)
                self.near_copy().start()
                for j in range(n_z // 2):
                    z = j * 2 + lax.rem(my_z, 2)
                    self.total[self.block(my_win, z, core), :] = both(z)

            def after_near(self, j):
                kept = self.total[self.block(my_win, j * 2 + lax.rem(my_z, 2), core), :]
                return kept + near_in[self.spot][self.span(j * self.rows), :].astype(F32)

            def start_far(self):
                self.near_copy().wait_recv()
                self.hold[self.span(self.at_far), :] = self.after_near(far_z // 2).astype(BF16)
                self.far_copy().start()

            def finish(self):
                self.far_copy().wait_recv()
                value = self.after_near(my_z // 2) + far_in[self.spot][...].astype(F32)
                if not self.by_head:
                    self.out[...] = value
                    return
                gather_in[my_win] = value.astype(BF16)
                for k in range(1, n_win):
                    self.gather_copy(k).start()

            def gather_copy(self, k):
                return self.copy(
                    n_win + 1 + k, gather_in.at[my_win], gather_in.at[my_win], {"win": win_peer(k)}
                )

            def finish_gather(self):
                for k in range(1, n_win):
                    source = lax.rem(my_win + n_win - k, n_win)
                    self.copy(
                        n_win + 1 + k, gather_in.at[my_win], gather_in.at[source], {"win": win_peer(k)}
                    ).wait_recv()
                for w in range(n_win):
                    self.out[w * self.rows : (w + 1) * self.rows, :] = gather_in[w].astype(F32)

            def drain(self):
                self.pair_copy().wait_send()
                for k in range(1, n_win):
                    self.plane_copy(k).wait_send()
                    if self.by_head:
                        self.gather_copy(k).wait_send()
                self.near_copy().wait_send()
                self.far_copy().wait_send()

        feeds = [Scatter(0, g_fc1, wfc1, o_fc1), Scatter(1, g_fc2, wfc2, o_fc2)]
        others = [Scatter(2, g_qkv, wqkv, o_qkv), Scatter(3, g_proj, wproj, o_proj), Scatter(4, g_red, wp, o_red, True)]

        def small_copy(j, source, target, to):
            return pltpu.make_async_remote_copy(
                src_ref=small_in.at[source], dst_ref=small_in.at[target], send_sem=sum_send.at[5, j],
                recv_sem=sum_recv.at[5, j], device_id=to, device_id_type=MESH,
            )

        at_pair, at_plane, at_near, at_far = 0, 2, 2 + n_win, 4 + n_win

        def small_pair():
            return small_copy(0, at_pair, at_pair + 1, {"head": sibling})

        def small_plane(k, target=None):
            return small_copy(k, at_plane + my_win, at_plane + (my_win if target is None else target), {"win": win_peer(k)})

        def small_near():
            return small_copy(n_win, at_near, at_near + 1, {"head": near_z * 2 + core})

        def small_far():
            return small_copy(n_win + 1, at_far, at_far + 1, {"head": far_z * 2 + core})

    def in_copy(c, k):
        to = peer(k)
        return pltpu.make_async_remote_copy(
            src_ref=send_in.at[c, to], dst_ref=rin.at[c, me], send_sem=in_send.at[c, k], recv_sem=in_recv.at[c, k],
            device_id={"head": to}, device_id_type=MESH,
        )

    def out_copy(c, k):
        to = peer(k)
        return pltpu.make_async_remote_copy(
            src_ref=rin.at[c, to], dst_ref=rout.at[c, me], send_sem=out_send.at[c, k], recv_sem=out_recv.at[c, k],
            device_id={"head": to}, device_id_type=MESH,
        )

    def own_in(c):
        return pltpu.make_async_copy(send_in.at[c, me], rin.at[c, me], own_sem)

    def own_out(c):
        return pltpu.make_async_copy(rin.at[c, me], rout.at[c, me], own_sem)

    def x_copy(c):
        return pltpu.make_async_copy(x_hbm.at[:, c], xv.at[c % 2], x_sem.at[c % 2])

    def cot_copy(c):
        return pltpu.make_async_copy(cot_hbm.at[pl.ds(c * CW, CW)], cot.at[lax.rem(c, 2)], cot_sem.at[lax.rem(c, 2)])

    def done_copy(c):
        return pltpu.make_async_copy(out_stage.at[lax.rem(c, 2)], out_ref.at[pl.ds(c * CW, CW)], done_sem.at[lax.rem(c, 2)])

    def sect_copy(c):
        return pltpu.make_async_copy(xv.at[c % 2], sect_hbm.at[:, c], sect_sem.at[c % 2])

    weights = [
        pltpu.make_async_copy(wqkv_hbm, wqkv, w_sem.at[1]),
        pltpu.make_async_copy(wproj_hbm, wproj, w_sem.at[2]),
        pltpu.make_async_copy(wfc1_hbm, wfc1, w_sem.at[3]),
        pltpu.make_async_copy(wfc2_hbm, wfc2, w_sem.at[4]),
    ]

    for c in range(min(2, n_chunk)):
        x_copy(c).start()
    barrier = pltpu.get_barrier_semaphore()
    for k in range(1, n_head):
        pl.semaphore_signal(barrier, inc=1, device_id={"head": peer(k)}, device_id_type=MESH)
    if n_win is not None:
        for k in range(1, n_win):
            pl.semaphore_signal(barrier, inc=1, device_id={"win": win_peer(k)}, device_id_type=MESH)
    for q in range(QUADS):
        for s in range(n_head):
            pltpu.make_async_copy(
                wp_hbm.at[q, s], wp.at[pl.ds((s * QUADS + q) * share, share), :], w_sem.at[0]
            ).start()
    for w in weights:
        w.start()
    cot_copy(0).start()

    def eye(rows, cols):
        spot = lax.broadcasted_iota(jnp.int32, (rows, cols), 0) - lax.broadcasted_iota(jnp.int32, (rows, cols), 1)
        return (spot == 0).astype(F32).astype(BF16)

    eye_rows, eye_lanes = eye(RW, WT), eye(lanes, lanes)
    eye_tokens, eye_heads = eye(RW, LN), eye(LN, LN)

    def repack(c):
        x_copy(c).wait()
        for d in range(n_head):
            rows = [dot_nt(eye_rows, xv[c % 2, d, w]) for w in range(CW)]
            send_in[c, d] = jnp.concatenate(rows, axis=0).astype(BF16)

    def send(c):
        for k in range(1, n_head):
            in_copy(c, k).start()
        own_in(c).start()
        own_in(c).wait()

    repack(0)
    pl.semaphore_wait(barrier, n_head - 1 + (0 if n_win is None else n_win - 1))
    send(0)

    def send_rest(c, carry):
        @pl.when(c < n_chunk - 1)
        def _():
            x_copy(c + 1).start()

        repack(c)

        @pl.when(c < AHEAD)
        def _():
            send(c)

        return carry

    lax.fori_loop(1, n_chunk, send_rest, 0)

    def zero(ref):
        def body(r, carry):
            ref[pl.ds(pl.multiple_of(r * 8, 8), 8), :] = jnp.zeros((8, ref.shape[1]), F32)
            return carry
        lax.fori_loop(0, ref.shape[0] // 8, body, 0)

    for ref in (g_fc1, g_fc2, g_qkv, g_proj, g_red, sums):
        zero(ref)
    ds_acc[...] = jnp.zeros_like(ds_acc)

    def zero_heads(c, carry):
        qkv[c] = jnp.zeros(qkv.shape[1:], BF16)
        return carry

    lax.fori_loop(0, SLOTS, zero_heads, 0)
    d_heads[...] = jnp.zeros_like(d_heads)
    bias_t[:, WT:, :] = jnp.full((HEADS, JP - WT, LN), -1e30, F32)

    for row, given in ((n0g, gain0), (n0b, bias0)):
        for s in range(n_head):
            row[:, s * lanes : (s + 1) * lanes] = jnp.concatenate(
                [given[q : q + 1, s * share : (s + 1) * share] for q in range(QUADS)], axis=1
            )
    table[...] = jnp.zeros_like(table)
    table[:, 0:RELS] = table_in[...]
    spot = lax.broadcasted_iota(jnp.int32, (2 * LN, LN), 0)
    token = lax.broadcasted_iota(jnp.int32, (2 * LN, LN), 1)
    token_row = (token * 205) >> 11
    pick = ((spot == token_row * SPAN + token - token_row * WIN) & (token < WT)).astype(F32).astype(BF16)
    for row in range(WIN):
        parts = []
        for col in range(WIN):
            off = offset_of(WT - 1) - offset_of(row * WIN + col)
            parts.append(table[:, off : off + 2 * LN])
        hi, mid, low = split3(jnp.concatenate(parts, axis=0))
        found = (dot(hi, pick) + dot(mid, pick) + dot(low, pick)) * LOG2E
        for col in range(WIN):
            bias_t[:, row * WIN + col, :] = found[col * HEADS : (col + 1) * HEADS]

    pltpu.make_async_copy(wp, wp, w_sem.at[0]).wait()
    for w in weights:
        w.wait()

    lane = lax.broadcasted_iota(jnp.int32, (1, LN), 1)
    masks = [((lane >= h * HD) & (lane < (h + 1) * HD)).astype(F32).astype(BF16) for h in range(PER)]

    def by_head(v):
        return jnp.concatenate([v * m for m in masks], axis=0)

    def merged_rows(c, r):
        return jnp.concatenate([rin[c, s, pl.ds(r, RB), :] for s in range(n_head)], axis=1).astype(F32)

    def padded(v):
        return jnp.concatenate([v, jnp.zeros((JP - RW, v.shape[1]), F32)], axis=0)

    def first_half(c):
        p = lax.rem(c, SLOTS)
        for k in range(1, n_head):
            in_copy_wait = pltpu.make_async_remote_copy(
                src_ref=send_in.at[c, me], dst_ref=rin.at[c, lax.rem(me + n_head - k, n_head)],
                send_sem=in_send.at[c, k], recv_sem=in_recv.at[c, k],
                device_id={"head": peer(k)}, device_id_type=MESH,
            )
            in_copy_wait.wait_recv()

        @pl.when(c + AHEAD < n_chunk)
        def _():
            send(c + AHEAD)

        for r in range(0, R, RB):
            xhat, unused = normalised(merged_rows(c, r))
            nrm[r : r + RB, :] = (xhat * n0g[...] + n0b[...]).astype(BF16)
        res[p] = dot(nrm[...], wp[...])
        for r in range(0, R, RB):
            xhat, unused = normalised(res[p, r : r + RB, :])
            fst[r : r + RB, :] = (xhat * n1g[...] + n1b[...]).astype(BF16)
        for t in range(3):
            part = dot(fst[...], wqkv[:, t * DM : (t + 1) * DM])
            if t == 0:
                part = part + qb[...]
            if t == 2:
                part = part + vb[...]
            for w in range(CW):
                for g in range(GROUPS):
                    piece = part[w * RW : (w + 1) * RW, g * LN : (g + 1) * LN]
                    qkv[p, w, t, g, 0:JP, :] = padded(piece).astype(BF16)

        def attend(w, carry):
            for g in range(GROUPS):
                wide[0, g * JP : (g + 1) * JP, :] = dot_nt(qkv[p, w, 1, g, 0:JP, :], by_head(qkv[p, w, 0, g]))
            for g in range(GROUPS):
                for h in range(PER):
                    lane_h = slice(h * LN, (h + 1) * LN)
                    s = wide[0, g * JP : (g + 1) * JP, lane_h] * (SCALE * LOG2E) + bias_t[g * PER + h]
                    e = jnp.exp2(s - jnp.max(s, axis=0, keepdims=True))
                    prob[p, w, g, :, lane_h] = (e * (1.0 / jnp.sum(e, axis=0, keepdims=True))).astype(BF16)
            for g in range(GROUPS):
                mixed = dot_tn(qkv[p, w, 2, g, 0:JP, :], prob[p, w, g])
                for h in range(PER):
                    owns[g, h * HD : (h + 1) * HD, :] = mixed[h * HD : (h + 1) * HD, h * LN : (h + 1) * LN]
            for g in range(GROUPS):
                stage[pl.ds(pl.multiple_of(w * RW, 8), RW), g * LN : (g + 1) * LN] = owns[g].T[0:RW]
            return carry

        lax.fori_loop(0, CW, attend, 0)
        att[p] = stage[:, 0:DM].astype(BF16)
        sec[...] = res[p] + dot(att[p], wproj[...]) + pb[...]
        for r in range(0, R, RB):
            xhat, unused = normalised(sec[r : r + RB, :])
            sn[r : r + RB, :] = (xhat * n2g[...] + n2b[...]).astype(BF16)
        cot_copy(c).wait()

        @pl.when(c + 1 < n_chunk)
        def _():
            cot_copy(c + 1).start()

        flags = [valid[c * CW + w].astype(F32) for w in range(CW)]
        tail = jnp.zeros((RW - WT, DM), F32)
        pieces = []
        for w in range(CW):
            pieces += [cot[lax.rem(c, 2), w].astype(F32) * flags[w], tail]
        up = jnp.concatenate(pieces, axis=0)
        dy[...] = up.astype(BF16)
        sums[:, O_FC2B : O_FC2B + DM] += fold(up)
        ffo[...] = sec[...] + fc2b[...]
        dsn[...] = jnp.zeros_like(dsn)

        def spread(t):
            b, half = t % 2, TILE // 2
            for n in range(2):
                cols = slice(t * TILE + n * half, t * TILE + (n + 1) * half)
                into = slice(n * half, (n + 1) * half)

                def one(cols=cols, into=into):
                    wide[b, 0:R, into] = dot(sn[...], wfc1[:, cols]) + fc1b[:, cols]

                def two(cols=cols, into=into):
                    wide[b, R : 2 * R, into] = dot_nt(dy[...], wfc2[cols, :])

                yield one
                yield two

        def bend(t):
            b = t % 2
            at = slice(O_FC1B + t * TILE, O_FC1B + (t + 1) * TILE)
            for r in range(0, R, RB):

                def one(r=r):
                    value, slope = gelu_parts(wide[b, r : r + RB, :])
                    slim[b, r : r + RB, :] = value.astype(BF16)
                    low = (wide[b, R + r : R + r + RB, :] * slope).astype(BF16)
                    slim[b, R + r : R + r + RB, :] = low
                    sums[:, at] += fold(low.astype(F32))

                yield one

        def gather(t):
            b, half = t % 2, TILE // 2
            cols = slice(t * TILE, (t + 1) * TILE)
            for n in range(2):
                into = slice(n * half, (n + 1) * half)

                def one(into=into):
                    ffo[:, into] += dot(slim[b, 0:R, :], wfc2[cols, into])

                def two(into=into):
                    dsn[:, into] += dot_nt(slim[b, R : 2 * R, :], wfc1[into, cols])

                yield one
                yield two
            for n in range(4):
                lanes_n = slice(n * LN, (n + 1) * LN)
                rows_n = slice(t * TILE + n * LN, t * TILE + (n + 1) * LN)

                def one(lanes_n=lanes_n, rows_n=rows_n):
                    g_fc2[rows_n, :] += dot_tn(slim[b, 0:R, lanes_n], dy[...])

                def two(lanes_n=lanes_n):
                    g_fc1[lanes_n, cols] += dot_tn(sn[:, lanes_n], slim[b, R : 2 * R, :])

                yield one
                yield two

        tiles = FF // TILE
        for piece in spread(0):
            piece()
        for t in range(tiles + 1):
            heavy = (list(gather(t - 1)) if t else []) + (list(spread(t + 1)) if t + 1 < tiles else [])
            light = list(bend(t)) if t < tiles else []
            weave(heavy, light)
        @pl.when(c >= 2)
        def _():
            done_copy(c - 2).wait()

        for w in range(CW):
            out_stage[lax.rem(c, 2), w] = (ffo[w * RW : w * RW + WT, :] * flags[w]).astype(BF16)
        done_copy(c).start()
        sum_g = jnp.zeros((8, DM), F32)
        sum_b = jnp.zeros((8, DM), F32)
        for r in range(0, R, RB):
            xhat, inv = normalised(sec[r : r + RB, :])
            d_out = dsn[r : r + RB, :]
            sum_g = sum_g + fold(d_out * xhat)
            sum_b = sum_b + fold(d_out)
            dsec[p, r : r + RB, :] = norm_back(d_out, n2g[...], xhat, inv) + dy[r : r + RB, :].astype(F32)
        sums[:, O_N2G : O_N2G + DM] += sum_g
        sums[:, O_N2B : O_N2B + DM] += sum_b

    def second_half(c):
        p = lax.rem(c, SLOTS)
        low = dsec[p].astype(BF16)
        sums[:, O_PB : O_PB + DM] += fold(low.astype(F32))
        dy[...] = low
        g_proj[...] += dot_tn(att[p], dy[...])
        back = dot_nt(dy[...], wproj[...])
        for w in range(CW):
            for g in range(GROUPS):
                piece = back[w * RW : (w + 1) * RW, g * LN : (g + 1) * LN]
                d_heads[w, g, 0:JP, :] = padded(piece).astype(BF16)

        def attend(w, carry):
            rows = pl.ds(pl.multiple_of(w * RW, 8), RW)
            for g in range(GROUPS):
                wide[0, g * JP : (g + 1) * JP, :] = dot_nt(qkv[p, w, 2, g, 0:JP, :], by_head(d_heads[w, g]))
            for g in range(GROUPS):
                stage[rows, 2 * DM + g * LN : 2 * DM + (g + 1) * LN] = dot(prob[p, w, g], by_head(d_heads[w, g]))[0:RW]
            for g in range(GROUPS):
                for h in range(PER):
                    lane_h = slice(h * LN, (h + 1) * LN)
                    pr = prob[p, w, g, :, lane_h].astype(F32)
                    pd = pr * wide[0, g * JP : (g + 1) * JP, lane_h]
                    d_s = pd - pr * jnp.sum(pd, axis=0, keepdims=True)
                    ds_acc[g * PER + h] += d_s
                    slim[0, g * JP : (g + 1) * JP, lane_h] = (d_s * SCALE).astype(BF16)
            for g in range(GROUPS):
                mixed = dot_tn(qkv[p, w, 1, g, 0:JP, :], slim[0, g * JP : (g + 1) * JP, :])
                for h in range(PER):
                    owns[g, h * HD : (h + 1) * HD, :] = mixed[h * HD : (h + 1) * HD, h * LN : (h + 1) * LN]
            for g in range(GROUPS):
                stage[rows, DM + g * LN : DM + (g + 1) * LN] = dot(slim[0, g * JP : (g + 1) * JP, :], by_head(qkv[p, w, 0, g]))[0:RW]
            for g in range(GROUPS):
                stage[rows, g * LN : (g + 1) * LN] = owns[g].T[0:RW]
            return carry

        lax.fori_loop(0, CW, attend, 0)
        sum_g = jnp.zeros((8, DM), F32)
        sum_b = jnp.zeros((8, DM), F32)
        sum_q = jnp.zeros((8, DM), F32)
        sum_v = jnp.zeros((8, DM), F32)
        for r in range(0, R, RB):
            low = stage[r : r + RB, :].astype(BF16)
            dpk[r : r + RB, :] = low
            sum_q = sum_q + fold(low[:, 0:DM].astype(F32))
            sum_v = sum_v + fold(low[:, 2 * DM :].astype(F32))
        sums[:, O_QB : O_QB + DM] += sum_q
        sums[:, O_VB : O_VB + DM] += sum_v
        dsn[...] = dot_nt(dpk[...], wqkv[...])
        for r in range(0, R, RB):
            xhat, inv = normalised(res[p, r : r + RB, :])
            fst[r : r + RB, :] = (xhat * n1g[...] + n1b[...]).astype(BF16)
            d_out = dsn[r : r + RB, :]
            sum_g = sum_g + fold(d_out * xhat)
            sum_b = sum_b + fold(d_out)
            d_res = norm_back(d_out, n1g[...], xhat, inv) + dsec[p, r : r + RB, :]
            sn[r : r + RB, :] = d_res.astype(BF16)
        sums[:, O_N1G : O_N1G + DM] += sum_g
        sums[:, O_N1B : O_N1B + DM] += sum_b
        wide[0, 0:R, :] = dot_nt(sn[...], wp[0:DM, :])
        wide[0, R : 2 * R, :] = dot_nt(sn[...], wp[DM:WIDTH, :])
        sum_g = jnp.zeros((8, WIDTH), F32)
        sum_b = jnp.zeros((8, WIDTH), F32)
        for r in range(0, R, RB):
            xhat, inv = normalised(merged_rows(c, r))
            nrm[r : r + RB, :] = (xhat * n0g[...] + n0b[...]).astype(BF16)
            d_out = jnp.concatenate([wide[0, r : r + RB, :], wide[0, R + r : R + r + RB, :]], axis=1)
            sum_g = sum_g + fold(d_out * xhat)
            sum_b = sum_b + fold(d_out)
            low = norm_back(d_out, n0g[...], xhat, inv).astype(BF16)
            for s in range(n_head):
                rin[c, s, r : r + RB, :] = low[:, s * lanes : (s + 1) * lanes]
        sums[:, O_N0G : O_N0G + WIDTH] += sum_g
        sums[:, O_N0B : O_N0B + WIDTH] += sum_b
        for k in range(1, n_head):
            out_copy(c, k).start()
        own_out(c).start()
        g_qkv[...] += dot_tn(fst[...], dpk[...])
        g_red[...] += dot_tn(nrm[...], sn[...])
        own_out(c).wait()

    def unpack(c):
        for k in range(1, n_head):
            pltpu.make_async_remote_copy(
                src_ref=rin.at[c, me], dst_ref=rout.at[c, lax.rem(me + n_head - k, n_head)],
                send_sem=out_send.at[c, k], recv_sem=out_recv.at[c, k],
                device_id={"head": peer(k)}, device_id_type=MESH,
            ).wait_recv()

        @pl.when(c >= 2)
        def _():
            sect_copy(c - 2).wait()

        for s in range(n_head):
            turned = dot_nt(eye_lanes, rout[c, s])
            for w in range(CW):
                xv[lax.rem(c, 2), s, w] = turned[:, w * RW : w * RW + WT].astype(BF16)
        sect_copy(c).start()

    def sent(c, carry):
        for k in range(1, n_head):
            in_copy(c, k).wait_send()
        return carry

    def step(s, carry):
        @pl.when(s < n_chunk)
        def _():
            first_half(s)

        if n_win is not None:
            @pl.when(s == n_chunk - 1)
            def _():
                for f in feeds:
                    f.start_pair()

            @pl.when(s == n_chunk)
            def _():
                for f in feeds:
                    f.start_plane()

        @pl.when(s == LAG)
        def _():
            lax.fori_loop(0, n_chunk, sent, 0)
            for k in range(1, n_head):
                pl.semaphore_signal(free_sem, inc=1, device_id={"head": peer(k)}, device_id_type=MESH)
            pl.semaphore_wait(free_sem, n_head - 1)

        @pl.when(s >= LAG)
        def _():
            second_half(s - LAG)

        if n_win is not None:
            @pl.when(s == n_chunk + LAG - 1)
            def _():
                for f in others:
                    f.start_pair()
                table_sums()
                small_in[at_pair, 0:HEADS, :] = vector_rows().astype(BF16)
                small_pair().start()

        return carry

    def vector_rows():
        row = jnp.sum(sums[...], axis=0, keepdims=True)
        return jnp.concatenate([row[:, r * DM : (r + 1) * DM] for r in range(O_END // DM)], axis=0)

    def table_sums():
        total = jnp.zeros((HEADS, 4 * LN), F32)
        for row in range(WIN):
            spread = jnp.zeros((WIN * HEADS, 2 * LN), F32)
            whole = jnp.concatenate([ds_acc[:, row * WIN + col, :] for col in range(WIN)], axis=0)
            for part in split3(whole):
                spread = spread + dot_nt(part, pick)
            for col in range(WIN):
                off = offset_of(WT - 1) - offset_of(row * WIN + col)
                piece = jnp.concatenate(
                    [spread[col * HEADS : (col + 1) * HEADS], jnp.zeros((HEADS, 2 * LN), F32)], axis=1
                )
                total = total + pltpu.roll(piece, off, 1)
        if n_win is None:
            g_small[HEADS:, :] = total
        else:
            small_in[at_pair, HEADS:, :] = total.astype(BF16)

    lax.fori_loop(0, n_chunk + LAG, step, 0)

    def unpack_range(low, high):
        def body(c, carry):
            unpack(c)
            return carry

        lax.fori_loop(low, high, body, 0)

    if n_win is None:
        g_small[0:HEADS, :] = vector_rows()
        table_sums()
        unpack_range(0, n_chunk)
    else:
        for f in others:
            f.start_plane()
        small_pair().wait_recv()
        small_in[at_plane + my_win] = (small_in[at_pair].astype(F32) + small_in[at_pair + 1].astype(F32)).astype(BF16)
        for k in range(1, n_win):
            small_plane(k).start()
        for f in feeds:
            f.start_near()
        unpack_range(0, n_chunk - 4)
        for f in feeds:
            f.start_far()
        unpack_range(n_chunk - 4, n_chunk - 3)
        for k in range(1, n_win):
            small_plane(k, lax.rem(my_win + n_win - k, n_win)).wait_recv()
        total = small_in[at_plane].astype(F32)
        for w in range(1, n_win):
            total = total + small_in[at_plane + w].astype(F32)
        small_in[at_near] = total.astype(BF16)
        small_near().start()
        for f in others:
            f.start_near()
        for f in feeds:
            f.finish()
        small_near().wait_recv()
        small_in[at_far] = (small_in[at_near].astype(F32) + small_in[at_near + 1].astype(F32)).astype(BF16)
        small_far().start()
        for f in others:
            f.start_far()
        unpack_range(n_chunk - 3, n_chunk - 1)
        for f in reversed(others):
            f.finish()
        small_far().wait_recv()
        g_small[...] = small_in[at_far].astype(F32) + small_in[at_far + 1].astype(F32)
        unpack_range(n_chunk - 1, n_chunk)
        others[-1].finish_gather()
        for f in feeds + others:
            f.drain()
        small_pair().wait_send()
        for k in range(1, n_win):
            small_plane(k).wait_send()
        small_near().wait_send()
        small_far().wait_send()
    for c in range(max(0, n_chunk - 2), n_chunk):
        sect_copy(c).wait()
        done_copy(c).wait()

    def drain(c, carry):
        for k in range(1, n_head):
            out_copy(c, k).wait_send()
        return carry

    lax.fori_loop(0, n_chunk, drain, 0)


def run_kernel(n_head, n_win, n_chunk, share, args):
    lanes = QUADS * share
    any_, vmem = pl.BlockSpec(memory_space=pl.ANY), pl.BlockSpec(memory_space=pltpu.VMEM)
    smem = pl.BlockSpec(memory_space=pltpu.SMEM)
    windows = n_chunk * CW
    in_specs = [
        any_, any_, vmem, vmem, vmem, vmem, any_, vmem, vmem, vmem, any_, vmem, vmem, vmem,
        any_, vmem, any_, vmem, smem, any_,
    ]
    out_shape = [
        jax.ShapeDtypeStruct((windows, WT, DM), BF16),
        jax.ShapeDtypeStruct((n_head, n_chunk, CW, lanes, WT), BF16),
    ]
    dma = pltpu.SemaphoreType.DMA
    scratch = []
    if n_win is None:
        out_shape += [jax.ShapeDtypeStruct(m, F32) for m in MATRICES]
    else:
        devices, n_z = n_win * n_head, n_head // 2
        scratch += [pltpu.VMEM(m, F32) for m in MATRICES]
        shares = [(m // devices, cols) for m, cols in MATRICES]
        out_shape += [jax.ShapeDtypeStruct(m, F32) for m in shares[:-1]]
        out_shape += [jax.ShapeDtypeStruct((shares[-1][0] * n_win, DM), F32)]
        scratch += [pltpu.VMEM((rows * n_win * n_z, cols), BF16) for rows, cols in shares]
        scratch += [pltpu.VMEM((n_win - 1, rows * n_z, cols), BF16) for rows, cols in shares]
        scratch += [pltpu.VMEM((rows * (n_z // 2), cols), BF16) for rows, cols in shares]
        scratch += [pltpu.VMEM((rows, cols), BF16) for rows, cols in shares]
        scratch += [
            pltpu.VMEM((n_win, shares[-1][0], DM), BF16),
            pltpu.VMEM((n_win + 6, 2 * HEADS, DM), BF16),
            dma((6, 2 * n_win + 2)), dma((6, 2 * n_win + 2)),
        ]
    out_shape += [jax.ShapeDtypeStruct((2 * HEADS, DM), F32)]
    out_specs = [any_, any_] + [vmem] * 6
    scratch += [
        pltpu.VMEM((2, n_head, CW, lanes, WT), BF16),
        pltpu.VMEM((n_chunk, n_head, R, lanes), BF16),
        pltpu.VMEM((n_chunk, n_head, R, lanes), BF16),
        pltpu.VMEM((WIDTH, DM), BF16),
        pltpu.VMEM((DM, 3 * DM), BF16),
        pltpu.VMEM((DM, DM), BF16),
        pltpu.VMEM((DM, FF), BF16),
        pltpu.VMEM((FF, DM), BF16),
        pltpu.VMEM((2, CW, WT, DM), BF16),
        pltpu.VMEM((R, WIDTH), BF16),
        pltpu.VMEM((SLOTS, R, DM), F32),
        pltpu.VMEM((R, DM), BF16),
        pltpu.VMEM((SLOTS, CW, 3, GROUPS, LN, LN), BF16),
        pltpu.VMEM((SLOTS, CW, GROUPS, JP, PER * LN), BF16),
        pltpu.VMEM((SLOTS, R, DM), BF16),
        pltpu.VMEM((R, 3 * DM), F32),
        pltpu.VMEM((R, DM), F32),
        pltpu.VMEM((R, DM), BF16),
        pltpu.VMEM((R, DM), BF16),
        pltpu.VMEM((2, GROUPS * JP, TILE), F32),
        pltpu.VMEM((2, GROUPS * JP, TILE), BF16),
        pltpu.VMEM((R, DM), F32),
        pltpu.VMEM((R, DM), F32),
        pltpu.VMEM((SLOTS, R, DM), F32),
        pltpu.VMEM((R, 3 * DM), BF16),
        pltpu.VMEM((CW, GROUPS, LN, LN), BF16),
        pltpu.VMEM((1, WIDTH), F32),
        pltpu.VMEM((1, WIDTH), F32),
        pltpu.VMEM((HEADS, 4 * LN), F32),
        pltpu.VMEM((GROUPS, LN, LN), F32),
        pltpu.VMEM((2, CW, WT, DM), BF16),
        pltpu.VMEM((8, O_END), F32),
        pltpu.VMEM((HEADS, JP, LN), F32),
        pltpu.VMEM((HEADS, JP, LN), F32),
        dma((n_chunk, n_head)), dma((n_chunk, n_head)), dma((n_chunk, n_head)), dma((n_chunk, n_head)),
        dma((2,)), dma((5,)), dma((2,)), dma, dma((2,)), pltpu.SemaphoreType.REGULAR, dma((2,)),
    ]
    return pl.pallas_call(
        functools.partial(kernel, n_head, n_win, n_chunk, share),
        out_shape=out_shape, in_specs=in_specs, out_specs=out_specs, scratch_shapes=scratch,
        compiler_params=pltpu.CompilerParams(
            collective_id=0, has_side_effects=True, vmem_limit_bytes=63 * 1024 * 1024
        ),
        cost_estimate=pl.CostEstimate(flops=27 * 10**9, bytes_accessed=30 * 10**6, transcendentals=10**7),
    )(*args)


def finish_kernel(n_head, devices, share, whole, *refs):
    arrays, small, outs = refs[:whole], refs[whole], refs[whole + 1 : -2 - whole]
    held, (in_sem, out_sem) = refs[-2 - whole : -2], refs[-2:]
    arriving, leaving = [], []
    for source, middle, target in zip(arrays, held, outs[:whole]):
        pieces = source.shape[0] if len(source.shape) > 2 else 1
        for i in range(pieces):
            part = pl.ds(i, 1) if pieces > 1 else pl.ds(0, source.shape[0])
            arriving.append(pltpu.make_async_copy(source.at[part], middle.at[part], in_sem.at[len(arriving)]))
            leaving.append(pltpu.make_async_copy(middle.at[part], target.at[part], out_sem.at[len(leaving)]))
    for copy in arriving:
        copy.start()
    n0g, n0b, n1g, n1b, qb, vb, table, pb, n2g, n2b, fc1b, fc2b = outs[whole:]
    head = lax.axis_index("head")
    at = lax.axis_index("win") * n_head + head

    def taken(start, size, spot):
        first = spot * size
        row = small[pl.ds(start // DM + first // DM, 1), :]
        return pltpu.roll(row, lax.rem(DM - lax.rem(first, DM), DM), 1)[:, 0:size]

    for target, start in (
        (n1g, O_N1G), (n1b, O_N1B), (qb, O_QB), (vb, O_VB), (pb, O_PB), (n2g, O_N2G), (n2b, O_N2B), (fc2b, O_FC2B),
    ):
        target[...] = taken(start, DM // devices, at)
    fc1b[...] = taken(O_FC1B, FF // devices, at)
    for target, start in ((n0g, O_N0G), (n0b, O_N0B)):
        row = taken(start, QUADS * share, head)
        for q in range(QUADS):
            target[q : q + 1, :] = row[:, q * share : (q + 1) * share]
    table[...] = small[HEADS:, 0:RELS]
    for copy, onward in zip(arriving, leaving):
        copy.wait()
        onward.start()
    for copy in leaving:
        copy.wait()


def run_finish(n_head, devices, share, args):
    any_, vmem = pl.BlockSpec(memory_space=pl.ANY), pl.BlockSpec(memory_space=pltpu.VMEM)
    block_out, section, red, qkv, proj, fc1, fc2, small = args
    whole = (block_out, section, red, qkv, proj, fc1, fc2)
    one, wide = (1, DM // devices), (1, FF // devices)
    norm = (QUADS, share)
    shapes = [(v.shape, v.dtype) for v in whole]
    shapes += [(m, F32) for m in (norm, norm, one, one, one, one, (HEADS, RELS), one, one, one, wide, one)]
    count = sum(v.shape[0] if v.ndim > 2 else 1 for v in whole)
    outs = pl.pallas_call(
        functools.partial(finish_kernel, n_head, devices, share, len(whole)),
        out_shape=[jax.ShapeDtypeStruct(m, t) for m, t in shapes],
        in_specs=[any_] * len(whole) + [vmem], out_specs=[any_] * len(whole) + [vmem] * 12,
        scratch_shapes=[pltpu.VMEM(v.shape, v.dtype) for v in whole]
        + [pltpu.SemaphoreType.DMA((count,)), pltpu.SemaphoreType.DMA((count,))],
        compiler_params=pltpu.CompilerParams(vmem_limit_bytes=63 * 1024 * 1024),
    )(*args)
    block_out, section, red, qkv, proj, fc1, fc2, n0g, n0b, n1g, n1b, qb, vb, table, pb, n2g, n2b, fc1b, fc2b = outs
    return block_out, section, red, n0g, n0b, n1g, n1b, qkv, qb, vb, table, proj, pb, n2g, n2b, fc1, fc1b, fc2, fc2b


def local(
    n_head, section_rows, reduce_weight, norm0_gain, norm0_bias, norm1_gain, norm1_bias, qkv_weight, q_bias, v_bias,
    rel_table, proj_weight, proj_bias, norm2_gain, norm2_bias, fc1_weight, fc1_bias, fc2_weight, fc2_bias,
    window_valid, cotangent,
):
    group_windows, tokens, quads, share = section_rows.shape
    windows = cotangent.shape[0]
    n_chunk = windows // CW
    lanes = quads * share
    rows = section_rows.transpose(0, 2, 3, 1).reshape(n_head, n_chunk, CW, lanes, tokens)

    def row(v):
        return v.reshape(1, -1)

    args = (
        rows, reduce_weight.reshape(quads, n_head, share, DM), norm0_gain, norm0_bias,
        row(norm1_gain), row(norm1_bias), qkv_weight, row(q_bias), row(v_bias),
        rel_table, proj_weight, row(proj_bias), row(norm2_gain), row(norm2_bias),
        fc1_weight, row(fc1_bias), fc2_weight, row(fc2_bias), window_valid, cotangent,
    )
    n_win = lax.axis_size("win")
    devices = n_win * n_head
    inside = n_head == 8 and all((m // devices) % 16 == 0 for m, unused in MATRICES)
    block_out, section, fc1, fc2, qkv, proj, red, small = run_kernel(
        n_head, n_win if inside else None, n_chunk, share, args
    )
    both = ("win", "head")

    def scattered(v):
        return lax.psum_scatter(v.astype(BF16), both, scatter_dimension=0, tiled=True).astype(F32)

    if not inside:
        fc1, fc2, qkv, proj = scattered(fc1), scattered(fc2), scattered(qkv), scattered(proj)
        red = lax.psum_scatter(red.astype(BF16), "head", scatter_dimension=0, tiled=True)
        red = lax.psum(red, "win").astype(F32)
        small = lax.psum(small, both)
    block_out, section, red, n0g, n0b, n1g, n1b, qkv, qb, vb, table, proj, pb, n2g, n2b, fc1, fc1b, fc2, fc2b = (
        run_finish(n_head, devices, share, (block_out, section, red, qkv, proj, fc1, fc2, small))
    )
    section_grad = section.reshape(group_windows, quads, share, tokens).transpose(0, 3, 1, 2)

    def flat(v):
        return v.reshape(-1)

    return (
        block_out, section_grad, red.reshape(quads, share, DM), n0g, n0b, flat(n1g), flat(n1b), qkv, flat(qb), flat(vb),
        table, proj, flat(pb), flat(n2g), flat(n2b), fc1, flat(fc1b), fc2, flat(fc2b),
    )


def solution(mesh):
    in_specs = (
        P("win", None, None, "head"),
        P(),
        P(),
        P(),
        P(),
        P(),
        P(),
        P(),
        P(),
        P(),
        P(),
        P(),
        P(),
        P(),
        P(),
        P(),
        P(),
        P(),
        P(("win", "head")),
        P(("win", "head"), None, None),
    )
    out_specs = (
        P(("win", "head"), None, None),
        P("win", None, None, "head"),
        P(None, "head", None),
        P(None, "head"),
        P(None, "head"),
        P(("win", "head")),
        P(("win", "head")),
        P(("win", "head"), None),
        P(("win", "head")),
        P(("win", "head")),
        P(),
        P(("win", "head"), None),
        P(("win", "head")),
        P(("win", "head")),
        P(("win", "head")),
        P(("win", "head"), None),
        P(("win", "head")),
        P(("win", "head"), None),
        P(("win", "head")),
    )
    return jax.shard_map(
        functools.partial(local, mesh.shape["head"]), mesh=mesh, in_specs=in_specs, out_specs=out_specs, check_vma=False)
```
